256 devices in a mesh: lat: 32 (over x, z), lev: 8 (over y, core).
Axes of the slice: x: 4, y: 4, z: 8, core: 2. Of those that a mesh axis runs over, the one named last changes fastest.
Arguments:
- fourier: bfloat16 [1280, 3, 128, 128], P('lat', None, 'lev'), may hold values from -6 to 6
- gauss: float32 [1280], P('lat'), may hold values from 0.2 to 2
- legendre: bfloat16 [32, 4, 1280, 640], P('lat'), may hold values from -0.15625 to 0.15625
- owner: int32 [64, 1], replicated, may hold values from 0 to 31; in each aligned block of 64 rows (0 to 63, 64 to 127, ...) at most 4 rows name the same one
- send_list: int32 [32, 32, 2], P('lat'), may hold values from 0 to 799, as said below
- stencil: int32 [8192, 4], P('lat'), may hold values from 0 to 63, as said below
- hweight: float32 [8192, 4, 128], P('lat'), may hold values from -3 to 3
- vweight: float32 [8192, 128], P('lat', 'lev'), may hold values from 0 to 1
Outputs:
- spectral: bfloat16 [32, 4, 3, 128, 2, 640], P('lat', None, None, 'lev')
- arrival: bfloat16 [8192, 3, 128, 128], P('lat', None, 'lev')
The draws below stay inside these ranges and needn't reach their ends.
Inputs may be any that keep to these rules, and one draw needn't show every extreme that they name: Every owner holds one to 4 wavenumbers, some owner exactly 4. send_list[d, r, :] names blocks of band d; stencil reads only devices d with |d - r| <= 16, and of these only the first one to 2 entries; entries for d = r always all 2; the others repeat the first entry. `stencil`: row a reads slots d * 2 + k of band a // 256 for live entries of send_list[d, a // 256, k], |d - a // 256| <= 16.
All inputs are finite; a program needn't handle non-finite values.
Results may differ from the reference program's by a relative error of at most 0.0072.
Values may be sent and summed in bfloat16 or wider, within the bound.
No kernel may reach another device: no remote copies, remote signals or barrier semaphores. Data moves between devices by JAX's collectives and lax.ppermute only.
A program may use at most 128 MiB of HBM per device.

```python
import math
import jax
import jax.numpy as jnp
import numpy as np
from jax import lax

FLD = 3
LAT_DEV = 40
NDEG = 640
NLON = 2560
BLK = 128
MOST = 4
CAP = 2
ARR = 256
NLAT = 1280
MW = 64
LEV = 128
REACH = 16
N_LAT = 32


def departure_counts(key):
    source = jnp.arange(N_LAT, dtype=jnp.int32)
    apart = jnp.abs(source[:, None] - source[None, :])
    counts = jax.random.randint(jax.random.fold_in(key, 11), (N_LAT, N_LAT), 1, CAP + 1)
    counts = jnp.where(apart <= REACH, counts, 0)
    return jnp.where(apart == 0, CAP, counts)


def draw_send_list(key, part):
    counts = departure_counts(key)
    key = jax.random.fold_in(key, 3)
    choices_made = jax.random.randint(key, (N_LAT, N_LAT, CAP), 0, LAT_DEV * (NLON // BLK))
    slot_index = jnp.arange(CAP, dtype=jnp.int32)
    return jnp.where(slot_index[None, None, :] < counts[:, :, None], choices_made, choices_made[:, :, :1])


def draw_stencil(key, part):
    counts = departure_counts(key)
    key = jax.random.fold_in(key, 5)
    row_count = N_LAT * ARR
    row_index = jnp.arange(row_count, dtype=jnp.int32)
    receiver = row_index // ARR
    offsets = jax.random.randint(jax.random.fold_in(key, 1), (row_count, 4), -REACH, REACH + 1)
    source = jnp.clip(receiver[:, None] + offsets, 0, N_LAT - 1)
    half_way = N_LAT // 2
    far_band = jnp.where(receiver + half_way < N_LAT, receiver + half_way, receiver - half_way)
    first_row = row_index % ARR == 0
    column_zero = jnp.where(first_row, far_band, source[:, 0])
    source = jnp.concatenate([column_zero[:, None], source[:, 1:]], axis=1)
    live_count = counts[source, receiver[:, None]]
    within = jax.random.randint(jax.random.fold_in(key, 2), (row_count, 4), 0, 1 << 20) % live_count
    return source * CAP + within


def block_levels(stream_key, dims, pieces, least, top_value):
    level = 1.0
    for axis_at, blocks in pieces:
        steps = jax.random.uniform(jax.random.fold_in(jax.random.fold_in(stream_key, 6), axis_at), (blocks,), jnp.float32, least / len(pieces), top_value / len(pieces))
        level = level * jnp.repeat(jnp.exp(steps), dims[axis_at] // blocks).reshape((-1,) + (1,) * (len(dims) - 1 - axis_at))
    return level


def assign_block(own_key, own, number, rows, amount, top, limit, slope):
    order = jax.random.permutation(own_key, amount)
    heavy_load, ordinary = shares(amount, rows * top, limit, slope, True), shares(amount, rows * top, limit, slope, False)
    places = jnp.arange(amount)

    def named(lengths, turn):
        used = int((lengths > 0).sum())
        fixed = max(1, used // 4)
        moved = fixed + (places - fixed + turn * (used - fixed)) % max(1, amount - fixed)
        return jnp.zeros((amount,), jnp.int32).at[order[jnp.where(places < fixed, places, moved)]].set(jnp.asarray(lengths, jnp.int32))

    lengths = jnp.where(number % 4 == 0, named(heavy_load, number // 4), named(ordinary, number - number // 4 - 1))
    mixed = jax.random.permutation(jax.random.fold_in(own, 3), amount)
    giver, taker = mixed[0:amount // 2 * 2:2], mixed[1:amount // 2 * 2:2]
    room = jnp.minimum(lengths[giver] - 1, limit - lengths[taker]) // 2
    room = jnp.where((giver == order[0]) | (taker == order[0]) | (lengths[taker] == 0), 0, jnp.maximum(room, 0))
    moved = jax.random.randint(jax.random.fold_in(own, 4), (amount // 2,), 0, 1 << 20) % (room + 1)
    lengths = lengths.at[giver].add(-moved).at[taker].add(moved)
    labels = jnp.searchsorted(jnp.cumsum(lengths), jnp.arange(rows * top), side="right").astype(jnp.int32)
    listing = labels.reshape(top, rows).T
    listing = listing[jax.random.permutation(jax.random.fold_in(own, 1), rows)]
    turn = jax.random.randint(jax.random.fold_in(own, 2), (rows, 1), 0, top)
    return jnp.take_along_axis(listing, (jnp.arange(top)[None, :] + turn) % top, axis=1)


def shares(count, total, most, slope, full):
    portions = [(1 << 20) // math.isqrt(standing ** slope) + 1 for standing in range(1, count + 1)]
    largest = most if full else min(most, max(-(-total // count), total * portions[0] // sum(portions)))
    least = 1 if total - largest >= count - 1 else 0
    given, surplus = [largest] + [least] * (count - 1), total - largest - least * (count - 1)
    while surplus > 0:
        candidates = [i for i in range(1, count) if given[i] < largest] or [i for i in range(1, count) if given[i] < most]
        whole, remaining = sum([portions[i] for i in candidates]), surplus
        for i in candidates:
            addition = min(most - given[i], max(1, remaining * portions[i] // whole), surplus)
            given[i] = given[i] + addition
            surplus = surplus - addition
    return np.array(given)


def centred(stream_key, dims, spread, most, pieces=(), kind=jnp.bfloat16):
    factor_of = block_levels(stream_key, dims, pieces, -0.22, 0.18) if pieces else 1.0
    result = jax.random.normal(stream_key, dims, jnp.float32) * spread * factor_of
    return jnp.minimum(jnp.maximum(result, -most), most).astype(kind)


def setup_inputs(seed: int = 0) -> dict:
    arg_keys = jax.random.split(jax.random.key(seed), 9)
    fourier = centred(arg_keys[0], (NLAT, FLD, LEV, 2 * MW), 1.0, 6.0, ((0, 32), (2, 8)))
    gauss = jnp.clip(jnp.exp(math.log(2.0) - 2.3025851 * jax.random.uniform(arg_keys[1], (NLAT,), jnp.float32) ** block_levels(arg_keys[1], (NLAT,), ((0, 32),), -0.2, 0.2)), 0.2, 2.0)
    legendre = centred(arg_keys[2], (N_LAT, MOST, NLAT, NDEG), NLAT ** -0.5, 0.15625, ((0, 32),))
    owner_keys = jax.random.split(jax.random.fold_in(arg_keys[3], 1), MW // MW)
    owner_turns = jax.random.permutation(jax.random.fold_in(arg_keys[3], 3), MW // MW)
    owner = jax.vmap(lambda own, number: assign_block(jax.random.fold_in(arg_keys[3], 2), own, number, MW, N_LAT, 1, MOST, 2))(owner_keys, owner_turns).reshape((MW, 1))
    send_list = draw_send_list(jax.random.fold_in(arg_keys[8], 71), 0)
    stencil = draw_stencil(jax.random.fold_in(arg_keys[8], 71), 0)
    hweight = centred(arg_keys[6], (N_LAT * ARR, 4, BLK), 0.5, 3.0, ((0, 32),), jnp.float32)
    vweight = jnp.clip(1.0 * jax.random.uniform(arg_keys[7], (N_LAT * ARR, LEV), jnp.float32) ** block_levels(arg_keys[7], (N_LAT * ARR, LEV), ((0, 32), (1, 8)), -0.2, 0.2), 0.0, 1.0)
    return {"fourier": fourier, "gauss": gauss, "legendre": legendre, "owner": owner, "send_list": send_list, "stencil": stencil, "hweight": hweight, "vweight": vweight}


diffusion = 3.0

def damping_curve(degrees):
    order_n = jnp.arange(degrees, dtype=jnp.float32)
    ratio = order_n * (order_n + 1.0) / float(degrees * (degrees - 1))
    return 1.0 / (1.0 + diffusion * ratio * ratio)

def zonal_rows(wave_number, present, longitudes, wave_total):
    points = jnp.arange(longitudes, dtype=jnp.int32)
    phases = wave_number[:, None] * points[None, :] % longitudes
    angles = phases.astype(jnp.float32) * (2.0 * math.pi / longitudes)
    norm_factor = present[:, None] / math.sqrt(wave_total)
    cosine = jnp.cos(angles) * norm_factor
    sine = -jnp.sin(angles) * norm_factor
    return jnp.stack([cosine, sine], axis=1).reshape(-1, longitudes).astype(jnp.bfloat16)

def reference(fourier, gauss, legendre, owner, send_list, stencil, hweight, vweight):
    owners = owner[:, 0]
    wave_index = jnp.arange(MW, dtype=jnp.int32)
    earlier = (owners[:, None] == owners[None, :]) & (wave_index[:, None] < wave_index[None, :])
    slot_rank = lax.optimization_barrier(jnp.sum(earlier.astype(jnp.int32), axis=0))
    wave_number = wave_index * (NDEG // MW)
    weighted = (fourier.astype(jnp.float32) * gauss[:, None, None, None]).astype(jnp.bfloat16)
    tables = legendre[owners, slot_rank].astype(jnp.float32)
    paired = weighted.astype(jnp.float32).reshape(NLAT, FLD, LEV, MW, 2)
    spectra = jnp.einsum('lfvjr,jln->jfvrn', paired, tables)
    keep_mask = (jnp.arange(NDEG, dtype=jnp.int32)[None, :] >= wave_number[:, None]).astype(jnp.float32)
    damping = keep_mask * damping_curve(NDEG)[None, :]
    field_spec = (spectra * damping[:, None, None, None, :]).astype(jnp.bfloat16)
    spectral = jnp.zeros((N_LAT, MOST, FLD, LEV, 2, NDEG), jnp.bfloat16).at[owners, slot_rank].set(field_spec)
    returned = jnp.einsum('jln,jfvrn->lfvjr', tables, field_spec.astype(jnp.float32))
    returned = returned.astype(jnp.bfloat16).reshape(NLAT, FLD, LEV, 2 * MW)
    zonal_table = zonal_rows(wave_number, jnp.ones((MW,), jnp.float32), NLON, MW)
    blocks_x = NLON // BLK
    zonal_tiles = zonal_table.astype(jnp.float32).reshape(2 * MW, blocks_x, BLK)
    band_start = jnp.arange(N_LAT, dtype=jnp.int32)[:, None] * LAT_DEV

    def arrive(inputs):
        receiver, near_slots, weights_h, weights_v = inputs
        block_ids = send_list[:, receiver, :]
        row_ids = (band_start + block_ids // blocks_x).reshape(-1)
        column_ids = (block_ids % blocks_x).reshape(-1)
        coefficients = returned[row_ids].astype(jnp.float32)
        zonal_piece = zonal_tiles[:, column_ids, :]
        blocks = jnp.einsum('kfvc,ckp->kfvp', coefficients, zonal_piece).astype(jnp.bfloat16)
        picked = blocks[near_slots].astype(jnp.float32)
        horizontal = jnp.einsum('aqp,aqfvp->afvp', weights_h, picked)
        above_level = jnp.concatenate([horizontal[:, :, 1:], horizontal[:, :, -1:]], axis=2)
        vertical_w = weights_v[:, None, :, None]
        return ((1.0 - vertical_w) * horizontal + vertical_w * above_level).astype(jnp.bfloat16)
    arrival = lax.map(arrive, (jnp.arange(N_LAT, dtype=jnp.int32), stencil.reshape(N_LAT, ARR, 4), hweight.reshape(N_LAT, ARR, 4, BLK), vweight.reshape(N_LAT, ARR, LEV)))
    return (spectral, arrival.reshape(N_LAT * ARR, FLD, LEV, BLK))
```

```python
import math

import jax
import jax.numpy as jnp
from jax import lax
from jax.experimental import pallas as pl
from jax.experimental.pallas import tpu as pltpu
from jax.sharding import PartitionSpec as P

NLON = 2560
BLK = 128
BLOCKS_X = NLON // BLK
LANES = 128

diffusion = 3.0

NT = (((1,), (1,)), ((), ()))
NN = (((1,), (0,)), ((), ()))


def mxu(left, right, dims):
    return lax.dot_general(left, right, dims, preferred_element_type=jnp.float32)


def identity(size):
    rows = lax.broadcasted_iota(jnp.int32, (size, size), 0)
    columns = lax.broadcasted_iota(jnp.int32, (size, size), 1)
    return (rows == columns).astype(jnp.float32).astype(jnp.bfloat16)


def damping_curve(degrees):
    order_n = jnp.arange(degrees, dtype=jnp.float32)
    ratio = order_n * (order_n + 1.0) / float(degrees * (degrees - 1))
    return 1.0 / (1.0 + diffusion * ratio * ratio)


def pack_kernel(gauss, fourier, owned_by, slot_mask, message, scratch):
    lat_dev, fields, levels, columns = fourier.shape
    owners = owned_by.shape[0]
    chooser = owned_by[...]
    masks = [slot_mask[i : i + 1, :] for i in range(slot_mask.shape[0])]

    def one_latitude(t, carry):
        rows = fourier[t].reshape(fields * levels, columns).astype(jnp.float32)
        rows = (rows * gauss[t]).astype(jnp.bfloat16)
        parts = []
        for slot in range(len(masks) // 2):
            for field in range(fields):
                for part in range(2):
                    parts.append(rows[field * levels : (field + 1) * levels] * masks[2 * slot + part])
        spread = jnp.concatenate(parts, axis=0)
        chosen = mxu(chooser, spread, NT)
        for tile in range(scratch.shape[0]):
            scratch[tile, pl.ds(t, owners, stride=lat_dev), :] = chosen[:, tile * LANES : (tile + 1) * LANES]
        return carry

    lax.fori_loop(0, lat_dev, one_latitude, 0, unroll=4)
    for o in range(owners):
        for tile in range(scratch.shape[0]):
            message[o, :, tile * LANES : (tile + 1) * LANES] = scratch[
                tile, o * lat_dev : (o + 1) * lat_dev, :
            ].astype(jnp.bfloat16)


def spectral_kernel(row_of, arrived, tables, damping, spectral, message, turned, rows_at):
    step = pl.program_id(0)
    slots = damping.shape[0]
    per_slot = turned.shape[0] // slots
    half = per_slot // 2
    field_rows = half // 3
    latitudes = arrived.shape[0]

    @pl.when(step == 0)
    def _():
        unit = identity(LANES)
        for tile in range(arrived.shape[1] // LANES):
            columns = arrived[:, tile * LANES : (tile + 1) * LANES]
            turned[tile * LANES : (tile + 1) * LANES, :] = mxu(unit, columns, NT).astype(jnp.bfloat16)

    table = tables[0]
    own = turned[pl.ds(pl.multiple_of(step * per_slot, 16), per_slot), :]
    spectra = mxu(own, table, NN)
    damped = (spectra * damping[pl.ds(step, 1), :]).astype(jnp.bfloat16)
    spectral[0] = damped
    gap = jnp.zeros((LANES - half, damped.shape[1]), jnp.bfloat16)
    sides = []
    for part in range(2):
        for field in range(3):
            at = (2 * field + part) * field_rows
            sides.append(damped[at : at + field_rows])
        sides.append(gap)
    sides = jnp.concatenate(sides, axis=0)
    chunk = 256
    for at in range(0, latitudes, chunk):
        back = mxu(table[at : at + chunk], sides, NT)
        for part in range(2):
            rows_at[pl.ds(at * 2 * slots + step * 2 + part, chunk, stride=2 * slots), :] = back[
                :, part * LANES : (part + 1) * LANES
            ]

    @pl.when(step == slots - 1)
    def _():
        receivers, message_rows, message_lanes = message.shape
        lane = lax.broadcasted_iota(jnp.int32, (8, LANES), 1)
        tiles = message_lanes // LANES

        def one_receiver(r, carry):
            for pair in range(message_rows // 16):
                halves = []
                for side in range(2):
                    built = [None] * tiles
                    for e in range(8):
                        entry = r * message_rows + (pair * 2 + side) * 8 + e
                        at = pl.multiple_of(row_of[entry] * 8, 8)
                        row = rows_at[pl.ds(at, 8), :]
                        start = e * half
                        if start % LANES:
                            row = pltpu.roll(row, start % LANES, 1)
                        for tile in range(start // LANES, (start + half - 1) // LANES + 1):
                            first = start - tile * LANES
                            if built[tile] is None:
                                built[tile] = row
                            else:
                                built[tile] = jnp.where(lane >= first, row, built[tile])
                    halves.append(jnp.concatenate(built, axis=1))
                both = jnp.concatenate(halves, axis=0).astype(jnp.bfloat16)
                message[r, pair * 16 : (pair + 1) * 16, :] = both
            return carry

        lax.fori_loop(0, receivers, one_receiver, 0)


def block_kernel(column_of, received, zonal, blocks, lowest, lowest_scratch):
    owners, message_rows, message_lanes = received.shape
    unit = identity(LANES)
    half = message_lanes // 8
    groups = message_rows // 8
    entries = blocks.shape[0]
    for pair in range(groups // 2):
        wide = received[:, pair * 16 : (pair + 1) * 16, :].astype(jnp.float32)
        for side in range(2):
            group = pair * 2 + side
            own = wide[:, side * 8 : (side + 1) * 8, :].reshape(owners * 8, message_lanes).astype(jnp.bfloat16)
            turned = [
                mxu(unit, own[:, tile * LANES : (tile + 1) * LANES], NT).astype(jnp.bfloat16)
                for tile in range(message_lanes // LANES)
            ]
            turned = jnp.concatenate(turned, axis=0)
            for e in range(8):
                entry = group * 8 + e
                made = mxu(turned[e * half : (e + 1) * half], zonal[column_of[entry]], NN)
                blocks[entry] = made.astype(jnp.bfloat16)
                for field in range(3):
                    lowest_scratch[field * entries + entry : field * entries + entry + 1, :] = made[
                        field * 16 : field * 16 + 1, :
                    ]
    lowest[...] = lowest_scratch[...].astype(jnp.bfloat16)


def arrive_kernel(stencil, at_top, blocks, above, hweight, vweight, arrival, wide):
    entries = blocks.shape[0]
    step = pl.program_id(0)
    rows, fields, levels, _ = arrival.shape

    @pl.when(step == 0)
    def _():
        top = at_top[0] == 1

        def widen(entry, carry):
            block = blocks[entry].astype(jnp.float32)
            wide[entry, 0 : fields * levels, :] = block
            for field in range(fields):
                own_last = block[(field + 1) * levels - 1 : (field + 1) * levels, :]
                over = above[pl.ds(field * entries + entry, 1), :]
                wide[entry, pl.ds(fields * levels + field, 1), :] = jnp.where(top, own_last, over)
            return carry

        lax.fori_loop(0, entries, widen, 0, unroll=4)

    level = lax.broadcasted_iota(jnp.int32, (levels, LANES), 0)

    def one_row(a, carry):
        total = None
        for q in range(4):
            place = stencil[(step * rows + a) * 4 + q]
            term = hweight[a, pl.ds(q, 1), :] * wide[place]
            total = term if total is None else total + term
        upper = vweight[a]
        for field in range(fields):
            here = total[field * levels : (field + 1) * levels]
            over = jnp.where(
                level == levels - 1,
                total[fields * levels + field : fields * levels + field + 1],
                pltpu.roll(here, levels - 1, 0),
            )
            arrival[a, field] = ((1.0 - upper) * here + upper * over).astype(jnp.bfloat16)
        return carry

    lax.fori_loop(0, rows, one_row, 0, unroll=4)


def whole(memory):
    return pl.BlockSpec(memory_space=memory)


def per_device(fourier, gauss, legendre, owner, send_list, stencil, hweight, vweight):
    lat_count = lax.axis_size("lat")
    device_row = lax.axis_index("lat")
    lat_dev, fields, levels, columns = fourier.shape
    wave_total = columns // 2
    slot_most = legendre.shape[1]
    degrees = legendre.shape[3]
    latitudes = legendre.shape[2]
    slot_count = lat_count * slot_most
    capacity = send_list.shape[2]
    arrivals = stencil.shape[0]
    half = fields * levels
    per_slot = 2 * half
    message_lanes = slot_most * per_slot
    entries = lat_count * capacity

    owners = owner[:, 0]
    wave_index = jnp.arange(wave_total, dtype=jnp.int32)
    earlier = (owners[:, None] == owners[None, :]) & (wave_index[:, None] < wave_index[None, :])
    slot_rank = jnp.sum(earlier.astype(jnp.int32), axis=0)
    slot_of = owners * slot_most + slot_rank
    wave_number = wave_index * (degrees // wave_total)
    lists = lax.all_gather(send_list[0], "lat", axis=0)

    column_index = jnp.arange(columns, dtype=jnp.int32)
    owner_column = jnp.repeat(owners, 2)
    rank_column = jnp.repeat(slot_rank, 2)
    owned_by = (jnp.arange(lat_count, dtype=jnp.int32)[:, None] == owner_column[None, :]).astype(jnp.bfloat16)
    slot_mask = (
        jnp.arange(2 * slot_most, dtype=jnp.int32)[:, None] == (2 * rank_column + column_index % 2)[None, :]
    ).astype(jnp.bfloat16)
    vmem = whole(pltpu.VMEM)
    smem = whole(pltpu.SMEM)
    message_one = pl.pallas_call(
        pack_kernel,
        out_shape=jax.ShapeDtypeStruct((lat_count, lat_dev, message_lanes), jnp.bfloat16),
        in_specs=[smem, vmem, vmem, vmem],
        out_specs=vmem,
        scratch_shapes=[pltpu.VMEM((message_lanes // LANES, lat_count * lat_dev, LANES), jnp.float32)],
        compiler_params=pltpu.CompilerParams(vmem_limit_bytes=48 * 2**20),
        name="pack",
    )(gauss, fourier, owned_by, slot_mask)
    arrived = lax.all_to_all(message_one, "lat", split_axis=0, concat_axis=0, tiled=True)

    placed = (slot_of[:, None] == jnp.arange(slot_count, dtype=jnp.int32)[None, :]).astype(jnp.int32)
    owned = lax.dynamic_slice_in_dim(placed, device_row * slot_most, slot_most, 1)
    filled = jnp.sum(owned, axis=0) > 0
    slot_wave = jnp.sum(owned * wave_number[:, None], axis=0)
    degree_index = jnp.arange(degrees, dtype=jnp.int32)
    keep_mask = (filled[:, None] & (degree_index[None, :] >= slot_wave[:, None])).astype(jnp.float32)
    damping = keep_mask * damping_curve(degrees)[None, :]

    band_start = jnp.arange(lat_count, dtype=jnp.int32)[:, None, None] * lat_dev
    row_of = jnp.transpose(band_start + lists // BLOCKS_X, (1, 0, 2)).reshape(-1)
    message_shape = (lat_count, entries // 8 * slot_most * 2, 8 * half)
    spectral_rows, message_two = pl.pallas_call(
        spectral_kernel,
        grid_spec=pltpu.PrefetchScalarGridSpec(
            num_scalar_prefetch=1,
            grid=(slot_most,),
            in_specs=[
                pl.BlockSpec((latitudes, message_lanes), lambda s, _: (0, 0)),
                pl.BlockSpec((1, latitudes, degrees), lambda s, _: (s, 0, 0)),
                pl.BlockSpec((slot_most, degrees), lambda s, _: (0, 0)),
            ],
            out_specs=[
                pl.BlockSpec((1, per_slot, degrees), lambda s, _: (s, 0, 0)),
                pl.BlockSpec(message_shape, lambda s, _: (0, 0, 0)),
            ],
            scratch_shapes=[
                pltpu.VMEM((message_lanes, latitudes), jnp.bfloat16),
                pltpu.VMEM((latitudes * 2 * slot_most, LANES), jnp.float32),
            ],
        ),
        out_shape=[
            jax.ShapeDtypeStruct((slot_most, per_slot, degrees), jnp.bfloat16),
            jax.ShapeDtypeStruct(message_shape, jnp.bfloat16),
        ],
        compiler_params=pltpu.CompilerParams(vmem_limit_bytes=48 * 2**20),
        name="spectral",
    )(row_of, arrived.reshape(latitudes, message_lanes), legendre[0], damping)
    received = lax.all_to_all(message_two, "lat", split_axis=0, concat_axis=0, tiled=True)

    spectral = jnp.transpose(
        spectral_rows.reshape(slot_most, fields, 2, levels, degrees), (0, 1, 3, 2, 4)
    )
    slot_waves = jnp.sum(placed * wave_number[:, None], axis=0)
    present = (jnp.sum(placed, axis=0) > 0).astype(jnp.float32)
    points = jnp.arange(NLON, dtype=jnp.int32).reshape(BLOCKS_X, 1, 1, BLK)
    phases = slot_waves[None, :, None, None] * points % NLON
    angles = phases.astype(jnp.float32) * (2.0 * math.pi / NLON)
    norm_factor = present[None, :, None, None] / math.sqrt(wave_total)
    zonal = jnp.concatenate([jnp.cos(angles) * norm_factor, -jnp.sin(angles) * norm_factor], axis=2)
    zonal = zonal.astype(jnp.bfloat16).reshape(BLOCKS_X, slot_count * 2, BLK)
    own_lists = lax.dynamic_slice_in_dim(lists, device_row, 1, 1)
    column_of = (own_lists % BLOCKS_X).reshape(-1)
    blocks, lowest = pl.pallas_call(
        block_kernel,
        out_shape=[
            jax.ShapeDtypeStruct((entries, half, BLK), jnp.bfloat16),
            jax.ShapeDtypeStruct((fields * entries, BLK), jnp.bfloat16),
        ],
        in_specs=[smem, vmem, vmem],
        out_specs=[vmem, vmem],
        scratch_shapes=[pltpu.VMEM((fields * entries, BLK), jnp.float32)],
        compiler_params=pltpu.CompilerParams(vmem_limit_bytes=48 * 2**20),
        name="blocks",
    )(column_of, received, zonal)

    lev_count = lax.axis_size("lev")
    above = lax.ppermute(lowest, "lev", [(i, i - 1) for i in range(1, lev_count)])
    at_top = (lax.axis_index("lev") == lev_count - 1).astype(jnp.int32).reshape(1)
    vertical = jnp.broadcast_to(vweight[:, :, None], (arrivals, levels, BLK))
    step_rows = 32
    arrival = pl.pallas_call(
        arrive_kernel,
        grid_spec=pltpu.PrefetchScalarGridSpec(
            num_scalar_prefetch=2,
            grid=(arrivals // step_rows,),
            in_specs=[
                pl.BlockSpec((entries, half, BLK), lambda i, *_: (0, 0, 0)),
                pl.BlockSpec((fields * entries, BLK), lambda i, *_: (0, 0)),
                pl.BlockSpec((step_rows, 4, BLK), lambda i, *_: (i, 0, 0)),
                pl.BlockSpec((step_rows, levels, BLK), lambda i, *_: (i, 0, 0)),
            ],
            out_specs=pl.BlockSpec((step_rows, fields, levels, BLK), lambda i, *_: (i, 0, 0, 0)),
            scratch_shapes=[pltpu.VMEM((entries, half + 8, BLK), jnp.float32)],
        ),
        out_shape=jax.ShapeDtypeStruct((arrivals, fields, levels, BLK), jnp.bfloat16),
        compiler_params=pltpu.CompilerParams(vmem_limit_bytes=48 * 2**20),
        name="arrive",
    )(stencil.reshape(-1), at_top, blocks, above.astype(jnp.float32), hweight, vertical)
    return (spectral[None], arrival)


def solution(mesh):
    return jax.shard_map(
        per_device,
        mesh=mesh,
        in_specs=(
            P("lat", None, "lev", None),
            P("lat"),
            P("lat", None, None, None),
            P(),
            P("lat", None, None),
            P("lat", None),
            P("lat", None, None),
            P("lat", "lev"),
        ),
        out_specs=(P("lat", None, None, "lev", None, None), P("lat", None, "lev", None)),
        check_vma=False,
    )
```

```python
import math

import jax
import jax.numpy as jnp
from jax import lax
from jax.experimental import pallas as pl
from jax.experimental.pallas import tpu as pltpu
from jax.sharding import PartitionSpec as P

NLON = 2560
BLK = 128
BLOCKS_X = NLON // BLK
LANES = 128

diffusion = 3.0

NT = (((1,), (1,)), ((), ()))
NN = (((1,), (0,)), ((), ()))


def mxu(left, right, dims):
    return lax.dot_general(left, right, dims, preferred_element_type=jnp.float32)


def identity(size):
    rows = lax.broadcasted_iota(jnp.int32, (size, size), 0)
    columns = lax.broadcasted_iota(jnp.int32, (size, size), 1)
    return (rows == columns).astype(jnp.float32).astype(jnp.bfloat16)


def damping_curve(degrees):
    order_n = jnp.arange(degrees, dtype=jnp.float32)
    ratio = order_n * (order_n + 1.0) / float(degrees * (degrees - 1))
    return 1.0 / (1.0 + diffusion * ratio * ratio)


def pack_kernel(gauss, fourier, owned_by, slot_mask, listed, message, scratch):
    lat_dev, fields, levels, columns = fourier.shape
    owners = owned_by.shape[0]
    chooser = owned_by[...]
    masks = [slot_mask[i : i + 1, :] for i in range(slot_mask.shape[0])]

    def one_latitude(t, carry):
        rows = fourier[t].reshape(fields * levels, columns).astype(jnp.float32)
        rows = (rows * gauss[t]).astype(jnp.bfloat16)
        parts = []
        for slot in range(len(masks) // 2):
            for field in range(fields):
                for part in range(2):
                    parts.append(rows[field * levels : (field + 1) * levels] * masks[2 * slot + part])
        spread = jnp.concatenate(parts, axis=0)
        chosen = mxu(chooser, spread, NT)
        for tile in range(scratch.shape[0]):
            scratch[tile, pl.ds(t, owners, stride=lat_dev), :] = chosen[:, tile * LANES : (tile + 1) * LANES]
        return carry

    lax.fori_loop(0, lat_dev, one_latitude, 0, unroll=4)
    extra = jnp.broadcast_to(listed[...], (8, LANES))
    for o in range(owners):
        parts = []
        for tile in range(scratch.shape[0]):
            parts.append(scratch[tile, o * lat_dev : (o + 1) * lat_dev, :])
        parts.append(extra)
        message[o] = jnp.concatenate(parts, axis=0).astype(jnp.bfloat16)


def spectral_kernel(arrived, tables, damping, spectral, message, turned, rows_at, listed, row_of, listed_sem):
    step = pl.program_id(0)
    slots = damping.shape[0]
    bands = arrived.shape[0]
    tiles = turned.shape[0] // LANES
    lat_dev = (arrived.shape[1] - 8) // tiles
    lists = pltpu.make_async_copy(listed, row_of, listed_sem)
    per_slot = turned.shape[0] // slots
    half = per_slot // 2
    field_rows = half // 3
    latitudes = bands * lat_dev

    @pl.when(step == 0)
    def _():
        wide = arrived[...].astype(jnp.float32)
        band = lax.broadcasted_iota(jnp.int32, (bands, LANES), 0)
        listed[...] = (wide[:, tiles * lat_dev, :].astype(jnp.int32) + band * lat_dev) * 8
        lists.start()
        unit = identity(LANES)
        for tile in range(tiles):
            columns = wide[:, tile * lat_dev : (tile + 1) * lat_dev, :].reshape(latitudes, LANES)
            turned[tile * LANES : (tile + 1) * LANES, :] = mxu(unit, columns.astype(jnp.bfloat16), NT).astype(
                jnp.bfloat16
            )

    table = tables[0]
    own = turned[pl.ds(pl.multiple_of(step * per_slot, 16), per_slot), :]
    spectra = mxu(own, table, NN)
    damped = (spectra * damping[pl.ds(step, 1), :]).astype(jnp.bfloat16)
    spectral[0] = damped
    gap = jnp.zeros((LANES - half, damped.shape[1]), jnp.bfloat16)
    sides = []
    for part in range(2):
        for field in range(3):
            at = (2 * field + part) * field_rows
            sides.append(damped[at : at + field_rows])
        sides.append(gap)
    sides = jnp.concatenate(sides, axis=0)
    chunk = 256
    for at in range(0, latitudes, chunk):
        back = mxu(table[at : at + chunk], sides, NT)
        for part in range(2):
            rows_at[pl.ds(at * 2 * slots + step * 2 + part, chunk, stride=2 * slots), :] = back[
                :, part * LANES : (part + 1) * LANES
            ]

    @pl.when(step == slots - 1)
    def _():
        lists.wait()
        receivers, message_rows, message_lanes = message.shape
        lane = lax.broadcasted_iota(jnp.int32, (8, LANES), 1)
        wide_tiles = message_lanes // LANES

        def one_receiver(r, carry):
            for pair in range(message_rows // 16):
                halves = []
                for side in range(2):
                    built = [None] * wide_tiles
                    for e in range(8):
                        entry = (pair * 2 + side) * 8 + e
                        at = pl.multiple_of(row_of[entry // 2, 2 * r + entry % 2], 8)
                        row = rows_at[pl.ds(at, 8), :]
                        start = e * half
                        if start % LANES:
                            row = pltpu.roll(row, start % LANES, 1)
                        for tile in range(start // LANES, (start + half - 1) // LANES + 1):
                            first = start - tile * LANES
                            if built[tile] is None:
                                built[tile] = row
                            else:
                                built[tile] = jnp.where(lane >= first, row, built[tile])
                    halves.append(jnp.concatenate(built, axis=1))
                both = jnp.concatenate(halves, axis=0).astype(jnp.bfloat16)
                message[r, pair * 16 : (pair + 1) * 16, :] = both
            return carry

        lax.fori_loop(0, receivers, one_receiver, 0)


def block_kernel(column_of, received, zonal, blocks, lowest, lowest_scratch):
    owners, message_rows, message_lanes = received.shape
    unit = identity(LANES)
    half = message_lanes // 8
    groups = message_rows // 8
    entries = blocks.shape[0]
    for pair in range(groups // 2):
        wide = received[:, pair * 16 : (pair + 1) * 16, :].astype(jnp.float32)
        for side in range(2):
            group = pair * 2 + side
            own = wide[:, side * 8 : (side + 1) * 8, :].reshape(owners * 8, message_lanes).astype(jnp.bfloat16)
            turned = [
                mxu(unit, own[:, tile * LANES : (tile + 1) * LANES], NT).astype(jnp.bfloat16)
                for tile in range(message_lanes // LANES)
            ]
            turned = jnp.concatenate(turned, axis=0)
            for e in range(8):
                entry = group * 8 + e
                made = mxu(turned[e * half : (e + 1) * half], zonal[column_of[entry]], NN)
                blocks[entry] = made.astype(jnp.bfloat16)
                for field in range(3):
                    lowest_scratch[field * entries + entry : field * entries + entry + 1, :] = made[
                        field * 16 : field * 16 + 1, :
                    ]
    lowest[...] = lowest_scratch[...].astype(jnp.bfloat16)


def arrive_kernel(stencil, at_top, blocks, above, hweight, vweight, arrival, wide):
    entries = blocks.shape[0]
    step = pl.program_id(0)
    rows, fields, levels, _ = arrival.shape

    @pl.when(step == 0)
    def _():
        top = at_top[0] == 1

        def widen(entry, carry):
            block = blocks[entry].astype(jnp.float32)
            wide[entry, 0 : fields * levels, :] = block
            for field in range(fields):
                own_last = block[(field + 1) * levels - 1 : (field + 1) * levels, :]
                over = above[pl.ds(field * entries + entry, 1), :]
                wide[entry, pl.ds(fields * levels + field, 1), :] = jnp.where(top, own_last, over)
            return carry

        lax.fori_loop(0, entries, widen, 0, unroll=4)

    level = lax.broadcasted_iota(jnp.int32, (levels, LANES), 0)

    def one_row(a, carry):
        total = None
        for q in range(4):
            place = stencil[(step * rows + a) * 4 + q]
            term = hweight[a, pl.ds(q, 1), :] * wide[place]
            total = term if total is None else total + term
        upper = vweight[a]
        for field in range(fields):
            here = total[field * levels : (field + 1) * levels]
            over = jnp.where(
                level == levels - 1,
                total[fields * levels + field : fields * levels + field + 1],
                pltpu.roll(here, levels - 1, 0),
            )
            arrival[a, field] = ((1.0 - upper) * here + upper * over).astype(jnp.bfloat16)
        return carry

    lax.fori_loop(0, rows, one_row, 0, unroll=4)


def whole(memory):
    return pl.BlockSpec(memory_space=memory)


def per_device(fourier, gauss, legendre, owner, send_list, stencil, hweight, vweight):
    lat_count = lax.axis_size("lat")
    device_row = lax.axis_index("lat")
    lat_dev, fields, levels, columns = fourier.shape
    wave_total = columns // 2
    slot_most = legendre.shape[1]
    degrees = legendre.shape[3]
    latitudes = legendre.shape[2]
    slot_count = lat_count * slot_most
    capacity = send_list.shape[2]
    arrivals = stencil.shape[0]
    half = fields * levels
    per_slot = 2 * half
    message_lanes = slot_most * per_slot
    tiles = message_lanes // LANES
    entries = lat_count * capacity

    owners = owner[:, 0]
    wave_index = jnp.arange(wave_total, dtype=jnp.int32)
    earlier = (owners[:, None] == owners[None, :]) & (wave_index[:, None] < wave_index[None, :])
    slot_rank = jnp.sum(earlier.astype(jnp.int32), axis=0)
    slot_of = owners * slot_most + slot_rank
    wave_number = wave_index * (degrees // wave_total)
    ids = send_list[0].reshape(1, entries)
    listed = jnp.concatenate([ids // BLOCKS_X, ids % BLOCKS_X], axis=1).astype(jnp.float32)

    column_index = jnp.arange(columns, dtype=jnp.int32)
    owner_column = jnp.repeat(owners, 2)
    rank_column = jnp.repeat(slot_rank, 2)
    owned_by = (jnp.arange(lat_count, dtype=jnp.int32)[:, None] == owner_column[None, :]).astype(jnp.bfloat16)
    slot_mask = (
        jnp.arange(2 * slot_most, dtype=jnp.int32)[:, None] == (2 * rank_column + column_index % 2)[None, :]
    ).astype(jnp.bfloat16)
    vmem = whole(pltpu.VMEM)
    smem = whole(pltpu.SMEM)
    message_one = pl.pallas_call(
        pack_kernel,
        out_shape=jax.ShapeDtypeStruct((lat_count, tiles * lat_dev + 8, LANES), jnp.bfloat16),
        in_specs=[smem, vmem, vmem, vmem, vmem],
        out_specs=vmem,
        scratch_shapes=[pltpu.VMEM((tiles, lat_count * lat_dev, LANES), jnp.float32)],
        compiler_params=pltpu.CompilerParams(vmem_limit_bytes=48 * 2**20),
        name="pack",
    )(gauss, fourier, owned_by, slot_mask, listed)
    arrived = lax.all_to_all(message_one, "lat", split_axis=0, concat_axis=0, tiled=True)

    placed = (slot_of[:, None] == jnp.arange(slot_count, dtype=jnp.int32)[None, :]).astype(jnp.int32)
    owned = lax.dynamic_slice_in_dim(placed, device_row * slot_most, slot_most, 1)
    filled = jnp.sum(owned, axis=0) > 0
    slot_wave = jnp.sum(owned * wave_number[:, None], axis=0)
    degree_index = jnp.arange(degrees, dtype=jnp.int32)
    keep_mask = (filled[:, None] & (degree_index[None, :] >= slot_wave[:, None])).astype(jnp.float32)
    damping = keep_mask * damping_curve(degrees)[None, :]

    message_shape = (lat_count, entries // 8 * slot_most * 2, 8 * half)
    spectral_rows, message_two = pl.pallas_call(
        spectral_kernel,
        grid=(slot_most,),
        in_specs=[
            pl.BlockSpec(arrived.shape, lambda s: (0, 0, 0)),
            pl.BlockSpec((1, latitudes, degrees), lambda s: (s, 0, 0)),
            pl.BlockSpec((slot_most, degrees), lambda s: (0, 0)),
        ],
        out_specs=[
            pl.BlockSpec((1, per_slot, degrees), lambda s: (s, 0, 0)),
            pl.BlockSpec(message_shape, lambda s: (0, 0, 0)),
        ],
        scratch_shapes=[
            pltpu.VMEM((message_lanes, latitudes), jnp.bfloat16),
            pltpu.VMEM((latitudes * 2 * slot_most, LANES), jnp.float32),
            pltpu.VMEM((lat_count, LANES), jnp.int32),
            pltpu.SMEM((lat_count, LANES), jnp.int32),
            pltpu.SemaphoreType.DMA,
        ],
        out_shape=[
            jax.ShapeDtypeStruct((slot_most, per_slot, degrees), jnp.bfloat16),
            jax.ShapeDtypeStruct(message_shape, jnp.bfloat16),
        ],
        compiler_params=pltpu.CompilerParams(vmem_limit_bytes=48 * 2**20),
        name="spectral",
    )(arrived, legendre[0], damping)
    received = lax.all_to_all(message_two, "lat", split_axis=0, concat_axis=0, tiled=True)

    spectral = jnp.transpose(
        spectral_rows.reshape(slot_most, fields, 2, levels, degrees), (0, 1, 3, 2, 4)
    )
    slot_waves = jnp.sum(placed * wave_number[:, None], axis=0)
    present = (jnp.sum(placed, axis=0) > 0).astype(jnp.float32)
    points = jnp.arange(NLON, dtype=jnp.int32).reshape(BLOCKS_X, 1, 1, BLK)
    phases = slot_waves[None, :, None, None] * points % NLON
    angles = phases.astype(jnp.float32) * (2.0 * math.pi / NLON)
    norm_factor = present[None, :, None, None] / math.sqrt(wave_total)
    zonal = jnp.concatenate([jnp.cos(angles) * norm_factor, -jnp.sin(angles) * norm_factor], axis=2)
    zonal = zonal.astype(jnp.bfloat16).reshape(BLOCKS_X, slot_count * 2, BLK)
    all_columns = arrived[:, tiles * lat_dev, entries:]
    column_of = lax.dynamic_slice_in_dim(all_columns, device_row * capacity, capacity, 1)
    column_of = column_of.astype(jnp.int32).reshape(-1)
    blocks, lowest = pl.pallas_call(
        block_kernel,
        out_shape=[
            jax.ShapeDtypeStruct((entries, half, BLK), jnp.bfloat16),
            jax.ShapeDtypeStruct((fields * entries, BLK), jnp.bfloat16),
        ],
        in_specs=[smem, vmem, vmem],
        out_specs=[vmem, vmem],
        scratch_shapes=[pltpu.VMEM((fields * entries, BLK), jnp.float32)],
        compiler_params=pltpu.CompilerParams(vmem_limit_bytes=48 * 2**20),
        name="blocks",
    )(column_of, received, zonal)

    lev_count = lax.axis_size("lev")
    above = lax.ppermute(lowest, "lev", [(i, i - 1) for i in range(1, lev_count)])
    at_top = (lax.axis_index("lev") == lev_count - 1).astype(jnp.int32).reshape(1)
    vertical = jnp.broadcast_to(vweight[:, :, None], (arrivals, levels, BLK))
    step_rows = 32
    arrival = pl.pallas_call(
        arrive_kernel,
        grid_spec=pltpu.PrefetchScalarGridSpec(
            num_scalar_prefetch=2,
            grid=(arrivals // step_rows,),
            in_specs=[
                pl.BlockSpec((entries, half, BLK), lambda i, *_: (0, 0, 0)),
                pl.BlockSpec((fields * entries, BLK), lambda i, *_: (0, 0)),
                pl.BlockSpec((step_rows, 4, BLK), lambda i, *_: (i, 0, 0)),
                pl.BlockSpec((step_rows, levels, BLK), lambda i, *_: (i, 0, 0)),
            ],
            out_specs=pl.BlockSpec((step_rows, fields, levels, BLK), lambda i, *_: (i, 0, 0, 0)),
            scratch_shapes=[pltpu.VMEM((entries, half + 8, BLK), jnp.float32)],
        ),
        out_shape=jax.ShapeDtypeStruct((arrivals, fields, levels, BLK), jnp.bfloat16),
        compiler_params=pltpu.CompilerParams(vmem_limit_bytes=48 * 2**20),
        name="arrive",
    )(stencil.reshape(-1), at_top, blocks, above.astype(jnp.float32), hweight, vertical)
    return (spectral[None], arrival)


def solution(mesh):
    return jax.shard_map(
        per_device,
        mesh=mesh,
        in_specs=(
            P("lat", None, "lev", None),
            P("lat"),
            P("lat", None, None, None),
            P(),
            P("lat", None, None),
            P("lat", None),
            P("lat", None, None),
            P("lat", "lev"),
        ),
        out_specs=(P("lat", None, None, "lev", None, None), P("lat", None, "lev", None)),
        check_vma=False,
    )
```

```python
import math

import jax
import jax.numpy as jnp
from jax import lax
from jax.experimental import pallas as pl
from jax.experimental.pallas import tpu as pltpu
from jax.sharding import PartitionSpec as P

NLON = 2560
BLK = 128
BLOCKS_X = NLON // BLK
LANES = 128

diffusion = 3.0

NT = (((1,), (1,)), ((), ()))
NN = (((1,), (0,)), ((), ()))


def mxu(left, right, dims):
    return lax.dot_general(left, right, dims, preferred_element_type=jnp.float32)


def identity(size):
    rows = lax.broadcasted_iota(jnp.int32, (size, size), 0)
    columns = lax.broadcasted_iota(jnp.int32, (size, size), 1)
    return (rows == columns).astype(jnp.float32).astype(jnp.bfloat16)


def damping_curve(degrees):
    order_n = jnp.arange(degrees, dtype=jnp.float32)
    ratio = order_n * (order_n + 1.0) / float(degrees * (degrees - 1))
    return 1.0 / (1.0 + diffusion * ratio * ratio)


def pack_kernel(owner, send_ids, gauss, fourier, message, scratch, owned_by, slot_mask, weight):
    step = pl.program_id(0)
    chunk, fields, levels, columns = fourier.shape
    owners = owned_by.shape[0]
    lat_dev = weight.shape[0]
    tiles = scratch.shape[0]

    @pl.when(step == 0)
    def _():
        waves = owner.shape[1]
        wave_at = lax.broadcasted_iota(jnp.int32, (waves, columns), 0)
        column = lax.broadcasted_iota(jnp.int32, (waves, columns), 1)
        square_row = lax.broadcasted_iota(jnp.int32, (waves, waves), 0)
        square_column = lax.broadcasted_iota(jnp.int32, (waves, waves), 1)
        listed = jnp.broadcast_to(owner[...], (waves, waves))
        upright = jnp.sum(jnp.where(square_row == square_column, listed, 0), axis=1, keepdims=True)
        upright = jnp.broadcast_to(upright, (waves, columns))
        column_owner = jnp.sum(jnp.where(wave_at == column // 2, upright, 0), axis=0, keepdims=True)
        earlier = (upright == jnp.broadcast_to(column_owner, (waves, columns))) & (wave_at < column // 2)
        column_rank = jnp.sum(jnp.where(earlier, 1, 0), axis=0, keepdims=True)
        owner_at = lax.broadcasted_iota(jnp.int32, (owners, columns), 0)
        owned_by[...] = jnp.where(owner_at == column_owner, 1.0, 0.0).astype(jnp.bfloat16)
        parts_at = lax.broadcasted_iota(jnp.int32, (16, columns), 0)
        part_column = lax.broadcasted_iota(jnp.int32, (16, columns), 1)
        in_slot = parts_at == 2 * column_rank + part_column % 2
        slot_mask[...] = jnp.where(in_slot, 1.0, 0.0).astype(jnp.bfloat16)
        turn_row = lax.broadcasted_iota(jnp.int32, (lat_dev, lat_dev), 0)
        turn_column = lax.broadcasted_iota(jnp.int32, (lat_dev, lat_dev), 1)
        weights = jnp.where(turn_row == turn_column, jnp.broadcast_to(gauss[...], (lat_dev, lat_dev)), 0.0)
        weight[...] = jnp.broadcast_to(jnp.sum(weights, axis=1, keepdims=True), weight.shape)

    chooser = owned_by[...]
    masks = [slot_mask[i : i + 1, :] for i in range(2 * (tiles * LANES) // (2 * fields * levels))]
    for k in range(chunk):
        t = step * chunk + k
        rows = fourier[k].reshape(fields * levels, columns).astype(jnp.float32)
        rows = (rows * weight[pl.ds(t, 1), :]).astype(jnp.bfloat16)
        parts = []
        for slot in range(len(masks) // 2):
            for field in range(fields):
                for part in range(2):
                    parts.append(rows[field * levels : (field + 1) * levels] * masks[2 * slot + part])
        spread = jnp.concatenate(parts, axis=0)
        chosen = mxu(chooser, spread, NT)
        for tile in range(tiles):
            scratch[tile, pl.ds(t, owners, stride=lat_dev), :] = chosen[:, tile * LANES : (tile + 1) * LANES]

    @pl.when(step == pl.num_programs(0) - 1)
    def _():
        ids = send_ids[...].astype(jnp.float32)
        in_row = jnp.floor((ids + 0.5) * (1.0 / BLOCKS_X))
        in_column = ids - in_row * BLOCKS_X
        sides = [in_row[k : k + 1] for k in range(ids.shape[0])] + [in_column[k : k + 1] for k in range(ids.shape[0])]
        extra = jnp.broadcast_to(jnp.concatenate(sides, axis=1), (8, LANES))
        for o in range(owners):
            parts = [scratch[tile, o * lat_dev : (o + 1) * lat_dev, :] for tile in range(tiles)]
            message[o] = jnp.concatenate(parts + [extra], axis=0).astype(jnp.bfloat16)


def spectral_kernel(arrived, tables, damping, spectral, message, turned, rows_at, listed, row_of, listed_sem):
    slots, per_slot, degrees = spectral.shape
    half = per_slot // 2
    field_rows = half // 3
    bands = arrived.shape[0]
    tiles = turned.shape[0] // LANES
    lat_dev = (arrived.shape[1] - 8) // tiles
    latitudes = bands * lat_dev
    receivers, message_rows, message_lanes = message.shape
    lists = pltpu.make_async_copy(listed, row_of, listed_sem)

    wide = arrived[...].astype(jnp.float32)
    band = lax.broadcasted_iota(jnp.int32, (bands, LANES), 0)
    listed[...] = (wide[:, tiles * lat_dev, :].astype(jnp.int32) + band * lat_dev) * 8
    lists.start()
    unit = identity(LANES)
    for tile in range(tiles):
        columns = wide[:, tile * lat_dev : (tile + 1) * lat_dev, :].reshape(latitudes, LANES)
        turned[tile * LANES : (tile + 1) * LANES, :] = mxu(unit, columns.astype(jnp.bfloat16), NT).astype(jnp.bfloat16)

    gap = jnp.zeros((LANES - half, degrees), jnp.bfloat16)
    chunk = 256
    for slot in range(slots):
        own = turned[slot * per_slot : (slot + 1) * per_slot, :]
        spectra = mxu(own, tables[slot], NN)
        damped = (spectra * damping[slot : slot + 1, :]).astype(jnp.bfloat16)
        spectral[slot] = damped
        sides = []
        for part in range(2):
            for field in range(3):
                at = (2 * field + part) * field_rows
                sides.append(damped[at : at + field_rows])
            sides.append(gap)
        sides = jnp.concatenate(sides, axis=0)
        for at in range(0, latitudes, chunk):
            back = mxu(tables[slot, at : at + chunk, :], sides, NT)
            for part in range(2):
                rows_at[pl.ds(at * 2 * slots + slot * 2 + part, chunk, stride=2 * slots), :] = back[
                    :, part * LANES : (part + 1) * LANES
                ]

    lists.wait()
    lane = lax.broadcasted_iota(jnp.int32, (8, LANES), 1)
    wide_tiles = message_lanes // LANES

    def one_receiver(r, carry):
        for pair in range(message_rows // 16):
            halves = []
            for side in range(2):
                built = [None] * wide_tiles
                for e in range(8):
                    entry = (pair * 2 + side) * 8 + e
                    at = pl.multiple_of(row_of[entry // 2, receivers * (entry % 2) + r], 8)
                    row = rows_at[pl.ds(at, 8), :]
                    start = e * half
                    if start % LANES:
                        row = pltpu.roll(row, start % LANES, 1)
                    for tile in range(start // LANES, (start + half - 1) // LANES + 1):
                        first = start - tile * LANES
                        if built[tile] is None:
                            built[tile] = row
                        else:
                            built[tile] = jnp.where(lane >= first, row, built[tile])
                halves.append(jnp.concatenate(built, axis=1))
            both = jnp.concatenate(halves, axis=0).astype(jnp.bfloat16)
            message[r, pair * 16 : (pair + 1) * 16, :] = both
        return carry

    lax.fori_loop(0, receivers, one_receiver, 0, unroll=4)


def block_kernel(column_of, received, zonal, blocks, lowest, lowest_scratch):
    owners, message_rows, message_lanes = received.shape
    unit = identity(LANES)
    half = message_lanes // 8
    groups = message_rows // 8
    entries = blocks.shape[0]
    for pair in range(groups // 2):
        wide = received[:, pair * 16 : (pair + 1) * 16, :].astype(jnp.float32)
        for side in range(2):
            group = pair * 2 + side
            own = wide[:, side * 8 : (side + 1) * 8, :].reshape(owners * 8, message_lanes).astype(jnp.bfloat16)
            turned = [
                mxu(unit, own[:, tile * LANES : (tile + 1) * LANES], NT).astype(jnp.bfloat16)
                for tile in range(message_lanes // LANES)
            ]
            turned = jnp.concatenate(turned, axis=0)
            for e in range(8):
                entry = group * 8 + e
                made = mxu(turned[e * half : (e + 1) * half], zonal[column_of[entry]], NN)
                blocks[entry] = made.astype(jnp.bfloat16)
                for field in range(3):
                    lowest_scratch[field * entries + entry : field * entries + entry + 1, :] = made[
                        field * 16 : field * 16 + 1, :
                    ]
    lowest[...] = lowest_scratch[...].astype(jnp.bfloat16)


def arrive_kernel(stencil, at_top, blocks, above, hweight, vweight, arrival, wide, over_rows):
    entries = blocks.shape[0]
    step = pl.program_id(0)
    rows, fields, levels, _ = arrival.shape

    @pl.when(step == 0)
    def _():
        top = at_top[0] == 1
        over_rows[...] = above[...].astype(jnp.float32)

        def widen(entry, carry):
            block = blocks[entry].astype(jnp.float32)
            wide[entry, 0 : fields * levels, :] = block
            for field in range(fields):
                own_last = block[(field + 1) * levels - 1 : (field + 1) * levels, :]
                over = over_rows[pl.ds(field * entries + entry, 1), :]
                wide[entry, pl.ds(fields * levels + field, 1), :] = jnp.where(top, own_last, over)
            return carry

        lax.fori_loop(0, entries, widen, 0, unroll=4)

    level = lax.broadcasted_iota(jnp.int32, (levels, LANES), 0)

    def one_row(a, carry):
        total = None
        for q in range(4):
            place = stencil[(step * rows + a) * 4 + q]
            term = hweight[a, pl.ds(q, 1), :] * wide[place]
            total = term if total is None else total + term
        upper = vweight[a]
        for field in range(fields):
            here = total[field * levels : (field + 1) * levels]
            over = jnp.where(
                level == levels - 1,
                total[fields * levels + field : fields * levels + field + 1],
                pltpu.roll(here, levels - 1, 0),
            )
            arrival[a, field] = ((1.0 - upper) * here + upper * over).astype(jnp.bfloat16)
        return carry

    lax.fori_loop(0, rows, one_row, 0, unroll=4)


def whole(memory):
    return pl.BlockSpec(memory_space=memory)


def per_device(fourier, gauss, legendre, owner, send_list, stencil, hweight, vweight):
    lat_count = lax.axis_size("lat")
    device_row = lax.axis_index("lat")
    lat_dev, fields, levels, columns = fourier.shape
    wave_total = columns // 2
    slot_most = legendre.shape[1]
    degrees = legendre.shape[3]
    latitudes = legendre.shape[2]
    slot_count = lat_count * slot_most
    capacity = send_list.shape[2]
    arrivals = stencil.shape[0]
    half = fields * levels
    per_slot = 2 * half
    message_lanes = slot_most * per_slot
    tiles = message_lanes // LANES
    entries = lat_count * capacity

    owners = owner[:, 0]
    wave_index = jnp.arange(wave_total, dtype=jnp.int32)
    earlier = (owners[:, None] == owners[None, :]) & (wave_index[:, None] < wave_index[None, :])
    slot_rank = jnp.sum(earlier.astype(jnp.int32), axis=0)
    slot_of = owners * slot_most + slot_rank
    wave_number = wave_index * (degrees // wave_total)
    vmem = whole(pltpu.VMEM)
    smem = whole(pltpu.SMEM)
    chunk = 8
    message_one = pl.pallas_call(
        pack_kernel,
        grid=(lat_dev // chunk,),
        out_shape=jax.ShapeDtypeStruct((lat_count, tiles * lat_dev + 8, LANES), jnp.bfloat16),
        in_specs=[
            pl.BlockSpec((1, wave_total), lambda i: (0, 0)),
            pl.BlockSpec((capacity, lat_count), lambda i: (0, 0)),
            pl.BlockSpec((1, lat_dev), lambda i: (0, 0)),
            pl.BlockSpec((chunk, fields, levels, columns), lambda i: (i, 0, 0, 0)),
        ],
        out_specs=pl.BlockSpec((lat_count, tiles * lat_dev + 8, LANES), lambda i: (0, 0, 0)),
        scratch_shapes=[
            pltpu.VMEM((tiles, lat_count * lat_dev, LANES), jnp.float32),
            pltpu.VMEM((lat_count, columns), jnp.bfloat16),
            pltpu.VMEM((16, columns), jnp.bfloat16),
            pltpu.VMEM((lat_dev, columns), jnp.float32),
        ],
        compiler_params=pltpu.CompilerParams(vmem_limit_bytes=16 * 2**20),
        name="pack",
    )(owner.reshape(1, wave_total), send_list[0].T, gauss.reshape(1, lat_dev), fourier)
    arrived = lax.all_to_all(message_one, "lat", split_axis=0, concat_axis=0, tiled=True)

    placed = (slot_of[:, None] == jnp.arange(slot_count, dtype=jnp.int32)[None, :]).astype(jnp.int32)
    owned = lax.dynamic_slice_in_dim(placed, device_row * slot_most, slot_most, 1)
    filled = jnp.sum(owned, axis=0) > 0
    slot_wave = jnp.sum(owned * wave_number[:, None], axis=0)
    degree_index = jnp.arange(degrees, dtype=jnp.int32)
    keep_mask = (filled[:, None] & (degree_index[None, :] >= slot_wave[:, None])).astype(jnp.float32)
    damping = keep_mask * damping_curve(degrees)[None, :]

    message_shape = (lat_count, entries // 8 * slot_most * 2, 8 * half)
    spectral_rows, message_two = pl.pallas_call(
        spectral_kernel,
        in_specs=[vmem, vmem, vmem],
        out_specs=[vmem, vmem],
        scratch_shapes=[
            pltpu.VMEM((message_lanes, latitudes), jnp.bfloat16),
            pltpu.VMEM((latitudes * 2 * slot_most, LANES), jnp.float32),
            pltpu.VMEM((lat_count, LANES), jnp.int32),
            pltpu.SMEM((lat_count, LANES), jnp.int32),
            pltpu.SemaphoreType.DMA,
        ],
        out_shape=[
            jax.ShapeDtypeStruct((slot_most, per_slot, degrees), jnp.bfloat16),
            jax.ShapeDtypeStruct(message_shape, jnp.bfloat16),
        ],
        compiler_params=pltpu.CompilerParams(vmem_limit_bytes=24 * 2**20),
        name="spectral",
    )(arrived, legendre[0], damping)
    received = lax.all_to_all(message_two, "lat", split_axis=0, concat_axis=0, tiled=True)

    spectral = jnp.transpose(
        spectral_rows.reshape(slot_most, fields, 2, levels, degrees), (0, 1, 3, 2, 4)
    )
    slot_waves = jnp.sum(placed * wave_number[:, None], axis=0)
    present = (jnp.sum(placed, axis=0) > 0).astype(jnp.float32)
    points = jnp.arange(NLON, dtype=jnp.int32).reshape(BLOCKS_X, 1, 1, BLK)
    phases = slot_waves[None, :, None, None] * points % NLON
    angles = phases.astype(jnp.float32) * (2.0 * math.pi / NLON)
    norm_factor = present[None, :, None, None] / math.sqrt(wave_total)
    zonal = jnp.concatenate([jnp.cos(angles) * norm_factor, -jnp.sin(angles) * norm_factor], axis=2)
    zonal = zonal.astype(jnp.bfloat16).reshape(BLOCKS_X, slot_count * 2, BLK)
    all_columns = arrived[:, tiles * lat_dev, entries:].reshape(lat_count, capacity, lat_count)
    column_of = lax.dynamic_index_in_dim(all_columns, device_row, 2, keepdims=False)
    column_of = column_of.astype(jnp.int32).reshape(-1)
    lev_count = lax.axis_size("lev")
    at_top = (lax.axis_index("lev") == lev_count - 1).astype(jnp.int32).reshape(1)
    vertical = jnp.broadcast_to(vweight[:, :, None], (arrivals, levels, BLK))
    corners = stencil.reshape(-1)
    received, vertical, corners, at_top = lax.optimization_barrier((received, vertical, corners, at_top))
    blocks, lowest = pl.pallas_call(
        block_kernel,
        out_shape=[
            jax.ShapeDtypeStruct((entries, half, BLK), jnp.bfloat16),
            jax.ShapeDtypeStruct((fields * entries, BLK), jnp.bfloat16),
        ],
        in_specs=[smem, vmem, vmem],
        out_specs=[vmem, vmem],
        scratch_shapes=[pltpu.VMEM((fields * entries, BLK), jnp.float32)],
        compiler_params=pltpu.CompilerParams(vmem_limit_bytes=16 * 2**20),
        name="blocks",
    )(column_of, received, zonal)

    above = lax.ppermute(lowest, "lev", [(i, i - 1) for i in range(1, lev_count)])
    step_rows = 32
    arrival = pl.pallas_call(
        arrive_kernel,
        grid_spec=pltpu.PrefetchScalarGridSpec(
            num_scalar_prefetch=2,
            grid=(arrivals // step_rows,),
            in_specs=[
                pl.BlockSpec((entries, half, BLK), lambda i, *_: (0, 0, 0)),
                pl.BlockSpec((fields * entries, BLK), lambda i, *_: (0, 0)),
                pl.BlockSpec((step_rows, 4, BLK), lambda i, *_: (i, 0, 0)),
                pl.BlockSpec((step_rows, levels, BLK), lambda i, *_: (i, 0, 0)),
            ],
            out_specs=pl.BlockSpec((step_rows, fields, levels, BLK), lambda i, *_: (i, 0, 0, 0)),
            scratch_shapes=[
                pltpu.VMEM((entries, half + 8, BLK), jnp.float32),
                pltpu.VMEM((fields * entries, BLK), jnp.float32),
            ],
        ),
        out_shape=jax.ShapeDtypeStruct((arrivals, fields, levels, BLK), jnp.bfloat16),
        compiler_params=pltpu.CompilerParams(vmem_limit_bytes=16 * 2**20),
        name="arrive",
    )(corners, at_top, blocks, above, hweight, vertical)
    return (spectral[None], arrival)


def solution(mesh):
    return jax.shard_map(
        per_device,
        mesh=mesh,
        in_specs=(
            P("lat", None, "lev", None),
            P("lat"),
            P("lat", None, None, None),
            P(),
            P("lat", None, None),
            P("lat", None),
            P("lat", None, None),
            P("lat", "lev"),
        ),
        out_specs=(P("lat", None, None, "lev", None, None), P("lat", None, "lev", None)),
        check_vma=False,
    )
```

```python
import math

import jax
import jax.numpy as jnp
from jax import lax
from jax.experimental import pallas as pl
from jax.experimental.pallas import tpu as pltpu
from jax.sharding import PartitionSpec as P

NLON = 2560
BLK = 128
BLOCKS_X = NLON // BLK
LANES = 128
GRANT = 56 * 2**20

diffusion = 3.0

NT = (((1,), (1,)), ((), ()))
NN = (((1,), (0,)), ((), ()))


def mxu(left, right, dims):
    return lax.dot_general(left, right, dims, preferred_element_type=jnp.float32)


def identity(size):
    rows = lax.broadcasted_iota(jnp.int32, (size, size), 0)
    columns = lax.broadcasted_iota(jnp.int32, (size, size), 1)
    return (rows == columns).astype(jnp.float32).astype(jnp.bfloat16)


def damping_curve(degrees):
    order_n = jnp.arange(degrees, dtype=jnp.float32)
    ratio = order_n * (order_n + 1.0) / float(degrees * (degrees - 1))
    return 1.0 / (1.0 + diffusion * ratio * ratio)


def pack_kernel(
    owner_in, ids_in, gauss_in, fourier_in, message, owner, send_ids, gauss, fourier, packed, scratch, weight, in_sem, out_sem
):
    lat_dev, fields, levels, columns = fourier.shape
    owners = packed.shape[0]
    tiles = scratch.shape[0]
    slots = (tiles * LANES) // (2 * fields * levels)
    chunk = 8
    pieces = lat_dev // chunk
    small = [
        pltpu.make_async_copy(source, target, in_sem.at[pieces + i])
        for i, (source, target) in enumerate(((owner_in, owner), (ids_in, send_ids), (gauss_in, gauss)))
    ]
    large = [
        pltpu.make_async_copy(
            fourier_in.at[pl.ds(i * chunk, chunk)], fourier.at[pl.ds(i * chunk, chunk)], in_sem.at[i]
        )
        for i in range(pieces)
    ]
    for copy in small + large:
        copy.start()
    for copy in small:
        copy.wait()

    waves = owner.shape[1]
    wave_at = lax.broadcasted_iota(jnp.int32, (waves, columns), 0)
    column = lax.broadcasted_iota(jnp.int32, (waves, columns), 1)
    square_row = lax.broadcasted_iota(jnp.int32, (waves, waves), 0)
    square_column = lax.broadcasted_iota(jnp.int32, (waves, waves), 1)
    listed = jnp.broadcast_to(owner[...], (waves, waves))
    upright = jnp.sum(jnp.where(square_row == square_column, listed, 0), axis=1, keepdims=True)
    upright = jnp.broadcast_to(upright, (waves, columns))
    column_owner = jnp.sum(jnp.where(wave_at == column // 2, upright, 0), axis=0, keepdims=True)
    earlier = (upright == jnp.broadcast_to(column_owner, (waves, columns))) & (wave_at < column // 2)
    column_rank = jnp.sum(jnp.where(earlier, 1, 0), axis=0, keepdims=True)
    owner_at = lax.broadcasted_iota(jnp.int32, (owners, columns), 0)
    chooser = jnp.where(owner_at == column_owner, 1.0, 0.0).astype(jnp.bfloat16)
    part_of = 2 * column_rank + lax.broadcasted_iota(jnp.int32, (1, columns), 1) % 2
    masks = [
        jnp.broadcast_to(jnp.where(part_of == i, 1.0, 0.0), (levels, columns)).astype(jnp.bfloat16)
        for i in range(2 * slots)
    ]
    turn_row = lax.broadcasted_iota(jnp.int32, (lat_dev, lat_dev), 0)
    turn_column = lax.broadcasted_iota(jnp.int32, (lat_dev, lat_dev), 1)
    weights = jnp.where(turn_row == turn_column, jnp.broadcast_to(gauss[...], (lat_dev, lat_dev)), 0.0)
    weight[...] = jnp.broadcast_to(jnp.sum(weights, axis=1, keepdims=True), weight.shape)

    for t in range(lat_dev):
        if t % chunk == 0:
            large[t // chunk].wait()
        rows = fourier[t].reshape(fields * levels, columns).astype(jnp.float32)
        rows = (rows * weight[t : t + 1, :]).astype(jnp.bfloat16)
        parts = []
        for slot in range(slots):
            for field in range(fields):
                for part in range(2):
                    parts.append(rows[field * levels : (field + 1) * levels] * masks[2 * slot + part])
        spread = jnp.concatenate(parts, axis=0)
        chosen = mxu(chooser, spread, NT)
        for tile in range(tiles):
            scratch[tile, pl.ds(t, owners, stride=lat_dev), :] = chosen[:, tile * LANES : (tile + 1) * LANES]

    ids = send_ids[...].astype(jnp.float32)
    in_row = jnp.floor((ids + 0.5) * (1.0 / BLOCKS_X))
    in_column = ids - in_row * BLOCKS_X
    sides = [in_row[k : k + 1] for k in range(ids.shape[0])] + [in_column[k : k + 1] for k in range(ids.shape[0])]
    extra = jnp.broadcast_to(jnp.concatenate(sides, axis=1), (8, LANES))
    group = 8
    copies = []
    for o in range(owners):
        parts = [scratch[tile, o * lat_dev : (o + 1) * lat_dev, :] for tile in range(tiles)]
        packed[o] = jnp.concatenate(parts + [extra], axis=0).astype(jnp.bfloat16)
        if o % group == group - 1:
            first = o + 1 - group
            copies.append(
                pltpu.make_async_copy(
                    packed.at[pl.ds(first, group)], message.at[pl.ds(first, group)], out_sem.at[o // group]
                )
            )
            copies[-1].start()
    for copy in copies:
        copy.wait()


def spectral_kernel(
    arrived, tables_in, damping, spectral, message, tables, made, turned, rows_at, listed, row_of, listed_sem, in_sem, out_sem
):
    slots, per_slot, degrees = spectral.shape
    fetches = [pltpu.make_async_copy(tables_in.at[i], tables.at[i], in_sem.at[i]) for i in range(slots)]
    for fetch in fetches:
        fetch.start()
    half = per_slot // 2
    field_rows = half // 3
    bands = arrived.shape[0]
    tiles = turned.shape[0] // LANES
    lat_dev = (arrived.shape[1] - 8) // tiles
    latitudes = bands * lat_dev
    receivers, message_rows, message_lanes = message.shape
    lists = pltpu.make_async_copy(listed, row_of, listed_sem)

    wide = arrived[...].astype(jnp.float32)
    band = lax.broadcasted_iota(jnp.int32, (bands, LANES), 0)
    listed[...] = (wide[:, tiles * lat_dev, :].astype(jnp.int32) + band * lat_dev) * 8
    lists.start()
    unit = identity(LANES)
    for tile in range(tiles):
        columns = wide[:, tile * lat_dev : (tile + 1) * lat_dev, :].reshape(latitudes, LANES)
        turned[tile * LANES : (tile + 1) * LANES, :] = mxu(unit, columns.astype(jnp.bfloat16), NT).astype(jnp.bfloat16)

    gap = jnp.zeros((LANES - half, degrees), jnp.bfloat16)
    chunk = 256
    for slot in range(slots):
        own = turned[slot * per_slot : (slot + 1) * per_slot, :]
        fetches[slot].wait()
        spectra = mxu(own, tables[slot], NN)
        damped = (spectra * damping[slot : slot + 1, :]).astype(jnp.bfloat16)
        spectral[slot] = damped
        sides = []
        for part in range(2):
            for field in range(3):
                at = (2 * field + part) * field_rows
                sides.append(damped[at : at + field_rows])
            sides.append(gap)
        sides = jnp.concatenate(sides, axis=0)
        for at in range(0, latitudes, chunk):
            back = mxu(tables[slot, at : at + chunk, :], sides, NT)
            for part in range(2):
                rows_at[pl.ds(at * 2 * slots + slot * 2 + part, chunk, stride=2 * slots), :] = back[
                    :, part * LANES : (part + 1) * LANES
                ]

    lists.wait()
    lane = lax.broadcasted_iota(jnp.int32, (8, LANES), 1)
    wide_tiles = message_lanes // LANES

    group = 4
    groups = receivers // group

    def send(g):
        at = pl.multiple_of(g * group, group)
        return pltpu.make_async_copy(made.at[pl.ds(at, group)], message.at[pl.ds(at, group)], out_sem.at[g])

    def one_group(g, carry):
        for k in range(group):
            r = g * group + k
            for pair in range(message_rows // 16):
                halves = []
                for side in range(2):
                    built = [None] * wide_tiles
                    for e in range(8):
                        entry = (pair * 2 + side) * 8 + e
                        at = pl.multiple_of(row_of[entry // 2, receivers * (entry % 2) + r], 8)
                        row = rows_at[pl.ds(at, 8), :]
                        start = e * half
                        if start % LANES:
                            row = pltpu.roll(row, start % LANES, 1)
                        for tile in range(start // LANES, (start + half - 1) // LANES + 1):
                            first = start - tile * LANES
                            if built[tile] is None:
                                built[tile] = row
                            else:
                                built[tile] = jnp.where(lane >= first, row, built[tile])
                    halves.append(jnp.concatenate(built, axis=1))
                both = jnp.concatenate(halves, axis=0).astype(jnp.bfloat16)
                made[r, pair * 16 : (pair + 1) * 16, :] = both
        send(g).start()
        return carry

    lax.fori_loop(0, groups, one_group, 0)
    for g in range(groups):
        send(g).wait()


def block_kernel(column_of, received, zonal, blocks, lowest, lowest_scratch):
    owners, message_rows, message_lanes = received.shape
    unit = identity(LANES)
    half = message_lanes // 8
    groups = message_rows // 8
    entries = blocks.shape[0]
    for pair in range(groups // 2):
        wide = received[:, pair * 16 : (pair + 1) * 16, :].astype(jnp.float32)
        for side in range(2):
            group = pair * 2 + side
            own = wide[:, side * 8 : (side + 1) * 8, :].reshape(owners * 8, message_lanes).astype(jnp.bfloat16)
            turned = [
                mxu(unit, own[:, tile * LANES : (tile + 1) * LANES], NT).astype(jnp.bfloat16)
                for tile in range(message_lanes // LANES)
            ]
            turned = jnp.concatenate(turned, axis=0)
            for e in range(8):
                entry = group * 8 + e
                made = mxu(turned[e * half : (e + 1) * half], zonal[column_of[entry]], NN)
                blocks[entry] = made.astype(jnp.bfloat16)
                for field in range(3):
                    lowest_scratch[field * entries + entry : field * entries + entry + 1, :] = made[
                        field * 16 : field * 16 + 1, :
                    ]
    lowest[...] = lowest_scratch[...].astype(jnp.bfloat16)


def arrive_kernel(stencil, at_top, blocks, above, hweight, vweight, arrival, made, wide, over_rows, out_sem):
    entries = blocks.shape[0]
    rows, fields, levels, _ = made.shape
    top = at_top[0] == 1
    over_rows[...] = above[...].astype(jnp.float32)

    def widen(entry, carry):
        block = blocks[entry].astype(jnp.float32)
        wide[entry, 0 : fields * levels, :] = block
        for field in range(fields):
            own_last = block[(field + 1) * levels - 1 : (field + 1) * levels, :]
            over = over_rows[pl.ds(field * entries + entry, 1), :]
            wide[entry, pl.ds(fields * levels + field, 1), :] = jnp.where(top, own_last, over)
        return carry

    lax.fori_loop(0, entries, widen, 0, unroll=4)

    level = lax.broadcasted_iota(jnp.int32, (levels, LANES), 0)
    together = 8
    piece = 32
    pieces = rows // piece

    def send(i):
        at = pl.multiple_of(i * piece, piece)
        return pltpu.make_async_copy(made.at[pl.ds(at, piece)], arrival.at[pl.ds(at, piece)], out_sem.at[i])

    def some_rows(i, carry):
        first = i * together
        tile = pl.multiple_of((first // LANES) * LANES, LANES)
        uppers = pltpu.roll(vweight[:, pl.ds(tile, LANES)], (LANES - first % LANES) % LANES, 1)
        for k in range(together):
            a = first + k
            total = None
            for q in range(4):
                term = hweight[a, q : q + 1, :] * wide[stencil[q, a]]
                total = term if total is None else total + term
            upper = jnp.broadcast_to(uppers[:, k : k + 1], (levels, LANES))
            lower = 1.0 - upper
            for field in range(fields):
                here = total[field * levels : (field + 1) * levels]
                over = jnp.where(
                    level == levels - 1,
                    total[fields * levels + field : fields * levels + field + 1],
                    pltpu.roll(here, levels - 1, 0),
                )
                made[a, field] = (lower * here + upper * over).astype(jnp.bfloat16)

        @pl.when(i % (piece // together) == piece // together - 1)
        def _():
            send(i // (piece // together)).start()

        return carry

    lax.fori_loop(0, rows // together, some_rows, 0)
    for i in range(pieces):
        send(i).wait()


def whole(memory):
    return pl.BlockSpec(memory_space=memory)


def per_device(fourier, gauss, legendre, owner, send_list, stencil, hweight, vweight):
    lat_count = lax.axis_size("lat")
    device_row = lax.axis_index("lat")
    lat_dev, fields, levels, columns = fourier.shape
    wave_total = columns // 2
    slot_most = legendre.shape[1]
    degrees = legendre.shape[3]
    latitudes = legendre.shape[2]
    slot_count = lat_count * slot_most
    capacity = send_list.shape[2]
    arrivals = stencil.shape[0]
    half = fields * levels
    per_slot = 2 * half
    message_lanes = slot_most * per_slot
    tiles = message_lanes // LANES
    entries = lat_count * capacity

    owners = owner[:, 0]
    wave_index = jnp.arange(wave_total, dtype=jnp.int32)
    earlier = (owners[:, None] == owners[None, :]) & (wave_index[:, None] < wave_index[None, :])
    slot_rank = jnp.sum(earlier.astype(jnp.int32), axis=0)
    slot_of = owners * slot_most + slot_rank
    wave_number = wave_index * (degrees // wave_total)
    vmem = whole(pltpu.VMEM)
    smem = whole(pltpu.SMEM)
    hbm = whole(pl.ANY)
    message_one = pl.pallas_call(
        pack_kernel,
        out_shape=jax.ShapeDtypeStruct((lat_count, tiles * lat_dev + 8, LANES), jnp.bfloat16),
        in_specs=[hbm, hbm, hbm, hbm],
        out_specs=hbm,
        scratch_shapes=[
            pltpu.VMEM((1, wave_total), jnp.int32),
            pltpu.VMEM((capacity, lat_count), jnp.int32),
            pltpu.VMEM((1, lat_dev), jnp.float32),
            pltpu.VMEM(fourier.shape, jnp.bfloat16),
            pltpu.VMEM((lat_count, tiles * lat_dev + 8, LANES), jnp.bfloat16),
            pltpu.VMEM((tiles, lat_count * lat_dev, LANES), jnp.float32),
            pltpu.VMEM((lat_dev, columns), jnp.float32),
            pltpu.SemaphoreType.DMA((lat_dev // 8 + 3,)),
            pltpu.SemaphoreType.DMA((lat_count // 8,)),
        ],
        compiler_params=pltpu.CompilerParams(vmem_limit_bytes=GRANT),
        name="pack",
    )(owner.reshape(1, wave_total), send_list[0].T, gauss.reshape(1, lat_dev), fourier)
    arrived = lax.all_to_all(message_one, "lat", split_axis=0, concat_axis=0, tiled=True)

    placed = (slot_of[:, None] == jnp.arange(slot_count, dtype=jnp.int32)[None, :]).astype(jnp.int32)
    owned = lax.dynamic_slice_in_dim(placed, device_row * slot_most, slot_most, 1)
    filled = jnp.sum(owned, axis=0) > 0
    slot_wave = jnp.sum(owned * wave_number[:, None], axis=0)
    degree_index = jnp.arange(degrees, dtype=jnp.int32)
    keep_mask = (filled[:, None] & (degree_index[None, :] >= slot_wave[:, None])).astype(jnp.float32)
    damping = keep_mask * damping_curve(degrees)[None, :]

    message_shape = (lat_count, entries // 8 * slot_most * 2, 8 * half)
    spectral_rows, message_two = pl.pallas_call(
        spectral_kernel,
        in_specs=[vmem, hbm, vmem],
        out_specs=[vmem, hbm],
        scratch_shapes=[
            pltpu.VMEM((slot_most, latitudes, degrees), jnp.bfloat16),
            pltpu.VMEM(message_shape, jnp.bfloat16),
            pltpu.VMEM((message_lanes, latitudes), jnp.bfloat16),
            pltpu.VMEM((latitudes * 2 * slot_most, LANES), jnp.float32),
            pltpu.VMEM((lat_count, LANES), jnp.int32),
            pltpu.SMEM((lat_count, LANES), jnp.int32),
            pltpu.SemaphoreType.DMA,
            pltpu.SemaphoreType.DMA((slot_most,)),
            pltpu.SemaphoreType.DMA((lat_count // 4,)),
        ],
        out_shape=[
            jax.ShapeDtypeStruct((slot_most, per_slot, degrees), jnp.bfloat16),
            jax.ShapeDtypeStruct(message_shape, jnp.bfloat16),
        ],
        compiler_params=pltpu.CompilerParams(vmem_limit_bytes=GRANT),
        name="spectral",
    )(arrived, legendre[0], damping)
    received = lax.all_to_all(message_two, "lat", split_axis=0, concat_axis=0, tiled=True)

    spectral = jnp.transpose(
        spectral_rows.reshape(slot_most, fields, 2, levels, degrees), (0, 1, 3, 2, 4)
    )
    slot_waves = jnp.sum(placed * wave_number[:, None], axis=0)
    present = (jnp.sum(placed, axis=0) > 0).astype(jnp.float32)
    points = jnp.arange(NLON, dtype=jnp.int32).reshape(BLOCKS_X, 1, 1, BLK)
    phases = slot_waves[None, :, None, None] * points % NLON
    angles = phases.astype(jnp.float32) * (2.0 * math.pi / NLON)
    norm_factor = present[None, :, None, None] / math.sqrt(wave_total)
    zonal = jnp.concatenate([jnp.cos(angles) * norm_factor, -jnp.sin(angles) * norm_factor], axis=2)
    zonal = zonal.astype(jnp.bfloat16).reshape(BLOCKS_X, slot_count * 2, BLK)
    all_columns = arrived[:, tiles * lat_dev, entries:].reshape(lat_count, capacity, lat_count)
    column_of = lax.dynamic_index_in_dim(all_columns, device_row, 2, keepdims=False)
    column_of = column_of.astype(jnp.int32).reshape(-1)
    lev_count = lax.axis_size("lev")
    at_top = (lax.axis_index("lev") == lev_count - 1).astype(jnp.int32).reshape(1)
    vertical = vweight.T
    corners = stencil.T
    received, vertical, corners, at_top = lax.optimization_barrier((received, vertical, corners, at_top))
    blocks, lowest = pl.pallas_call(
        block_kernel,
        out_shape=[
            jax.ShapeDtypeStruct((entries, half, BLK), jnp.bfloat16),
            jax.ShapeDtypeStruct((fields * entries, BLK), jnp.bfloat16),
        ],
        in_specs=[smem, vmem, vmem],
        out_specs=[vmem, vmem],
        scratch_shapes=[pltpu.VMEM((fields * entries, BLK), jnp.float32)],
        compiler_params=pltpu.CompilerParams(vmem_limit_bytes=16 * 2**20),
        name="blocks",
    )(column_of, received, zonal)

    above = lax.ppermute(lowest, "lev", [(i, i - 1) for i in range(1, lev_count)])
    arrival = pl.pallas_call(
        arrive_kernel,
        out_shape=jax.ShapeDtypeStruct((arrivals, fields, levels, BLK), jnp.bfloat16),
        in_specs=[smem, smem, vmem, vmem, vmem, vmem],
        out_specs=hbm,
        scratch_shapes=[
            pltpu.VMEM((arrivals, fields, levels, BLK), jnp.bfloat16),
            pltpu.VMEM((entries, half + 8, BLK), jnp.float32),
            pltpu.VMEM((fields * entries, BLK), jnp.float32),
            pltpu.SemaphoreType.DMA((arrivals // 32,)),
        ],
        compiler_params=pltpu.CompilerParams(vmem_limit_bytes=16 * 2**20),
        name="arrive",
    )(corners, at_top, blocks, above, hweight, vertical)
    return (spectral[None], arrival)


def solution(mesh):
    return jax.shard_map(
        per_device,
        mesh=mesh,
        in_specs=(
            P("lat", None, "lev", None),
            P("lat"),
            P("lat", None, None, None),
            P(),
            P("lat", None, None),
            P("lat", None),
            P("lat", None, None),
            P("lat", "lev"),
        ),
        out_specs=(P("lat", None, None, "lev", None, None), P("lat", None, "lev", None)),
        check_vma=False,
    )
```

```python
import math

import jax
import jax.numpy as jnp
from jax import lax
from jax.experimental import pallas as pl
from jax.experimental.pallas import tpu as pltpu
from jax.sharding import PartitionSpec as P

NLON = 2560
BLK = 128
BLOCKS_X = NLON // BLK
LANES = 128
GRANT = 56 * 2**20

diffusion = 3.0

NT = (((1,), (1,)), ((), ()))
NN = (((1,), (0,)), ((), ()))


def mxu(left, right, dims):
    return lax.dot_general(left, right, dims, preferred_element_type=jnp.float32)


def identity(size):
    rows = lax.broadcasted_iota(jnp.int32, (size, size), 0)
    columns = lax.broadcasted_iota(jnp.int32, (size, size), 1)
    return (rows == columns).astype(jnp.float32).astype(jnp.bfloat16)


def damping_curve(degrees):
    order_n = jnp.arange(degrees, dtype=jnp.float32)
    ratio = order_n * (order_n + 1.0) / float(degrees * (degrees - 1))
    return 1.0 / (1.0 + diffusion * ratio * ratio)


def pack_kernel(
    owner_in, ids_in, gauss_in, fourier_in, message, owner, send_ids, gauss, fourier, packed, scratch, weight, in_sem, out_sem
):
    lat_dev, fields, levels, columns = fourier.shape
    owners = packed.shape[0]
    tiles = scratch.shape[0]
    slots = (tiles * LANES) // (2 * fields * levels)
    chunk = 8
    pieces = lat_dev // chunk
    small = [
        pltpu.make_async_copy(source, target, in_sem.at[pieces + i])
        for i, (source, target) in enumerate(((owner_in, owner), (ids_in, send_ids), (gauss_in, gauss)))
    ]
    large = [
        pltpu.make_async_copy(
            fourier_in.at[pl.ds(i * chunk, chunk)], fourier.at[pl.ds(i * chunk, chunk)], in_sem.at[i]
        )
        for i in range(pieces)
    ]
    for copy in small + large:
        copy.start()
    for copy in small:
        copy.wait()

    waves = owner.shape[1]
    wave_at = lax.broadcasted_iota(jnp.int32, (waves, columns), 0)
    column = lax.broadcasted_iota(jnp.int32, (waves, columns), 1)
    square_row = lax.broadcasted_iota(jnp.int32, (waves, waves), 0)
    square_column = lax.broadcasted_iota(jnp.int32, (waves, waves), 1)
    listed = jnp.broadcast_to(owner[...], (waves, waves))
    upright = jnp.sum(jnp.where(square_row == square_column, listed, 0), axis=1, keepdims=True)
    upright = jnp.broadcast_to(upright, (waves, columns))
    column_owner = jnp.sum(jnp.where(wave_at == column // 2, upright, 0), axis=0, keepdims=True)
    earlier = (upright == jnp.broadcast_to(column_owner, (waves, columns))) & (wave_at < column // 2)
    column_rank = jnp.sum(jnp.where(earlier, 1, 0), axis=0, keepdims=True)
    owner_at = lax.broadcasted_iota(jnp.int32, (owners, columns), 0)
    chooser = jnp.where(owner_at == column_owner, 1.0, 0.0).astype(jnp.bfloat16)
    part_of = 2 * column_rank + lax.broadcasted_iota(jnp.int32, (1, columns), 1) % 2
    masks = [
        jnp.broadcast_to(jnp.where(part_of == i, 1.0, 0.0), (levels, columns)).astype(jnp.bfloat16)
        for i in range(2 * slots)
    ]
    turn_row = lax.broadcasted_iota(jnp.int32, (lat_dev, lat_dev), 0)
    turn_column = lax.broadcasted_iota(jnp.int32, (lat_dev, lat_dev), 1)
    weights = jnp.where(turn_row == turn_column, jnp.broadcast_to(gauss[...], (lat_dev, lat_dev)), 0.0)
    weight[...] = jnp.broadcast_to(jnp.sum(weights, axis=1, keepdims=True), weight.shape)

    for t in range(lat_dev):
        if t % chunk == 0:
            large[t // chunk].wait()
        rows = fourier[t].reshape(fields * levels, columns).astype(jnp.float32)
        rows = (rows * weight[t : t + 1, :]).astype(jnp.bfloat16)
        parts = []
        for slot in range(slots):
            for field in range(fields):
                for part in range(2):
                    parts.append(rows[field * levels : (field + 1) * levels] * masks[2 * slot + part])
        spread = jnp.concatenate(parts, axis=0)
        chosen = mxu(chooser, spread, NT)
        for tile in range(tiles):
            scratch[tile, pl.ds(t, owners, stride=lat_dev), :] = chosen[:, tile * LANES : (tile + 1) * LANES]

    ids = send_ids[...].astype(jnp.float32)
    in_row = jnp.floor((ids + 0.5) * (1.0 / BLOCKS_X))
    in_column = ids - in_row * BLOCKS_X
    sides = [in_row[k : k + 1] for k in range(ids.shape[0])] + [in_column[k : k + 1] for k in range(ids.shape[0])]
    extra = jnp.broadcast_to(jnp.concatenate(sides, axis=1), (8, LANES))
    group = 8
    copies = []
    for o in range(owners):
        parts = [scratch[tile, o * lat_dev : (o + 1) * lat_dev, :] for tile in range(tiles)]
        packed[o] = jnp.concatenate(parts + [extra], axis=0).astype(jnp.bfloat16)
        if o % group == group - 1:
            first = o + 1 - group
            copies.append(
                pltpu.make_async_copy(
                    packed.at[pl.ds(first, group)], message.at[pl.ds(first, group)], out_sem.at[o // group]
                )
            )
            copies[-1].start()
    for copy in copies:
        copy.wait()


def fetch_kernel(tables_in, tables, sem):
    copies = [pltpu.make_async_copy(tables_in.at[i], tables.at[i], sem.at[i]) for i in range(tables.shape[0])]
    for copy in copies:
        copy.start()
    for copy in copies:
        copy.wait()


def spectral_kernel(
    arrived, tables, damping, spectral, message, made, turned, rows_at, listed, row_of, listed_sem, out_sem
):
    slots, per_slot, degrees = spectral.shape
    half = per_slot // 2
    field_rows = half // 3
    bands = arrived.shape[0]
    tiles = turned.shape[0] // LANES
    lat_dev = (arrived.shape[1] - 8) // tiles
    latitudes = bands * lat_dev
    receivers, message_rows, message_lanes = message.shape
    lists = pltpu.make_async_copy(listed, row_of, listed_sem)

    wide = arrived[...].astype(jnp.float32)
    band = lax.broadcasted_iota(jnp.int32, (bands, LANES), 0)
    listed[...] = (wide[:, tiles * lat_dev, :].astype(jnp.int32) + band * lat_dev) * 8
    lists.start()
    unit = identity(LANES)
    for tile in range(tiles):
        columns = wide[:, tile * lat_dev : (tile + 1) * lat_dev, :].reshape(latitudes, LANES)
        turned[tile * LANES : (tile + 1) * LANES, :] = mxu(unit, columns.astype(jnp.bfloat16), NT).astype(jnp.bfloat16)

    gap = jnp.zeros((LANES - half, degrees), jnp.bfloat16)
    chunk = 256
    for slot in range(slots):
        own = turned[slot * per_slot : (slot + 1) * per_slot, :]
        spectra = mxu(own, tables[slot], NN)
        damped = (spectra * damping[slot : slot + 1, :]).astype(jnp.bfloat16)
        spectral[slot] = damped
        sides = []
        for part in range(2):
            for field in range(3):
                at = (2 * field + part) * field_rows
                sides.append(damped[at : at + field_rows])
            sides.append(gap)
        sides = jnp.concatenate(sides, axis=0)
        for at in range(0, latitudes, chunk):
            back = mxu(tables[slot, at : at + chunk, :], sides, NT)
            for part in range(2):
                rows_at[pl.ds(at * 2 * slots + slot * 2 + part, chunk, stride=2 * slots), :] = back[
                    :, part * LANES : (part + 1) * LANES
                ]

    lists.wait()
    lane = lax.broadcasted_iota(jnp.int32, (8, LANES), 1)
    wide_tiles = message_lanes // LANES

    group = 4
    groups = receivers // group

    def send(g):
        at = pl.multiple_of(g * group, group)
        return pltpu.make_async_copy(made.at[pl.ds(at, group)], message.at[pl.ds(at, group)], out_sem.at[g])

    def one_group(g, carry):
        for k in range(group):
            r = g * group + k
            for pair in range(message_rows // 16):
                halves = []
                for side in range(2):
                    built = [None] * wide_tiles
                    for e in range(8):
                        entry = (pair * 2 + side) * 8 + e
                        at = pl.multiple_of(row_of[entry // 2, receivers * (entry % 2) + r], 8)
                        row = rows_at[pl.ds(at, 8), :]
                        start = e * half
                        if start % LANES:
                            row = pltpu.roll(row, start % LANES, 1)
                        for tile in range(start // LANES, (start + half - 1) // LANES + 1):
                            first = start - tile * LANES
                            if built[tile] is None:
                                built[tile] = row
                            else:
                                built[tile] = jnp.where(lane >= first, row, built[tile])
                    halves.append(jnp.concatenate(built, axis=1))
                both = jnp.concatenate(halves, axis=0).astype(jnp.bfloat16)
                made[r, pair * 16 : (pair + 1) * 16, :] = both
        send(g).start()
        return carry

    lax.fori_loop(0, groups, one_group, 0)
    for g in range(groups):
        send(g).wait()


def block_kernel(column_of, received, zonal, blocks, lowest, highest, lowest_scratch, highest_scratch):
    owners, message_rows, message_lanes = received.shape
    unit = identity(LANES)
    half = message_lanes // 8
    groups = message_rows // 8
    entries = blocks.shape[0]
    for pair in range(groups // 2):
        wide = received[:, pair * 16 : (pair + 1) * 16, :].astype(jnp.float32)
        for side in range(2):
            group = pair * 2 + side
            own = wide[:, side * 8 : (side + 1) * 8, :].reshape(owners * 8, message_lanes).astype(jnp.bfloat16)
            turned = [
                mxu(unit, own[:, tile * LANES : (tile + 1) * LANES], NT).astype(jnp.bfloat16)
                for tile in range(message_lanes // LANES)
            ]
            turned = jnp.concatenate(turned, axis=0)
            for e in range(8):
                entry = group * 8 + e
                made = mxu(turned[e * half : (e + 1) * half], zonal[column_of[entry]], NN)
                blocks[entry] = made.astype(jnp.bfloat16)
                for field in range(3):
                    lowest_scratch[field * entries + entry : field * entries + entry + 1, :] = made[
                        field * 16 : field * 16 + 1, :
                    ]
                    highest_scratch[field * entries + entry : field * entries + entry + 1, :] = made[
                        field * 16 + 15 : field * 16 + 16, :
                    ]
    lowest[...] = lowest_scratch[...].astype(jnp.bfloat16)
    highest[...] = highest_scratch[...].astype(jnp.bfloat16)


def horizontal_kernel(stencil, blocks, hweight, horizontal, wide):
    entries = blocks.shape[0]
    rows = horizontal.shape[0]
    together = 8

    def widen(i, carry):
        for k in range(together):
            wide[i * together + k] = blocks[i * together + k].astype(jnp.float32)
        return carry

    lax.fori_loop(0, entries // together, widen, 0)

    def some_rows(i, carry):
        for k in range(together):
            a = i * together + k
            total = None
            for q in range(4):
                term = hweight[a, q : q + 1, :] * wide[stencil[q, a]]
                total = term if total is None else total + term
            horizontal[a] = total
        return carry

    lax.fori_loop(0, rows // together, some_rows, 0)


def vertical_kernel(stencil, at_top, horizontal, highest, above, hweight, vweight, arrival, made, over_rows, wide, out_sem):
    rows, fields, levels, _ = made.shape
    entries = wide.shape[0]
    top = at_top[0] == 1
    over_rows[...] = jnp.where(top, highest[...].astype(jnp.float32), above[...].astype(jnp.float32))
    together = 8

    def widen(i, carry):
        for k in range(together):
            entry = i * together + k
            for field in range(fields):
                wide[entry, field : field + 1, :] = over_rows[pl.ds(field * entries + entry, 1), :]
        return carry

    lax.fori_loop(0, entries // together, widen, 0)

    level = lax.broadcasted_iota(jnp.int32, (levels, LANES), 0)
    piece = 32
    pieces = rows // piece

    def send(i):
        at = pl.multiple_of(i * piece, piece)
        return pltpu.make_async_copy(made.at[pl.ds(at, piece)], arrival.at[pl.ds(at, piece)], out_sem.at[i])

    def some_rows(i, carry):
        first = i * piece
        tile = pl.multiple_of((first // LANES) * LANES, LANES)
        uppers = pltpu.roll(vweight[:, pl.ds(tile, LANES)], (LANES - first % LANES) % LANES, 1)
        for k in range(piece):
            a = first + k
            last = None
            for q in range(4):
                term = hweight[a, q : q + 1, :] * wide[stencil[q, a]]
                last = term if last is None else last + term
            upper = jnp.broadcast_to(uppers[:, k : k + 1], (levels, LANES))
            lower = 1.0 - upper
            for field in range(fields):
                here = horizontal[a, field * levels : (field + 1) * levels, :]
                over = jnp.where(level == levels - 1, last[field : field + 1], pltpu.roll(here, levels - 1, 0))
                made[a, field] = (lower * here + upper * over).astype(jnp.bfloat16)
        send(i).start()
        return carry

    lax.fori_loop(0, pieces, some_rows, 0)
    for i in range(pieces):
        send(i).wait()


def whole(memory):
    return pl.BlockSpec(memory_space=memory)


def per_device(fourier, gauss, legendre, owner, send_list, stencil, hweight, vweight):
    lat_count = lax.axis_size("lat")
    device_row = lax.axis_index("lat")
    lat_dev, fields, levels, columns = fourier.shape
    wave_total = columns // 2
    slot_most = legendre.shape[1]
    degrees = legendre.shape[3]
    latitudes = legendre.shape[2]
    slot_count = lat_count * slot_most
    capacity = send_list.shape[2]
    arrivals = stencil.shape[0]
    half = fields * levels
    per_slot = 2 * half
    message_lanes = slot_most * per_slot
    tiles = message_lanes // LANES
    entries = lat_count * capacity

    owners = owner[:, 0]
    wave_index = jnp.arange(wave_total, dtype=jnp.int32)
    earlier = (owners[:, None] == owners[None, :]) & (wave_index[:, None] < wave_index[None, :])
    slot_rank = jnp.sum(earlier.astype(jnp.int32), axis=0)
    slot_of = owners * slot_most + slot_rank
    wave_number = wave_index * (degrees // wave_total)
    vmem = whole(pltpu.VMEM)
    smem = whole(pltpu.SMEM)
    hbm = whole(pl.ANY)
    message_one = pl.pallas_call(
        pack_kernel,
        out_shape=jax.ShapeDtypeStruct((lat_count, tiles * lat_dev + 8, LANES), jnp.bfloat16),
        in_specs=[hbm, hbm, hbm, hbm],
        out_specs=hbm,
        scratch_shapes=[
            pltpu.VMEM((1, wave_total), jnp.int32),
            pltpu.VMEM((capacity, lat_count), jnp.int32),
            pltpu.VMEM((1, lat_dev), jnp.float32),
            pltpu.VMEM(fourier.shape, jnp.bfloat16),
            pltpu.VMEM((lat_count, tiles * lat_dev + 8, LANES), jnp.bfloat16),
            pltpu.VMEM((tiles, lat_count * lat_dev, LANES), jnp.float32),
            pltpu.VMEM((lat_dev, columns), jnp.float32),
            pltpu.SemaphoreType.DMA((lat_dev // 8 + 3,)),
            pltpu.SemaphoreType.DMA((lat_count // 8,)),
        ],
        compiler_params=pltpu.CompilerParams(vmem_limit_bytes=GRANT),
        name="pack",
    )(owner.reshape(1, wave_total), send_list[0].T, gauss.reshape(1, lat_dev), fourier)
    arrived = lax.all_to_all(message_one, "lat", split_axis=0, concat_axis=0, tiled=True)

    placed = (slot_of[:, None] == jnp.arange(slot_count, dtype=jnp.int32)[None, :]).astype(jnp.int32)
    owned = lax.dynamic_slice_in_dim(placed, device_row * slot_most, slot_most, 1)
    filled = jnp.sum(owned, axis=0) > 0
    slot_wave = jnp.sum(owned * wave_number[:, None], axis=0)
    degree_index = jnp.arange(degrees, dtype=jnp.int32)
    keep_mask = (filled[:, None] & (degree_index[None, :] >= slot_wave[:, None])).astype(jnp.float32)
    damping = keep_mask * damping_curve(degrees)[None, :]

    message_shape = (lat_count, entries // 8 * slot_most * 2, 8 * half)
    tables = pl.pallas_call(
        fetch_kernel,
        out_shape=jax.ShapeDtypeStruct(legendre.shape[1:], legendre.dtype),
        in_specs=[hbm],
        out_specs=vmem,
        scratch_shapes=[pltpu.SemaphoreType.DMA((slot_most,))],
        compiler_params=pltpu.CompilerParams(vmem_limit_bytes=16 * 2**20),
        cost_estimate=pl.CostEstimate(flops=0, bytes_accessed=2 * legendre.size * 2, transcendentals=0),
        name="fetch",
    )(legendre[0])
    spectral_rows, message_two = pl.pallas_call(
        spectral_kernel,
        in_specs=[vmem, vmem, vmem],
        out_specs=[vmem, hbm],
        scratch_shapes=[
            pltpu.VMEM(message_shape, jnp.bfloat16),
            pltpu.VMEM((message_lanes, latitudes), jnp.bfloat16),
            pltpu.VMEM((latitudes * 2 * slot_most, LANES), jnp.float32),
            pltpu.VMEM((lat_count, LANES), jnp.int32),
            pltpu.SMEM((lat_count, LANES), jnp.int32),
            pltpu.SemaphoreType.DMA,
            pltpu.SemaphoreType.DMA((lat_count // 4,)),
        ],
        out_shape=[
            jax.ShapeDtypeStruct((slot_most, per_slot, degrees), jnp.bfloat16),
            jax.ShapeDtypeStruct(message_shape, jnp.bfloat16),
        ],
        compiler_params=pltpu.CompilerParams(vmem_limit_bytes=24 * 2**20),
        name="spectral",
    )(arrived, tables, damping)
    received = lax.all_to_all(message_two, "lat", split_axis=0, concat_axis=0, tiled=True)

    spectral = jnp.transpose(
        spectral_rows.reshape(slot_most, fields, 2, levels, degrees), (0, 1, 3, 2, 4)
    )
    slot_waves = jnp.sum(placed * wave_number[:, None], axis=0)
    present = (jnp.sum(placed, axis=0) > 0).astype(jnp.float32)
    points = jnp.arange(NLON, dtype=jnp.int32).reshape(BLOCKS_X, 1, 1, BLK)
    phases = slot_waves[None, :, None, None] * points % NLON
    angles = phases.astype(jnp.float32) * (2.0 * math.pi / NLON)
    norm_factor = present[None, :, None, None] / math.sqrt(wave_total)
    zonal = jnp.concatenate([jnp.cos(angles) * norm_factor, -jnp.sin(angles) * norm_factor], axis=2)
    zonal = zonal.astype(jnp.bfloat16).reshape(BLOCKS_X, slot_count * 2, BLK)
    all_columns = arrived[:, tiles * lat_dev, entries:].reshape(lat_count, capacity, lat_count)
    column_of = lax.dynamic_index_in_dim(all_columns, device_row, 2, keepdims=False)
    column_of = column_of.astype(jnp.int32).reshape(-1)
    lev_count = lax.axis_size("lev")
    at_top = (lax.axis_index("lev") == lev_count - 1).astype(jnp.int32).reshape(1)
    vertical = vweight.T
    corners = stencil.T
    received, vertical, corners, at_top = lax.optimization_barrier((received, vertical, corners, at_top))
    blocks, lowest, highest = pl.pallas_call(
        block_kernel,
        out_shape=[
            jax.ShapeDtypeStruct((entries, half, BLK), jnp.bfloat16),
            jax.ShapeDtypeStruct((fields * entries, BLK), jnp.bfloat16),
            jax.ShapeDtypeStruct((fields * entries, BLK), jnp.bfloat16),
        ],
        in_specs=[smem, vmem, vmem],
        out_specs=[vmem, vmem, vmem],
        scratch_shapes=[pltpu.VMEM((fields * entries, BLK), jnp.float32)] * 2,
        compiler_params=pltpu.CompilerParams(vmem_limit_bytes=16 * 2**20),
        name="blocks",
    )(column_of, received, zonal)

    above = lax.ppermute(lowest, "lev", [(i, i - 1) for i in range(1, lev_count)])
    horizontal = pl.pallas_call(
        horizontal_kernel,
        out_shape=jax.ShapeDtypeStruct((arrivals, half, BLK), jnp.float32),
        in_specs=[smem, vmem, vmem],
        out_specs=vmem,
        scratch_shapes=[pltpu.VMEM((entries, half, BLK), jnp.float32)],
        compiler_params=pltpu.CompilerParams(vmem_limit_bytes=16 * 2**20),
        cost_estimate=pl.CostEstimate(
            flops=8 * arrivals * half * BLK, bytes_accessed=4 * arrivals * half * BLK, transcendentals=0
        ),
        name="horizontal",
    )(corners, blocks, hweight)
    arrival = pl.pallas_call(
        vertical_kernel,
        out_shape=jax.ShapeDtypeStruct((arrivals, fields, levels, BLK), jnp.bfloat16),
        in_specs=[smem, smem, vmem, vmem, vmem, vmem, vmem],
        out_specs=hbm,
        scratch_shapes=[
            pltpu.VMEM((arrivals, fields, levels, BLK), jnp.bfloat16),
            pltpu.VMEM((fields * entries, BLK), jnp.float32),
            pltpu.VMEM((entries, 8, BLK), jnp.float32),
            pltpu.SemaphoreType.DMA((arrivals // 32,)),
        ],
        compiler_params=pltpu.CompilerParams(vmem_limit_bytes=16 * 2**20),
        name="vertical",
    )(corners, at_top, horizontal, highest, above, hweight, vertical)
    return (spectral[None], arrival)


def solution(mesh):
    return jax.shard_map(
        per_device,
        mesh=mesh,
        in_specs=(
            P("lat", None, "lev", None),
            P("lat"),
            P("lat", None, None, None),
            P(),
            P("lat", None, None),
            P("lat", None),
            P("lat", None, None),
            P("lat", "lev"),
        ),
        out_specs=(P("lat", None, None, "lev", None, None), P("lat", None, "lev", None)),
        check_vma=False,
    )
```

```python
import math

import jax
import jax.numpy as jnp
from jax import lax
from jax.experimental import pallas as pl
from jax.experimental.pallas import tpu as pltpu
from jax.sharding import PartitionSpec as P

NLON = 2560
BLK = 128
BLOCKS_X = NLON // BLK
LANES = 128
GRANT = 56 * 2**20

diffusion = 3.0

NT = (((1,), (1,)), ((), ()))
NN = (((1,), (0,)), ((), ()))


def mxu(left, right, dims):
    return lax.dot_general(left, right, dims, preferred_element_type=jnp.float32)


def identity(size):
    rows = lax.broadcasted_iota(jnp.int32, (size, size), 0)
    columns = lax.broadcasted_iota(jnp.int32, (size, size), 1)
    return (rows == columns).astype(jnp.float32).astype(jnp.bfloat16)


def damping_curve(degrees):
    order_n = jnp.arange(degrees, dtype=jnp.float32)
    ratio = order_n * (order_n + 1.0) / float(degrees * (degrees - 1))
    return 1.0 / (1.0 + diffusion * ratio * ratio)


def pack_kernel(
    owner_in, ids_in, gauss_in, fourier_in, message, owner, send_ids, gauss, fourier, packed, scratch, weight, in_sem, out_sem
):
    lat_dev, fields, levels, columns = fourier.shape
    owners = packed.shape[0]
    tiles = scratch.shape[0]
    slots = (tiles * LANES) // (2 * fields * levels)
    chunk = 8
    pieces = lat_dev // chunk
    small = [
        pltpu.make_async_copy(source, target, in_sem.at[pieces + i])
        for i, (source, target) in enumerate(((owner_in, owner), (ids_in, send_ids), (gauss_in, gauss)))
    ]
    large = [
        pltpu.make_async_copy(
            fourier_in.at[pl.ds(i * chunk, chunk)], fourier.at[pl.ds(i * chunk, chunk)], in_sem.at[i]
        )
        for i in range(pieces)
    ]
    for copy in small + large:
        copy.start()
    for copy in small:
        copy.wait()

    waves = owner.shape[1]
    wave_at = lax.broadcasted_iota(jnp.int32, (waves, columns), 0)
    column = lax.broadcasted_iota(jnp.int32, (waves, columns), 1)
    square_row = lax.broadcasted_iota(jnp.int32, (waves, waves), 0)
    square_column = lax.broadcasted_iota(jnp.int32, (waves, waves), 1)
    listed = jnp.broadcast_to(owner[...], (waves, waves))
    upright = jnp.sum(jnp.where(square_row == square_column, listed, 0), axis=1, keepdims=True)
    upright = jnp.broadcast_to(upright, (waves, columns))
    column_owner = jnp.sum(jnp.where(wave_at == column // 2, upright, 0), axis=0, keepdims=True)
    earlier = (upright == jnp.broadcast_to(column_owner, (waves, columns))) & (wave_at < column // 2)
    column_rank = jnp.sum(jnp.where(earlier, 1, 0), axis=0, keepdims=True)
    owner_at = lax.broadcasted_iota(jnp.int32, (owners, columns), 0)
    chooser = jnp.where(owner_at == column_owner, 1.0, 0.0).astype(jnp.bfloat16)
    part_of = 2 * column_rank + lax.broadcasted_iota(jnp.int32, (1, columns), 1) % 2
    masks = [
        jnp.broadcast_to(jnp.where(part_of == i, 1.0, 0.0), (levels, columns)).astype(jnp.bfloat16)
        for i in range(2 * slots)
    ]
    turn_row = lax.broadcasted_iota(jnp.int32, (lat_dev, lat_dev), 0)
    turn_column = lax.broadcasted_iota(jnp.int32, (lat_dev, lat_dev), 1)
    weights = jnp.where(turn_row == turn_column, jnp.broadcast_to(gauss[...], (lat_dev, lat_dev)), 0.0)
    weight[...] = jnp.broadcast_to(jnp.sum(weights, axis=1, keepdims=True), weight.shape)

    for t in range(lat_dev):
        if t % chunk == 0:
            large[t // chunk].wait()
        rows = fourier[t].reshape(fields * levels, columns).astype(jnp.float32)
        rows = (rows * weight[t : t + 1, :]).astype(jnp.bfloat16)
        parts = []
        for slot in range(slots):
            for field in range(fields):
                for part in range(2):
                    parts.append(rows[field * levels : (field + 1) * levels] * masks[2 * slot + part])
        spread = jnp.concatenate(parts, axis=0)
        chosen = mxu(chooser, spread, NT)
        for tile in range(tiles):
            scratch[tile, pl.ds(t, owners, stride=lat_dev), :] = chosen[:, tile * LANES : (tile + 1) * LANES]

    ids = send_ids[...].astype(jnp.float32)
    in_row = jnp.floor((ids + 0.5) * (1.0 / BLOCKS_X))
    in_column = ids - in_row * BLOCKS_X
    sides = [in_row[k : k + 1] for k in range(ids.shape[0])] + [in_column[k : k + 1] for k in range(ids.shape[0])]
    extra = jnp.broadcast_to(jnp.concatenate(sides, axis=1), (8, LANES))
    group = 8
    copies = []
    for o in range(owners):
        parts = [scratch[tile, o * lat_dev : (o + 1) * lat_dev, :] for tile in range(tiles)]
        packed[o] = jnp.concatenate(parts + [extra], axis=0).astype(jnp.bfloat16)
        if o % group == group - 1:
            first = o + 1 - group
            copies.append(
                pltpu.make_async_copy(
                    packed.at[pl.ds(first, group)], message.at[pl.ds(first, group)], out_sem.at[o // group]
                )
            )
            copies[-1].start()
    for copy in copies:
        copy.wait()


def spectral_kernel(
    arrived, tables_in, damping, spectral, message, tables, made, turned, rows_at, listed, row_of, listed_sem, in_sem, out_sem
):
    slots, per_slot, degrees = spectral.shape
    latitudes = tables.shape[1]

    def fetch(slot):
        return pltpu.make_async_copy(tables_in.at[slot], tables.at[slot], in_sem.at[slot])

    def fetch_one(slot, carry):
        fetch(slot).start()
        return carry

    lax.fori_loop(0, slots, fetch_one, 0)
    half = per_slot // 2
    field_rows = half // 3
    bands = arrived.shape[0]
    tiles = turned.shape[0] // LANES
    lat_dev = (arrived.shape[1] - 8) // tiles
    receivers, message_rows, message_lanes = message.shape
    lists = pltpu.make_async_copy(listed, row_of, listed_sem)

    wide = arrived[...].astype(jnp.float32)
    band = lax.broadcasted_iota(jnp.int32, (bands, LANES), 0)
    listed[...] = (wide[:, tiles * lat_dev, :].astype(jnp.int32) + band * lat_dev) * 8
    lists.start()
    unit = identity(LANES)
    for tile in range(tiles):
        columns = wide[:, tile * lat_dev : (tile + 1) * lat_dev, :].reshape(latitudes, LANES)
        turned[tile * LANES : (tile + 1) * LANES, :] = mxu(unit, columns.astype(jnp.bfloat16), NT).astype(jnp.bfloat16)

    gap = jnp.zeros((LANES - half, degrees), jnp.bfloat16)
    chunk = 256

    def one_slot(slot, carry):
        fetch(slot).wait()
        own = turned[pl.ds(pl.multiple_of(slot * per_slot, 32), per_slot), :]
        spectra = mxu(own, tables[slot], NN)
        damped = (spectra * damping[pl.ds(slot, 1), :]).astype(jnp.bfloat16)
        spectral[slot] = damped
        sides = []
        for part in range(2):
            for field in range(3):
                at = (2 * field + part) * field_rows
                sides.append(damped[at : at + field_rows])
            sides.append(gap)
        sides = jnp.concatenate(sides, axis=0)
        for at in range(0, latitudes, chunk):
            back = mxu(tables[slot, at : at + chunk, :], sides, NT)
            for part in range(2):
                rows_at[pl.ds(at * 2 * slots + slot * 2 + part, chunk, stride=2 * slots), :] = back[
                    :, part * LANES : (part + 1) * LANES
                ]
        return carry

    lax.fori_loop(0, slots, one_slot, 0)

    lists.wait()
    lane = lax.broadcasted_iota(jnp.int32, (8, LANES), 1)
    wide_tiles = message_lanes // LANES

    group = 4
    groups = receivers // group

    def send(g):
        at = pl.multiple_of(g * group, group)
        return pltpu.make_async_copy(made.at[pl.ds(at, group)], message.at[pl.ds(at, group)], out_sem.at[g])

    def one_group(g, carry):
        for k in range(group):
            r = g * group + k
            for pair in range(message_rows // 16):
                halves = []
                for side in range(2):
                    built = [None] * wide_tiles
                    for e in range(8):
                        entry = (pair * 2 + side) * 8 + e
                        at = pl.multiple_of(row_of[entry // 2, receivers * (entry % 2) + r], 8)
                        row = rows_at[pl.ds(at, 8), :]
                        start = e * half
                        if start % LANES:
                            row = pltpu.roll(row, start % LANES, 1)
                        for tile in range(start // LANES, (start + half - 1) // LANES + 1):
                            first = start - tile * LANES
                            if built[tile] is None:
                                built[tile] = row
                            else:
                                built[tile] = jnp.where(lane >= first, row, built[tile])
                    halves.append(jnp.concatenate(built, axis=1))
                both = jnp.concatenate(halves, axis=0).astype(jnp.bfloat16)
                made[r, pair * 16 : (pair + 1) * 16, :] = both
        send(g).start()
        return carry

    lax.fori_loop(0, groups, one_group, 0)
    for g in range(groups):
        send(g).wait()


def block_kernel(
    column_of, received, zonal, vweight, blocks, lowest, highest, spread, lowest_scratch, highest_scratch
):
    owners, message_rows, message_lanes = received.shape
    unit = identity(LANES)
    half = message_lanes // 8
    groups = message_rows // 8
    entries = blocks.shape[0]
    rows, levels, _ = spread.shape
    per_entry = rows // entries
    for pair in range(groups // 2):
        wide = received[:, pair * 16 : (pair + 1) * 16, :].astype(jnp.float32)
        for side in range(2):
            group = pair * 2 + side
            own = wide[:, side * 8 : (side + 1) * 8, :].reshape(owners * 8, message_lanes).astype(jnp.bfloat16)
            turned = [
                mxu(unit, own[:, tile * LANES : (tile + 1) * LANES], NT).astype(jnp.bfloat16)
                for tile in range(message_lanes // LANES)
            ]
            turned = jnp.concatenate(turned, axis=0)
            for e in range(8):
                entry = group * 8 + e
                made = mxu(turned[e * half : (e + 1) * half], zonal[column_of[entry]], NN)
                blocks[entry] = made.astype(jnp.bfloat16)
                for a in range(entry * per_entry, (entry + 1) * per_entry):
                    spread[a] = jnp.broadcast_to(vweight[:, a : a + 1], (levels, LANES))
                for field in range(3):
                    lowest_scratch[field * entries + entry : field * entries + entry + 1, :] = made[
                        field * 16 : field * 16 + 1, :
                    ]
                    highest_scratch[field * entries + entry : field * entries + entry + 1, :] = made[
                        field * 16 + 15 : field * 16 + 16, :
                    ]
    lowest[...] = lowest_scratch[...].astype(jnp.bfloat16)
    highest[...] = highest_scratch[...].astype(jnp.bfloat16)


def horizontal_kernel(stencil, blocks, hweight, horizontal, wide):
    entries = blocks.shape[0]
    rows = horizontal.shape[0]
    together = 8

    def widen(i, carry):
        for k in range(together):
            wide[i * together + k] = blocks[i * together + k].astype(jnp.float32)
        return carry

    lax.fori_loop(0, entries // together, widen, 0)

    def some_rows(i, carry):
        for k in range(together):
            a = i * together + k
            total = None
            for q in range(4):
                term = hweight[a, q : q + 1, :] * wide[stencil[q, a]]
                total = term if total is None else total + term
            horizontal[a] = total
        return carry

    lax.fori_loop(0, rows // together, some_rows, 0)


def vertical_kernel(stencil, at_top, horizontal, highest, above, hweight, spread, arrival, made, over_rows, wide, out_sem):
    rows, fields, levels, _ = made.shape
    entries = wide.shape[0]
    top = at_top[0] == 1
    over_rows[...] = jnp.where(top, highest[...].astype(jnp.float32), above[...].astype(jnp.float32))
    together = 8

    def widen(i, carry):
        for k in range(together):
            entry = i * together + k
            for field in range(fields):
                wide[entry, 7 - field : 8 - field, :] = over_rows[pl.ds(field * entries + entry, 1), :]
        return carry

    lax.fori_loop(0, entries // together, widen, 0)

    row = lax.broadcasted_iota(jnp.int32, (8, LANES), 0)
    piece = 64
    pieces = rows // piece

    def send(i):
        at = pl.multiple_of(i * piece, piece)
        return pltpu.make_async_copy(made.at[pl.ds(at, piece)], arrival.at[pl.ds(at, piece)], out_sem.at[i])

    def some_rows(i, carry):
        for k in range(piece):
            a = i * piece + k
            last = None
            for q in range(4):
                term = hweight[a, q : q + 1, :] * wide[stencil[q, a]]
                last = term if last is None else last + term
            for field in range(fields):
                parts = []
                over = last if field == 0 else pltpu.roll(last, field, 0)
                for part in reversed(range(levels // 8)):
                    here = horizontal[a, field * levels + part * 8 : field * levels + (part + 1) * 8, :]
                    turned = pltpu.roll(here, 7, 0)
                    up = jnp.where(row == 7, over, turned)
                    parts.insert(0, here + spread[a, part * 8 : (part + 1) * 8, :] * (up - here))
                    over = turned
                made[a, field] = jnp.concatenate(parts, axis=0).astype(jnp.bfloat16)
        send(i).start()
        return carry

    lax.fori_loop(0, pieces, some_rows, 0)
    for i in range(pieces):
        send(i).wait()


def whole(memory):
    return pl.BlockSpec(memory_space=memory)


def per_device(fourier, gauss, legendre, owner, send_list, stencil, hweight, vweight):
    lat_count = lax.axis_size("lat")
    device_row = lax.axis_index("lat")
    lat_dev, fields, levels, columns = fourier.shape
    wave_total = columns // 2
    slot_most = legendre.shape[1]
    degrees = legendre.shape[3]
    latitudes = legendre.shape[2]
    slot_count = lat_count * slot_most
    capacity = send_list.shape[2]
    arrivals = stencil.shape[0]
    half = fields * levels
    per_slot = 2 * half
    message_lanes = slot_most * per_slot
    tiles = message_lanes // LANES
    entries = lat_count * capacity

    owners = owner[:, 0]
    wave_index = jnp.arange(wave_total, dtype=jnp.int32)
    earlier = (owners[:, None] == owners[None, :]) & (wave_index[:, None] < wave_index[None, :])
    slot_rank = jnp.sum(earlier.astype(jnp.int32), axis=0)
    slot_of = owners * slot_most + slot_rank
    wave_number = wave_index * (degrees // wave_total)
    vmem = whole(pltpu.VMEM)
    smem = whole(pltpu.SMEM)
    hbm = whole(pl.ANY)
    message_one = pl.pallas_call(
        pack_kernel,
        out_shape=jax.ShapeDtypeStruct((lat_count, tiles * lat_dev + 8, LANES), jnp.bfloat16),
        in_specs=[hbm, hbm, hbm, hbm],
        out_specs=hbm,
        scratch_shapes=[
            pltpu.VMEM((1, wave_total), jnp.int32),
            pltpu.VMEM((capacity, lat_count), jnp.int32),
            pltpu.VMEM((1, lat_dev), jnp.float32),
            pltpu.VMEM(fourier.shape, jnp.bfloat16),
            pltpu.VMEM((lat_count, tiles * lat_dev + 8, LANES), jnp.bfloat16),
            pltpu.VMEM((tiles, lat_count * lat_dev, LANES), jnp.float32),
            pltpu.VMEM((lat_dev, columns), jnp.float32),
            pltpu.SemaphoreType.DMA((lat_dev // 8 + 3,)),
            pltpu.SemaphoreType.DMA((lat_count // 8,)),
        ],
        compiler_params=pltpu.CompilerParams(vmem_limit_bytes=GRANT),
        name="pack",
    )(owner.reshape(1, wave_total), send_list[0].T, gauss.reshape(1, lat_dev), fourier)
    arrived = lax.all_to_all(message_one, "lat", split_axis=0, concat_axis=0, tiled=True)

    placed = (slot_of[:, None] == jnp.arange(slot_count, dtype=jnp.int32)[None, :]).astype(jnp.int32)
    owned = lax.dynamic_slice_in_dim(placed, device_row * slot_most, slot_most, 1)
    filled = jnp.sum(owned, axis=0) > 0
    slot_wave = jnp.sum(owned * wave_number[:, None], axis=0)
    degree_index = jnp.arange(degrees, dtype=jnp.int32)
    keep_mask = (filled[:, None] & (degree_index[None, :] >= slot_wave[:, None])).astype(jnp.float32)
    damping = keep_mask * damping_curve(degrees)[None, :]

    message_shape = (lat_count, entries // 8 * slot_most * 2, 8 * half)
    spectral_rows, message_two = pl.pallas_call(
        spectral_kernel,
        in_specs=[vmem, hbm, vmem],
        out_specs=[vmem, hbm],
        scratch_shapes=[
            pltpu.VMEM((slot_most, latitudes, degrees), jnp.bfloat16),
            pltpu.VMEM(message_shape, jnp.bfloat16),
            pltpu.VMEM((message_lanes, latitudes), jnp.bfloat16),
            pltpu.VMEM((latitudes * 2 * slot_most, LANES), jnp.float32),
            pltpu.VMEM((lat_count, LANES), jnp.int32),
            pltpu.SMEM((lat_count, LANES), jnp.int32),
            pltpu.SemaphoreType.DMA,
            pltpu.SemaphoreType.DMA((slot_most,)),
            pltpu.SemaphoreType.DMA((lat_count // 4,)),
        ],
        out_shape=[
            jax.ShapeDtypeStruct((slot_most, per_slot, degrees), jnp.bfloat16),
            jax.ShapeDtypeStruct(message_shape, jnp.bfloat16),
        ],
        compiler_params=pltpu.CompilerParams(vmem_limit_bytes=50 * 2**20),
        name="spectral",
    )(arrived, legendre[0], damping)
    received = lax.all_to_all(message_two, "lat", split_axis=0, concat_axis=0, tiled=True)

    spectral = jnp.transpose(
        spectral_rows.reshape(slot_most, fields, 2, levels, degrees), (0, 1, 3, 2, 4)
    )
    slot_waves = jnp.sum(placed * wave_number[:, None], axis=0)
    slot_waves, spectral = lax.optimization_barrier((slot_waves, spectral))
    present = (jnp.sum(placed, axis=0) > 0).astype(jnp.float32)
    points = jnp.arange(NLON, dtype=jnp.int32).reshape(BLOCKS_X, 1, 1, BLK)
    phases = slot_waves[None, :, None, None] * points % NLON
    angles = phases.astype(jnp.float32) * (2.0 * math.pi / NLON)
    norm_factor = present[None, :, None, None] / math.sqrt(wave_total)
    zonal = jnp.concatenate([jnp.cos(angles) * norm_factor, -jnp.sin(angles) * norm_factor], axis=2)
    zonal = zonal.astype(jnp.bfloat16).reshape(BLOCKS_X, slot_count * 2, BLK)
    all_columns = arrived[:, tiles * lat_dev, entries:].reshape(lat_count, capacity, lat_count)
    column_of = lax.dynamic_index_in_dim(all_columns, device_row, 2, keepdims=False)
    column_of = column_of.astype(jnp.int32).reshape(-1)
    lev_count = lax.axis_size("lev")
    at_top = (lax.axis_index("lev") == lev_count - 1).astype(jnp.int32).reshape(1)
    vertical = vweight.T
    corners = stencil.T
    received, vertical, corners, at_top = lax.optimization_barrier((received, vertical, corners, at_top))
    blocks, lowest, highest, spread = pl.pallas_call(
        block_kernel,
        out_shape=[
            jax.ShapeDtypeStruct((entries, half, BLK), jnp.bfloat16),
            jax.ShapeDtypeStruct((fields * entries, BLK), jnp.bfloat16),
            jax.ShapeDtypeStruct((fields * entries, BLK), jnp.bfloat16),
            jax.ShapeDtypeStruct((arrivals, levels, BLK), jnp.float32),
        ],
        in_specs=[smem, vmem, vmem, vmem],
        out_specs=[vmem, vmem, vmem, vmem],
        scratch_shapes=[pltpu.VMEM((fields * entries, BLK), jnp.float32)] * 2,
        compiler_params=pltpu.CompilerParams(vmem_limit_bytes=16 * 2**20),
        name="blocks",
    )(column_of, received, zonal, vertical)

    above = lax.ppermute(lowest, "lev", [(i, i - 1) for i in range(1, lev_count)])
    horizontal = pl.pallas_call(
        horizontal_kernel,
        out_shape=jax.ShapeDtypeStruct((arrivals, half, BLK), jnp.float32),
        in_specs=[smem, vmem, vmem],
        out_specs=vmem,
        scratch_shapes=[pltpu.VMEM((entries, half, BLK), jnp.float32)],
        compiler_params=pltpu.CompilerParams(vmem_limit_bytes=16 * 2**20),
        cost_estimate=pl.CostEstimate(
            flops=8 * arrivals * half * BLK, bytes_accessed=4 * arrivals * half * BLK, transcendentals=0
        ),
        name="horizontal",
    )(corners, blocks, hweight)
    arrival = pl.pallas_call(
        vertical_kernel,
        out_shape=jax.ShapeDtypeStruct((arrivals, fields, levels, BLK), jnp.bfloat16),
        in_specs=[smem, smem, vmem, vmem, vmem, vmem, vmem],
        out_specs=hbm,
        scratch_shapes=[
            pltpu.VMEM((arrivals, fields, levels, BLK), jnp.bfloat16),
            pltpu.VMEM((fields * entries, BLK), jnp.float32),
            pltpu.VMEM((entries, 8, BLK), jnp.float32),
            pltpu.SemaphoreType.DMA((arrivals // 64,)),
        ],
        compiler_params=pltpu.CompilerParams(vmem_limit_bytes=16 * 2**20),
        name="vertical",
    )(corners, at_top, horizontal, highest, above, hweight, spread)
    return (spectral[None], arrival)


def solution(mesh):
    return jax.shard_map(
        per_device,
        mesh=mesh,
        in_specs=(
            P("lat", None, "lev", None),
            P("lat"),
            P("lat", None, None, None),
            P(),
            P("lat", None, None),
            P("lat", None),
            P("lat", None, None),
            P("lat", "lev"),
        ),
        out_specs=(P("lat", None, None, "lev", None, None), P("lat", None, "lev", None)),
        check_vma=False,
    )
```

```python
import math

import jax
import jax.numpy as jnp
from jax import lax
from jax.experimental import pallas as pl
from jax.experimental.pallas import tpu as pltpu
from jax.sharding import PartitionSpec as P

NLON = 2560
BLK = 128
BLOCKS_X = NLON // BLK
LANES = 128
GRANT = 56 * 2**20

diffusion = 3.0

NT = (((1,), (1,)), ((), ()))
NN = (((1,), (0,)), ((), ()))


def mxu(left, right, dims):
    return lax.dot_general(left, right, dims, preferred_element_type=jnp.float32)


def identity(size):
    rows = lax.broadcasted_iota(jnp.int32, (size, size), 0)
    columns = lax.broadcasted_iota(jnp.int32, (size, size), 1)
    return (rows == columns).astype(jnp.float32).astype(jnp.bfloat16)


def damping_curve(degrees):
    order_n = jnp.arange(degrees, dtype=jnp.float32)
    ratio = order_n * (order_n + 1.0) / float(degrees * (degrees - 1))
    return 1.0 / (1.0 + diffusion * ratio * ratio)


def pack_kernel(
    owner_in, ids_in, gauss_in, fourier_in, message, owner, send_ids, gauss, fourier, packed, scratch, weight, in_sem, out_sem
):
    lat_dev, fields, levels, columns = fourier.shape
    owners = packed.shape[0]
    tiles = scratch.shape[0]
    slots = (tiles * LANES) // (2 * fields * levels)
    chunk = 8
    pieces = lat_dev // chunk
    small = [
        pltpu.make_async_copy(source, target, in_sem.at[pieces + i])
        for i, (source, target) in enumerate(((owner_in, owner), (ids_in, send_ids), (gauss_in, gauss)))
    ]
    large = [
        pltpu.make_async_copy(
            fourier_in.at[pl.ds(i * chunk, chunk)], fourier.at[pl.ds(i * chunk, chunk)], in_sem.at[i]
        )
        for i in range(pieces)
    ]
    for copy in small + large:
        copy.start()
    for copy in small:
        copy.wait()

    waves = owner.shape[1]
    wave_at = lax.broadcasted_iota(jnp.int32, (waves, columns), 0)
    column = lax.broadcasted_iota(jnp.int32, (waves, columns), 1)
    square_row = lax.broadcasted_iota(jnp.int32, (waves, waves), 0)
    square_column = lax.broadcasted_iota(jnp.int32, (waves, waves), 1)
    listed = jnp.broadcast_to(owner[...], (waves, waves))
    upright = jnp.sum(jnp.where(square_row == square_column, listed, 0), axis=1, keepdims=True)
    upright = jnp.broadcast_to(upright, (waves, columns))
    column_owner = jnp.sum(jnp.where(wave_at == column // 2, upright, 0), axis=0, keepdims=True)
    earlier = (upright == jnp.broadcast_to(column_owner, (waves, columns))) & (wave_at < column // 2)
    column_rank = jnp.sum(jnp.where(earlier, 1, 0), axis=0, keepdims=True)
    owner_at = lax.broadcasted_iota(jnp.int32, (owners, columns), 0)
    chooser = jnp.where(owner_at == column_owner, 1.0, 0.0).astype(jnp.bfloat16)
    part_of = 2 * column_rank + lax.broadcasted_iota(jnp.int32, (1, columns), 1) % 2
    masks = [
        jnp.broadcast_to(jnp.where(part_of == i, 1.0, 0.0), (levels, columns)).astype(jnp.bfloat16)
        for i in range(2 * slots)
    ]
    turn_row = lax.broadcasted_iota(jnp.int32, (lat_dev, lat_dev), 0)
    turn_column = lax.broadcasted_iota(jnp.int32, (lat_dev, lat_dev), 1)
    weights = jnp.where(turn_row == turn_column, jnp.broadcast_to(gauss[...], (lat_dev, lat_dev)), 0.0)
    weight[...] = jnp.broadcast_to(jnp.sum(weights, axis=1, keepdims=True), weight.shape)

    for t in range(lat_dev):
        if t % chunk == 0:
            large[t // chunk].wait()
        rows = fourier[t].reshape(fields * levels, columns).astype(jnp.float32)
        rows = (rows * weight[t : t + 1, :]).astype(jnp.bfloat16)
        parts = []
        for slot in range(slots):
            for field in range(fields):
                for part in range(2):
                    parts.append(rows[field * levels : (field + 1) * levels] * masks[2 * slot + part])
        spread = jnp.concatenate(parts, axis=0)
        chosen = mxu(chooser, spread, NT)
        for tile in range(tiles):
            scratch[tile, pl.ds(t, owners, stride=lat_dev), :] = chosen[:, tile * LANES : (tile + 1) * LANES]

    ids = send_ids[...].astype(jnp.float32)
    in_row = jnp.floor((ids + 0.5) * (1.0 / BLOCKS_X))
    in_column = ids - in_row * BLOCKS_X
    sides = [in_row[k : k + 1] for k in range(ids.shape[0])] + [in_column[k : k + 1] for k in range(ids.shape[0])]
    extra = jnp.broadcast_to(jnp.concatenate(sides, axis=1), (8, LANES))
    group = 8
    copies = []
    for o in range(owners):
        parts = [scratch[tile, o * lat_dev : (o + 1) * lat_dev, :] for tile in range(tiles)]
        packed[o] = jnp.concatenate(parts + [extra], axis=0).astype(jnp.bfloat16)
        if o % group == group - 1:
            first = o + 1 - group
            copies.append(
                pltpu.make_async_copy(
                    packed.at[pl.ds(first, group)], message.at[pl.ds(first, group)], out_sem.at[o // group]
                )
            )
            copies[-1].start()
    for copy in copies:
        copy.wait()


def spectral_kernel(
    arrived, tables_in, damping, spectral, message, tables, made, turned, rows_at, listed, row_of, listed_sem, in_sem, out_sem
):
    slots, per_slot, degrees = spectral.shape
    latitudes = tables.shape[1]

    def fetch(slot):
        return pltpu.make_async_copy(tables_in.at[slot], tables.at[slot], in_sem.at[slot])

    def fetch_one(slot, carry):
        fetch(slot).start()
        return carry

    lax.fori_loop(0, slots, fetch_one, 0)
    half = per_slot // 2
    field_rows = half // 3
    bands = arrived.shape[0]
    tiles = turned.shape[0] // LANES
    lat_dev = (arrived.shape[1] - 8) // tiles
    receivers, message_rows, message_lanes = message.shape
    lists = pltpu.make_async_copy(listed, row_of, listed_sem)

    wide = arrived[...].astype(jnp.float32)
    band = lax.broadcasted_iota(jnp.int32, (bands, LANES), 0)
    listed[...] = (wide[:, tiles * lat_dev, :].astype(jnp.int32) + band * lat_dev) * 8
    lists.start()
    unit = identity(LANES)
    for tile in range(tiles):
        columns = wide[:, tile * lat_dev : (tile + 1) * lat_dev, :].reshape(latitudes, LANES)
        turned[tile * LANES : (tile + 1) * LANES, :] = mxu(unit, columns.astype(jnp.bfloat16), NT).astype(jnp.bfloat16)

    gap = jnp.zeros((LANES - half, degrees), jnp.bfloat16)
    chunk = 256

    def one_slot(slot, carry):
        fetch(slot).wait()
        own = turned[pl.ds(pl.multiple_of(slot * per_slot, 32), per_slot), :]
        spectra = mxu(own, tables[slot], NN)
        damped = (spectra * damping[pl.ds(slot, 1), :]).astype(jnp.bfloat16)
        spectral[slot] = damped
        sides = []
        for part in range(2):
            for field in range(3):
                at = (2 * field + part) * field_rows
                sides.append(damped[at : at + field_rows])
            sides.append(gap)
        sides = jnp.concatenate(sides, axis=0)
        for at in range(0, latitudes, chunk):
            back = mxu(tables[slot, at : at + chunk, :], sides, NT)
            for part in range(2):
                rows_at[pl.ds(at * 2 * slots + slot * 2 + part, chunk, stride=2 * slots), :] = back[
                    :, part * LANES : (part + 1) * LANES
                ]
        return carry

    lax.fori_loop(0, slots, one_slot, 0)

    lists.wait()
    lane = lax.broadcasted_iota(jnp.int32, (8, LANES), 1)
    wide_tiles = message_lanes // LANES

    group = 4
    groups = receivers // group

    def send(g):
        at = pl.multiple_of(g * group, group)
        return pltpu.make_async_copy(made.at[pl.ds(at, group)], message.at[pl.ds(at, group)], out_sem.at[g])

    def one_group(g, carry):
        for k in range(group):
            r = g * group + k
            for pair in range(message_rows // 16):
                halves = []
                for side in range(2):
                    built = [None] * wide_tiles
                    for e in range(8):
                        entry = (pair * 2 + side) * 8 + e
                        at = pl.multiple_of(row_of[entry // 2, receivers * (entry % 2) + r], 8)
                        row = rows_at[pl.ds(at, 8), :]
                        start = e * half
                        if start % LANES:
                            row = pltpu.roll(row, start % LANES, 1)
                        for tile in range(start // LANES, (start + half - 1) // LANES + 1):
                            first = start - tile * LANES
                            if built[tile] is None:
                                built[tile] = row
                            else:
                                built[tile] = jnp.where(lane >= first, row, built[tile])
                    halves.append(jnp.concatenate(built, axis=1))
                both = jnp.concatenate(halves, axis=0).astype(jnp.bfloat16)
                made[r, pair * 16 : (pair + 1) * 16, :] = both
        send(g).start()
        return carry

    lax.fori_loop(0, groups, one_group, 0)
    for g in range(groups):
        send(g).wait()


def block_kernel(
    column_of, received, zonal, vweight, blocks, lowest, highest, spread, lowest_scratch, highest_scratch
):
    owners, message_rows, message_lanes = received.shape
    unit = identity(LANES)
    half = message_lanes // 8
    groups = message_rows // 8
    entries = blocks.shape[0]
    rows, levels, _ = spread.shape
    per_entry = rows // entries
    for pair in range(groups // 2):
        wide = received[:, pair * 16 : (pair + 1) * 16, :].astype(jnp.float32)
        for side in range(2):
            group = pair * 2 + side
            own = wide[:, side * 8 : (side + 1) * 8, :].reshape(owners * 8, message_lanes).astype(jnp.bfloat16)
            turned = [
                mxu(unit, own[:, tile * LANES : (tile + 1) * LANES], NT).astype(jnp.bfloat16)
                for tile in range(message_lanes // LANES)
            ]
            turned = jnp.concatenate(turned, axis=0)
            for e in range(8):
                entry = group * 8 + e
                made = mxu(turned[e * half : (e + 1) * half], zonal[column_of[entry]], NN)
                blocks[entry] = made.astype(jnp.bfloat16)
                for a in range(entry * per_entry, (entry + 1) * per_entry):
                    spread[a] = jnp.broadcast_to(vweight[:, a : a + 1], (levels, LANES))
                for field in range(3):
                    lowest_scratch[field * entries + entry : field * entries + entry + 1, :] = made[
                        field * 16 : field * 16 + 1, :
                    ]
                    highest_scratch[field * entries + entry : field * entries + entry + 1, :] = made[
                        field * 16 + 15 : field * 16 + 16, :
                    ]
    lowest[...] = lowest_scratch[...].astype(jnp.bfloat16)
    highest[...] = highest_scratch[...].astype(jnp.bfloat16)


def horizontal_kernel(stencil, blocks, hweight, horizontal, wide):
    entries = blocks.shape[0]
    rows = horizontal.shape[0]
    together = 8

    def widen(i, carry):
        for k in range(together):
            wide[i * together + k] = blocks[i * together + k].astype(jnp.float32)
        return carry

    lax.fori_loop(0, entries // together, widen, 0)

    def some_rows(i, carry):
        for k in range(together):
            a = i * together + k
            total = None
            for q in range(4):
                term = hweight[a, q : q + 1, :] * wide[stencil[q, a]]
                total = term if total is None else total + term
            horizontal[a] = total
        return carry

    lax.fori_loop(0, rows // together, some_rows, 0)


def vertical_kernel(stencil, at_top, horizontal, highest, above, hweight, spread, arrival, made, over_rows, wide, out_sem):
    rows, fields, levels, _ = made.shape
    entries = wide.shape[0]
    top = at_top[0] == 1
    over_rows[...] = jnp.where(top, highest[...].astype(jnp.float32), above[...].astype(jnp.float32))
    together = 8

    def widen(i, carry):
        for k in range(together):
            entry = i * together + k
            for field in range(fields):
                wide[entry, 7 - field : 8 - field, :] = over_rows[pl.ds(field * entries + entry, 1), :]
        return carry

    lax.fori_loop(0, entries // together, widen, 0)

    row = lax.broadcasted_iota(jnp.int32, (8, LANES), 0)
    piece = 64
    pieces = rows // piece

    def send(i):
        at = pl.multiple_of(i * piece, piece)
        return pltpu.make_async_copy(made.at[pl.ds(at, piece)], arrival.at[pl.ds(at, piece)], out_sem.at[i])

    def some_rows(i, carry):
        for k in range(piece):
            a = i * piece + k
            last = None
            for q in range(4):
                term = hweight[a, q : q + 1, :] * wide[stencil[q, a]]
                last = term if last is None else last + term
            for field in range(fields):
                parts = []
                over = last if field == 0 else pltpu.roll(last, field, 0)
                for part in reversed(range(levels // 8)):
                    here = horizontal[a, field * levels + part * 8 : field * levels + (part + 1) * 8, :]
                    turned = pltpu.roll(here, 7, 0)
                    up = jnp.where(row == 7, over, turned)
                    parts.insert(0, here + spread[a, part * 8 : (part + 1) * 8, :] * (up - here))
                    over = turned
                made[a, field] = jnp.concatenate(parts, axis=0).astype(jnp.bfloat16)
        send(i).start()
        return carry

    lax.fori_loop(0, pieces, some_rows, 0)
    for i in range(pieces):
        send(i).wait()


def whole(memory):
    return pl.BlockSpec(memory_space=memory)


def per_device(fourier, gauss, legendre, owner, send_list, stencil, hweight, vweight):
    lat_count = lax.axis_size("lat")
    device_row = lax.axis_index("lat")
    lat_dev, fields, levels, columns = fourier.shape
    wave_total = columns // 2
    slot_most = legendre.shape[1]
    degrees = legendre.shape[3]
    latitudes = legendre.shape[2]
    slot_count = lat_count * slot_most
    capacity = send_list.shape[2]
    arrivals = stencil.shape[0]
    half = fields * levels
    per_slot = 2 * half
    message_lanes = slot_most * per_slot
    tiles = message_lanes // LANES
    entries = lat_count * capacity

    owners = owner[:, 0]
    wave_index = jnp.arange(wave_total, dtype=jnp.int32)
    earlier = (owners[:, None] == owners[None, :]) & (wave_index[:, None] < wave_index[None, :])
    slot_rank = jnp.sum(earlier.astype(jnp.int32), axis=0)
    slot_of = owners * slot_most + slot_rank
    wave_number = wave_index * (degrees // wave_total)
    vmem = whole(pltpu.VMEM)
    smem = whole(pltpu.SMEM)
    hbm = whole(pl.ANY)
    message_one = pl.pallas_call(
        pack_kernel,
        out_shape=jax.ShapeDtypeStruct((lat_count, tiles * lat_dev + 8, LANES), jnp.bfloat16),
        in_specs=[hbm, hbm, hbm, hbm],
        out_specs=hbm,
        scratch_shapes=[
            pltpu.VMEM((1, wave_total), jnp.int32),
            pltpu.VMEM((capacity, lat_count), jnp.int32),
            pltpu.VMEM((1, lat_dev), jnp.float32),
            pltpu.VMEM(fourier.shape, jnp.bfloat16),
            pltpu.VMEM((lat_count, tiles * lat_dev + 8, LANES), jnp.bfloat16),
            pltpu.VMEM((tiles, lat_count * lat_dev, LANES), jnp.float32),
            pltpu.VMEM((lat_dev, columns), jnp.float32),
            pltpu.SemaphoreType.DMA((lat_dev // 8 + 3,)),
            pltpu.SemaphoreType.DMA((lat_count // 8,)),
        ],
        compiler_params=pltpu.CompilerParams(vmem_limit_bytes=GRANT),
        name="pack",
    )(owner.reshape(1, wave_total), send_list[0].T, gauss.reshape(1, lat_dev), fourier)
    arrived = lax.all_to_all(message_one, "lat", split_axis=0, concat_axis=0, tiled=True)

    placed = (slot_of[:, None] == jnp.arange(slot_count, dtype=jnp.int32)[None, :]).astype(jnp.int32)
    owned = lax.dynamic_slice_in_dim(placed, device_row * slot_most, slot_most, 1)
    filled = jnp.sum(owned, axis=0) > 0
    slot_wave = jnp.sum(owned * wave_number[:, None], axis=0)
    degree_index = jnp.arange(degrees, dtype=jnp.int32)
    keep_mask = (filled[:, None] & (degree_index[None, :] >= slot_wave[:, None])).astype(jnp.float32)
    damping = keep_mask * damping_curve(degrees)[None, :]

    message_shape = (lat_count, entries // 8 * slot_most * 2, 8 * half)
    spectral_rows, message_two = pl.pallas_call(
        spectral_kernel,
        in_specs=[vmem, hbm, vmem],
        out_specs=[vmem, hbm],
        scratch_shapes=[
            pltpu.VMEM((slot_most, latitudes, degrees), jnp.bfloat16),
            pltpu.VMEM(message_shape, jnp.bfloat16),
            pltpu.VMEM((message_lanes, latitudes), jnp.bfloat16),
            pltpu.VMEM((latitudes * 2 * slot_most, LANES), jnp.float32),
            pltpu.VMEM((lat_count, LANES), jnp.int32),
            pltpu.SMEM((lat_count, LANES), jnp.int32),
            pltpu.SemaphoreType.DMA,
            pltpu.SemaphoreType.DMA((slot_most,)),
            pltpu.SemaphoreType.DMA((lat_count // 4,)),
        ],
        out_shape=[
            jax.ShapeDtypeStruct((slot_most, per_slot, degrees), jnp.bfloat16),
            jax.ShapeDtypeStruct(message_shape, jnp.bfloat16),
        ],
        compiler_params=pltpu.CompilerParams(vmem_limit_bytes=52 * 2**20),
        name="spectral",
    )(arrived, legendre[0], damping)
    received = lax.all_to_all(message_two, "lat", split_axis=0, concat_axis=0, tiled=True)

    spectral = jnp.transpose(
        spectral_rows.reshape(slot_most, fields, 2, levels, degrees), (0, 1, 3, 2, 4)
    )
    slot_waves = jnp.sum(placed * wave_number[:, None], axis=0)
    slot_waves, spectral = lax.optimization_barrier((slot_waves, spectral))
    present = (jnp.sum(placed, axis=0) > 0).astype(jnp.float32)
    points = jnp.arange(NLON, dtype=jnp.int32).reshape(BLOCKS_X, 1, 1, BLK)
    phases = slot_waves[None, :, None, None] * points % NLON
    angles = phases.astype(jnp.float32) * (2.0 * math.pi / NLON)
    norm_factor = present[None, :, None, None] / math.sqrt(wave_total)
    zonal = jnp.concatenate([jnp.cos(angles) * norm_factor, -jnp.sin(angles) * norm_factor], axis=2)
    zonal = zonal.astype(jnp.bfloat16).reshape(BLOCKS_X, slot_count * 2, BLK)
    all_columns = arrived[:, tiles * lat_dev, entries:].reshape(lat_count, capacity, lat_count)
    column_of = lax.dynamic_index_in_dim(all_columns, device_row, 2, keepdims=False)
    column_of = column_of.astype(jnp.int32).reshape(-1)
    lev_count = lax.axis_size("lev")
    at_top = (lax.axis_index("lev") == lev_count - 1).astype(jnp.int32).reshape(1)
    vertical = vweight.T
    corners = stencil.T
    received, vertical, corners, at_top = lax.optimization_barrier((received, vertical, corners, at_top))
    blocks, lowest, highest, spread = pl.pallas_call(
        block_kernel,
        out_shape=[
            jax.ShapeDtypeStruct((entries, half, BLK), jnp.bfloat16),
            jax.ShapeDtypeStruct((fields * entries, BLK), jnp.bfloat16),
            jax.ShapeDtypeStruct((fields * entries, BLK), jnp.bfloat16),
            jax.ShapeDtypeStruct((arrivals, levels, BLK), jnp.float32),
        ],
        in_specs=[smem, vmem, vmem, vmem],
        out_specs=[vmem, vmem, vmem, vmem],
        scratch_shapes=[pltpu.VMEM((fields * entries, BLK), jnp.float32)] * 2,
        compiler_params=pltpu.CompilerParams(vmem_limit_bytes=16 * 2**20),
        name="blocks",
    )(column_of, received, zonal, vertical)

    above = lax.ppermute(lowest, "lev", [(i, i - 1) for i in range(1, lev_count)])
    horizontal = pl.pallas_call(
        horizontal_kernel,
        out_shape=jax.ShapeDtypeStruct((arrivals, half, BLK), jnp.float32),
        in_specs=[smem, vmem, vmem],
        out_specs=vmem,
        scratch_shapes=[pltpu.VMEM((entries, half, BLK), jnp.float32)],
        compiler_params=pltpu.CompilerParams(vmem_limit_bytes=16 * 2**20),
        cost_estimate=pl.CostEstimate(
            flops=8 * arrivals * half * BLK, bytes_accessed=4 * arrivals * half * BLK, transcendentals=0
        ),
        name="horizontal",
    )(corners, blocks, hweight)
    arrival = pl.pallas_call(
        vertical_kernel,
        out_shape=jax.ShapeDtypeStruct((arrivals, fields, levels, BLK), jnp.bfloat16),
        in_specs=[smem, smem, vmem, vmem, vmem, vmem, vmem],
        out_specs=hbm,
        scratch_shapes=[
            pltpu.VMEM((arrivals, fields, levels, BLK), jnp.bfloat16),
            pltpu.VMEM((fields * entries, BLK), jnp.float32),
            pltpu.VMEM((entries, 8, BLK), jnp.float32),
            pltpu.SemaphoreType.DMA((arrivals // 64,)),
        ],
        compiler_params=pltpu.CompilerParams(vmem_limit_bytes=16 * 2**20),
        name="vertical",
    )(corners, at_top, horizontal, highest, above, hweight, spread)
    return (spectral[None], arrival)


def solution(mesh):
    return jax.shard_map(
        per_device,
        mesh=mesh,
        in_specs=(
            P("lat", None, "lev", None),
            P("lat"),
            P("lat", None, None, None),
            P(),
            P("lat", None, None),
            P("lat", None),
            P("lat", None, None),
            P("lat", "lev"),
        ),
        out_specs=(P("lat", None, None, "lev", None, None), P("lat", None, "lev", None)),
        check_vma=False,
    )
```

```python
import math

import jax
import jax.numpy as jnp
from jax import lax
from jax.experimental import pallas as pl
from jax.experimental.pallas import tpu as pltpu
from jax.sharding import PartitionSpec as P

NLON = 2560
BLK = 128
BLOCKS_X = NLON // BLK
LANES = 128
GRANT = 56 * 2**20

diffusion = 3.0

NT = (((1,), (1,)), ((), ()))
NN = (((1,), (0,)), ((), ()))


def mxu(left, right, dims):
    return lax.dot_general(left, right, dims, preferred_element_type=jnp.float32)


def identity(size):
    rows = lax.broadcasted_iota(jnp.int32, (size, size), 0)
    columns = lax.broadcasted_iota(jnp.int32, (size, size), 1)
    return (rows == columns).astype(jnp.float32).astype(jnp.bfloat16)


def damping_curve(degrees):
    order_n = jnp.arange(degrees, dtype=jnp.float32)
    ratio = order_n * (order_n + 1.0) / float(degrees * (degrees - 1))
    return 1.0 / (1.0 + diffusion * ratio * ratio)


def pack_kernel(
    owner_in, ids_in, gauss_in, fourier_in, message, owner, send_ids, gauss, fourier, packed, scratch, weight, in_sem, out_sem
):
    lat_dev, fields, levels, columns = fourier.shape
    owners = packed.shape[0]
    tiles = scratch.shape[0]
    slots = (tiles * LANES) // (2 * fields * levels)
    chunk = 8
    pieces = lat_dev // chunk
    small = [
        pltpu.make_async_copy(source, target, in_sem.at[pieces + i])
        for i, (source, target) in enumerate(((owner_in, owner), (ids_in, send_ids), (gauss_in, gauss)))
    ]
    large = [
        pltpu.make_async_copy(
            fourier_in.at[pl.ds(i * chunk, chunk)], fourier.at[pl.ds(i * chunk, chunk)], in_sem.at[i]
        )
        for i in range(pieces)
    ]
    for copy in small + large:
        copy.start()
    for copy in small:
        copy.wait()

    waves = owner.shape[1]
    wave_at = lax.broadcasted_iota(jnp.int32, (waves, columns), 0)
    column = lax.broadcasted_iota(jnp.int32, (waves, columns), 1)
    square_row = lax.broadcasted_iota(jnp.int32, (waves, waves), 0)
    square_column = lax.broadcasted_iota(jnp.int32, (waves, waves), 1)
    listed = jnp.broadcast_to(owner[...], (waves, waves))
    upright = jnp.sum(jnp.where(square_row == square_column, listed, 0), axis=1, keepdims=True)
    upright = jnp.broadcast_to(upright, (waves, columns))
    column_owner = jnp.sum(jnp.where(wave_at == column // 2, upright, 0), axis=0, keepdims=True)
    earlier = (upright == jnp.broadcast_to(column_owner, (waves, columns))) & (wave_at < column // 2)
    column_rank = jnp.sum(jnp.where(earlier, 1, 0), axis=0, keepdims=True)
    owner_at = lax.broadcasted_iota(jnp.int32, (owners, columns), 0)
    chooser = jnp.where(owner_at == column_owner, 1.0, 0.0).astype(jnp.bfloat16)
    part_of = 2 * column_rank + lax.broadcasted_iota(jnp.int32, (1, columns), 1) % 2
    masks = [
        jnp.broadcast_to(jnp.where(part_of == i, 1.0, 0.0), (levels, columns)).astype(jnp.bfloat16)
        for i in range(2 * slots)
    ]
    turn_row = lax.broadcasted_iota(jnp.int32, (lat_dev, lat_dev), 0)
    turn_column = lax.broadcasted_iota(jnp.int32, (lat_dev, lat_dev), 1)
    weights = jnp.where(turn_row == turn_column, jnp.broadcast_to(gauss[...], (lat_dev, lat_dev)), 0.0)
    weight[...] = jnp.broadcast_to(jnp.sum(weights, axis=1, keepdims=True), weight.shape)

    for t in range(lat_dev):
        if t % chunk == 0:
            large[t // chunk].wait()
        rows = fourier[t].reshape(fields * levels, columns).astype(jnp.float32)
        rows = (rows * weight[t : t + 1, :]).astype(jnp.bfloat16)
        parts = []
        for slot in range(slots):
            for field in range(fields):
                for part in range(2):
                    parts.append(rows[field * levels : (field + 1) * levels] * masks[2 * slot + part])
        spread = jnp.concatenate(parts, axis=0)
        chosen = mxu(chooser, spread, NT)
        for tile in range(tiles):
            scratch[tile, pl.ds(t, owners, stride=lat_dev), :] = chosen[:, tile * LANES : (tile + 1) * LANES]

    ids = send_ids[...].astype(jnp.float32)
    in_row = jnp.floor((ids + 0.5) * (1.0 / BLOCKS_X))
    in_column = ids - in_row * BLOCKS_X
    sides = [in_row[k : k + 1] for k in range(ids.shape[0])] + [in_column[k : k + 1] for k in range(ids.shape[0])]
    extra = jnp.broadcast_to(jnp.concatenate(sides, axis=1), (8, LANES))
    group = 8

    def send(g):
        first = pl.multiple_of(g * group, group)
        return pltpu.make_async_copy(packed.at[pl.ds(first, group)], message.at[pl.ds(first, group)], out_sem.at[g])

    def finish(g, carry):
        for k in range(group):
            o = g * group + k
            parts = [scratch[tile, pl.ds(pl.multiple_of(o * lat_dev, 8), lat_dev), :] for tile in range(tiles)]
            packed[o] = jnp.concatenate(parts + [extra], axis=0).astype(jnp.bfloat16)
        send(g).start()
        return carry

    lax.fori_loop(0, owners // group, finish, 0)
    for g in range(owners // group):
        send(g).wait()


def spectral_kernel(
    arrived, tables_in, damping, spectral, message, tables, made, turned, rows_at, listed, row_of, listed_sem, in_sem, out_sem
):
    slots, per_slot, degrees = spectral.shape
    latitudes = tables.shape[1]

    def fetch(slot):
        return pltpu.make_async_copy(tables_in.at[slot], tables.at[slot], in_sem.at[slot])

    def fetch_one(slot, carry):
        fetch(slot).start()
        return carry

    lax.fori_loop(0, slots, fetch_one, 0)
    half = per_slot // 2
    field_rows = half // 3
    bands = arrived.shape[0]
    tiles = turned.shape[0] // LANES
    lat_dev = (arrived.shape[1] - 8) // tiles
    receivers, message_rows, message_lanes = message.shape
    lists = pltpu.make_async_copy(listed, row_of, listed_sem)

    wide = arrived[...].astype(jnp.float32)
    band = lax.broadcasted_iota(jnp.int32, (bands, LANES), 0)
    listed[...] = (wide[:, tiles * lat_dev, :].astype(jnp.int32) + band * lat_dev) * 8
    lists.start()
    unit = identity(LANES)
    for tile in range(tiles):
        columns = wide[:, tile * lat_dev : (tile + 1) * lat_dev, :].reshape(latitudes, LANES)
        turned[tile * LANES : (tile + 1) * LANES, :] = mxu(unit, columns.astype(jnp.bfloat16), NT).astype(jnp.bfloat16)

    gap = jnp.zeros((LANES - half, degrees), jnp.bfloat16)
    chunk = 256

    def one_slot(slot, carry):
        fetch(slot).wait()
        own = turned[pl.ds(pl.multiple_of(slot * per_slot, 32), per_slot), :]
        spectra = mxu(own, tables[slot], NN)
        damped = (spectra * damping[pl.ds(slot, 1), :]).astype(jnp.bfloat16)
        spectral[slot] = damped
        sides = []
        for part in range(2):
            for field in range(3):
                at = (2 * field + part) * field_rows
                sides.append(damped[at : at + field_rows])
            sides.append(gap)
        sides = jnp.concatenate(sides, axis=0)
        for at in range(0, latitudes, chunk):
            back = mxu(tables[slot, at : at + chunk, :], sides, NT)
            for part in range(2):
                rows_at[pl.ds(at * 2 * slots + slot * 2 + part, chunk, stride=2 * slots), :] = back[
                    :, part * LANES : (part + 1) * LANES
                ]
        return carry

    lax.fori_loop(0, slots, one_slot, 0)

    lists.wait()
    lane = lax.broadcasted_iota(jnp.int32, (8, LANES), 1)
    wide_tiles = message_lanes // LANES

    group = 4
    groups = receivers // group

    def send(g):
        at = pl.multiple_of(g * group, group)
        return pltpu.make_async_copy(made.at[pl.ds(at, group)], message.at[pl.ds(at, group)], out_sem.at[g])

    def one_group(g, carry):
        for k in range(group):
            r = g * group + k
            for pair in range(message_rows // 16):
                halves = []
                for side in range(2):
                    built = [None] * wide_tiles
                    for e in range(8):
                        entry = (pair * 2 + side) * 8 + e
                        at = pl.multiple_of(row_of[entry // 2, receivers * (entry % 2) + r], 8)
                        row = rows_at[pl.ds(at, 8), :]
                        start = e * half
                        if start % LANES:
                            row = pltpu.roll(row, start % LANES, 1)
                        for tile in range(start // LANES, (start + half - 1) // LANES + 1):
                            first = start - tile * LANES
                            if built[tile] is None:
                                built[tile] = row
                            else:
                                built[tile] = jnp.where(lane >= first, row, built[tile])
                    halves.append(jnp.concatenate(built, axis=1))
                both = jnp.concatenate(halves, axis=0).astype(jnp.bfloat16)
                made[r, pair * 16 : (pair + 1) * 16, :] = both
        send(g).start()
        return carry

    lax.fori_loop(0, groups, one_group, 0)
    for g in range(groups):
        send(g).wait()


def block_kernel(
    column_of, received, zonal, vweight, blocks, lowest, highest, spread, lowest_scratch, highest_scratch
):
    owners, message_rows, message_lanes = received.shape
    unit = identity(LANES)
    half = message_lanes // 8
    groups = message_rows // 8
    entries = blocks.shape[0]
    rows, levels, _ = spread.shape
    per_entry = rows // entries
    for pair in range(groups // 2):
        wide = received[:, pair * 16 : (pair + 1) * 16, :].astype(jnp.float32)
        for side in range(2):
            group = pair * 2 + side
            own = wide[:, side * 8 : (side + 1) * 8, :].reshape(owners * 8, message_lanes).astype(jnp.bfloat16)
            turned = [
                mxu(unit, own[:, tile * LANES : (tile + 1) * LANES], NT).astype(jnp.bfloat16)
                for tile in range(message_lanes // LANES)
            ]
            turned = jnp.concatenate(turned, axis=0)
            for e in range(8):
                entry = group * 8 + e
                made = mxu(turned[e * half : (e + 1) * half], zonal[column_of[entry]], NN)
                made = made.astype(jnp.bfloat16).astype(jnp.float32)
                blocks[entry] = made
                for a in range(entry * per_entry, (entry + 1) * per_entry):
                    spread[a] = jnp.broadcast_to(vweight[:, a : a + 1], (levels, LANES))
                for field in range(3):
                    lowest_scratch[field * entries + entry : field * entries + entry + 1, :] = made[
                        field * 16 : field * 16 + 1, :
                    ]
                    highest_scratch[field * entries + entry : field * entries + entry + 1, :] = made[
                        field * 16 + 15 : field * 16 + 16, :
                    ]
    lowest[...] = lowest_scratch[...].astype(jnp.bfloat16)
    highest[...] = highest_scratch[...].astype(jnp.bfloat16)


def horizontal_kernel(stencil, blocks, hweight, horizontal):
    rows = horizontal.shape[0]
    together = 32

    def some_rows(i, carry):
        for k in range(together):
            a = i * together + k
            total = None
            for q in range(4):
                term = hweight[a, q : q + 1, :] * blocks[stencil[q, a]]
                total = term if total is None else total + term
            horizontal[a] = total
        return carry

    lax.fori_loop(0, rows // together, some_rows, 0)


def vertical_kernel(stencil, at_top, horizontal, highest, above, hweight, spread, arrival, made, over_rows, wide, out_sem):
    rows, fields, levels, _ = made.shape
    entries = wide.shape[0]
    top = at_top[0] == 1
    over_rows[...] = jnp.where(top, highest[...].astype(jnp.float32), above[...].astype(jnp.float32))
    together = 8

    def widen(i, carry):
        for k in range(together):
            entry = i * together + k
            for field in range(fields):
                wide[entry, 7 - field : 8 - field, :] = over_rows[pl.ds(field * entries + entry, 1), :]
        return carry

    lax.fori_loop(0, entries // together, widen, 0)

    row = lax.broadcasted_iota(jnp.int32, (8, LANES), 0)
    piece = 32
    pieces = rows // piece

    def send(i):
        at = pl.multiple_of(i * piece, piece)
        return pltpu.make_async_copy(made.at[pl.ds(at, piece)], arrival.at[pl.ds(at, piece)], out_sem.at[i])

    def some_rows(i, carry):
        for k in range(piece):
            a = i * piece + k
            last = None
            for q in range(4):
                term = hweight[a, q : q + 1, :] * wide[stencil[q, a]]
                last = term if last is None else last + term
            for field in range(fields):
                parts = []
                over = last if field == 0 else pltpu.roll(last, field, 0)
                for part in reversed(range(levels // 8)):
                    here = horizontal[a, field * levels + part * 8 : field * levels + (part + 1) * 8, :]
                    turned = pltpu.roll(here, 7, 0)
                    up = jnp.where(row == 7, over, turned)
                    parts.insert(0, here + spread[a, part * 8 : (part + 1) * 8, :] * (up - here))
                    over = turned
                made[a, field] = jnp.concatenate(parts, axis=0).astype(jnp.bfloat16)
        send(i).start()
        return carry

    lax.fori_loop(0, pieces, some_rows, 0)
    for i in range(pieces):
        send(i).wait()


def whole(memory):
    return pl.BlockSpec(memory_space=memory)


def per_device(fourier, gauss, legendre, owner, send_list, stencil, hweight, vweight):
    lat_count = lax.axis_size("lat")
    device_row = lax.axis_index("lat")
    lat_dev, fields, levels, columns = fourier.shape
    wave_total = columns // 2
    slot_most = legendre.shape[1]
    degrees = legendre.shape[3]
    latitudes = legendre.shape[2]
    slot_count = lat_count * slot_most
    capacity = send_list.shape[2]
    arrivals = stencil.shape[0]
    half = fields * levels
    per_slot = 2 * half
    message_lanes = slot_most * per_slot
    tiles = message_lanes // LANES
    entries = lat_count * capacity

    owners = owner[:, 0]
    wave_index = jnp.arange(wave_total, dtype=jnp.int32)
    earlier = (owners[:, None] == owners[None, :]) & (wave_index[:, None] < wave_index[None, :])
    slot_rank = jnp.sum(earlier.astype(jnp.int32), axis=0)
    slot_of = owners * slot_most + slot_rank
    wave_number = wave_index * (degrees // wave_total)
    vmem = whole(pltpu.VMEM)
    smem = whole(pltpu.SMEM)
    hbm = whole(pl.ANY)
    message_one = pl.pallas_call(
        pack_kernel,
        out_shape=jax.ShapeDtypeStruct((lat_count, tiles * lat_dev + 8, LANES), jnp.bfloat16),
        in_specs=[hbm, hbm, hbm, hbm],
        out_specs=hbm,
        scratch_shapes=[
            pltpu.VMEM((1, wave_total), jnp.int32),
            pltpu.VMEM((capacity, lat_count), jnp.int32),
            pltpu.VMEM((1, lat_dev), jnp.float32),
            pltpu.VMEM(fourier.shape, jnp.bfloat16),
            pltpu.VMEM((lat_count, tiles * lat_dev + 8, LANES), jnp.bfloat16),
            pltpu.VMEM((tiles, lat_count * lat_dev, LANES), jnp.float32),
            pltpu.VMEM((lat_dev, columns), jnp.float32),
            pltpu.SemaphoreType.DMA((lat_dev // 8 + 3,)),
            pltpu.SemaphoreType.DMA((lat_count // 8,)),
        ],
        compiler_params=pltpu.CompilerParams(vmem_limit_bytes=GRANT),
        name="pack",
    )(owner.reshape(1, wave_total), send_list[0].T, gauss.reshape(1, lat_dev), fourier)
    arrived = lax.all_to_all(message_one, "lat", split_axis=0, concat_axis=0, tiled=True)

    placed = (slot_of[:, None] == jnp.arange(slot_count, dtype=jnp.int32)[None, :]).astype(jnp.int32)
    owned = lax.dynamic_slice_in_dim(placed, device_row * slot_most, slot_most, 1)
    filled = jnp.sum(owned, axis=0) > 0
    slot_wave = jnp.sum(owned * wave_number[:, None], axis=0)
    degree_index = jnp.arange(degrees, dtype=jnp.int32)
    keep_mask = (filled[:, None] & (degree_index[None, :] >= slot_wave[:, None])).astype(jnp.float32)
    damping = keep_mask * damping_curve(degrees)[None, :]

    message_shape = (lat_count, entries // 8 * slot_most * 2, 8 * half)
    spectral_rows, message_two = pl.pallas_call(
        spectral_kernel,
        in_specs=[vmem, hbm, vmem],
        out_specs=[vmem, hbm],
        scratch_shapes=[
            pltpu.VMEM((slot_most, latitudes, degrees), jnp.bfloat16),
            pltpu.VMEM(message_shape, jnp.bfloat16),
            pltpu.VMEM((message_lanes, latitudes), jnp.bfloat16),
            pltpu.VMEM((latitudes * 2 * slot_most, LANES), jnp.float32),
            pltpu.VMEM((lat_count, LANES), jnp.int32),
            pltpu.SMEM((lat_count, LANES), jnp.int32),
            pltpu.SemaphoreType.DMA,
            pltpu.SemaphoreType.DMA((slot_most,)),
            pltpu.SemaphoreType.DMA((lat_count // 4,)),
        ],
        out_shape=[
            jax.ShapeDtypeStruct((slot_most, per_slot, degrees), jnp.bfloat16),
            jax.ShapeDtypeStruct(message_shape, jnp.bfloat16),
        ],
        compiler_params=pltpu.CompilerParams(vmem_limit_bytes=52 * 2**20),
        name="spectral",
    )(arrived, legendre[0], damping)
    received = lax.all_to_all(message_two, "lat", split_axis=0, concat_axis=0, tiled=True)

    spectral = jnp.transpose(
        spectral_rows.reshape(slot_most, fields, 2, levels, degrees), (0, 1, 3, 2, 4)
    )
    slot_waves = jnp.sum(placed * wave_number[:, None], axis=0)
    slot_waves, spectral = lax.optimization_barrier((slot_waves, spectral))
    present = (jnp.sum(placed, axis=0) > 0).astype(jnp.float32)
    points = jnp.arange(NLON, dtype=jnp.int32).reshape(BLOCKS_X, 1, 1, BLK)
    phases = slot_waves[None, :, None, None] * points % NLON
    angles = phases.astype(jnp.float32) * (2.0 * math.pi / NLON)
    norm_factor = present[None, :, None, None] / math.sqrt(wave_total)
    zonal = jnp.concatenate([jnp.cos(angles) * norm_factor, -jnp.sin(angles) * norm_factor], axis=2)
    zonal = zonal.astype(jnp.bfloat16).reshape(BLOCKS_X, slot_count * 2, BLK)
    all_columns = arrived[:, tiles * lat_dev, entries:].reshape(lat_count, capacity, lat_count)
    column_of = lax.dynamic_index_in_dim(all_columns, device_row, 2, keepdims=False)
    column_of = column_of.astype(jnp.int32).reshape(-1)
    lev_count = lax.axis_size("lev")
    at_top = (lax.axis_index("lev") == lev_count - 1).astype(jnp.int32).reshape(1)
    vertical = vweight.T
    corners = stencil.T
    received, vertical, corners, at_top = lax.optimization_barrier((received, vertical, corners, at_top))
    blocks, lowest, highest, spread = pl.pallas_call(
        block_kernel,
        out_shape=[
            jax.ShapeDtypeStruct((entries, half, BLK), jnp.float32),
            jax.ShapeDtypeStruct((fields * entries, BLK), jnp.bfloat16),
            jax.ShapeDtypeStruct((fields * entries, BLK), jnp.bfloat16),
            jax.ShapeDtypeStruct((arrivals, levels, BLK), jnp.float32),
        ],
        in_specs=[smem, vmem, vmem, vmem],
        out_specs=[vmem, vmem, vmem, vmem],
        scratch_shapes=[pltpu.VMEM((fields * entries, BLK), jnp.float32)] * 2,
        compiler_params=pltpu.CompilerParams(vmem_limit_bytes=16 * 2**20),
        name="blocks",
    )(column_of, received, zonal, vertical)

    above = lax.ppermute(lowest, "lev", [(i, i - 1) for i in range(1, lev_count)])
    horizontal = pl.pallas_call(
        horizontal_kernel,
        out_shape=jax.ShapeDtypeStruct((arrivals, half, BLK), jnp.float32),
        in_specs=[smem, vmem, vmem],
        out_specs=vmem,
        compiler_params=pltpu.CompilerParams(vmem_limit_bytes=16 * 2**20),
        cost_estimate=pl.CostEstimate(
            flops=8 * arrivals * half * BLK, bytes_accessed=4 * arrivals * half * BLK, transcendentals=0
        ),
        name="horizontal",
    )(corners, blocks, hweight)
    arrival = pl.pallas_call(
        vertical_kernel,
        out_shape=jax.ShapeDtypeStruct((arrivals, fields, levels, BLK), jnp.bfloat16),
        in_specs=[smem, smem, vmem, vmem, vmem, vmem, vmem],
        out_specs=hbm,
        scratch_shapes=[
            pltpu.VMEM((arrivals, fields, levels, BLK), jnp.bfloat16),
            pltpu.VMEM((fields * entries, BLK), jnp.float32),
            pltpu.VMEM((entries, 8, BLK), jnp.float32),
            pltpu.SemaphoreType.DMA((arrivals // 32,)),
        ],
        compiler_params=pltpu.CompilerParams(vmem_limit_bytes=16 * 2**20),
        name="vertical",
    )(corners, at_top, horizontal, highest, above, hweight, spread)
    return (spectral[None], arrival)


def solution(mesh):
    return jax.shard_map(
        per_device,
        mesh=mesh,
        in_specs=(
            P("lat", None, "lev", None),
            P("lat"),
            P("lat", None, None, None),
            P(),
            P("lat", None, None),
            P("lat", None),
            P("lat", None, None),
            P("lat", "lev"),
        ),
        out_specs=(P("lat", None, None, "lev", None, None), P("lat", None, "lev", None)),
        check_vma=False,
    )
```

```python
import math

import jax
import jax.numpy as jnp
from jax import lax
from jax.experimental import pallas as pl
from jax.experimental.pallas import tpu as pltpu
from jax.sharding import PartitionSpec as P

NLON = 2560
BLK = 128
BLOCKS_X = NLON // BLK
LANES = 128
GRANT = 56 * 2**20

diffusion = 3.0

NT = (((1,), (1,)), ((), ()))
NN = (((1,), (0,)), ((), ()))


def mxu(left, right, dims):
    return lax.dot_general(left, right, dims, preferred_element_type=jnp.float32)


def identity(size):
    rows = lax.broadcasted_iota(jnp.int32, (size, size), 0)
    columns = lax.broadcasted_iota(jnp.int32, (size, size), 1)
    return (rows == columns).astype(jnp.float32).astype(jnp.bfloat16)


def damping_curve(degrees):
    order_n = jnp.arange(degrees, dtype=jnp.float32)
    ratio = order_n * (order_n + 1.0) / float(degrees * (degrees - 1))
    return 1.0 / (1.0 + diffusion * ratio * ratio)


def pack_kernel(
    owner_in, ids_in, gauss_in, fourier_in, message, owner, send_ids, gauss, fourier, packed, scratch, weight, in_sem, out_sem
):
    lat_dev, fields, levels, columns = fourier.shape
    owners = packed.shape[0]
    tiles = scratch.shape[0]
    slots = (tiles * LANES) // (2 * fields * levels)
    chunk = 8
    pieces = lat_dev // chunk
    small = [
        pltpu.make_async_copy(source, target, in_sem.at[pieces + i])
        for i, (source, target) in enumerate(((owner_in, owner), (ids_in, send_ids), (gauss_in, gauss)))
    ]
    large = [
        pltpu.make_async_copy(
            fourier_in.at[pl.ds(i * chunk, chunk)], fourier.at[pl.ds(i * chunk, chunk)], in_sem.at[i]
        )
        for i in range(pieces)
    ]
    for copy in small + large:
        copy.start()
    for copy in small:
        copy.wait()

    waves = owner.shape[1]
    wave_at = lax.broadcasted_iota(jnp.int32, (waves, columns), 0)
    column = lax.broadcasted_iota(jnp.int32, (waves, columns), 1)
    square_row = lax.broadcasted_iota(jnp.int32, (waves, waves), 0)
    square_column = lax.broadcasted_iota(jnp.int32, (waves, waves), 1)
    listed = jnp.broadcast_to(owner[...], (waves, waves))
    upright = jnp.sum(jnp.where(square_row == square_column, listed, 0), axis=1, keepdims=True)
    upright = jnp.broadcast_to(upright, (waves, columns))
    column_owner = jnp.sum(jnp.where(wave_at == column // 2, upright, 0), axis=0, keepdims=True)
    earlier = (upright == jnp.broadcast_to(column_owner, (waves, columns))) & (wave_at < column // 2)
    column_rank = jnp.sum(jnp.where(earlier, 1, 0), axis=0, keepdims=True)
    owner_at = lax.broadcasted_iota(jnp.int32, (owners, columns), 0)
    chooser = jnp.where(owner_at == column_owner, 1.0, 0.0).astype(jnp.bfloat16)
    part_of = 2 * column_rank + lax.broadcasted_iota(jnp.int32, (1, columns), 1) % 2
    masks = [
        jnp.broadcast_to(jnp.where(part_of == i, 1.0, 0.0), (levels, columns)).astype(jnp.bfloat16)
        for i in range(2 * slots)
    ]
    turn_row = lax.broadcasted_iota(jnp.int32, (lat_dev, lat_dev), 0)
    turn_column = lax.broadcasted_iota(jnp.int32, (lat_dev, lat_dev), 1)
    weights = jnp.where(turn_row == turn_column, jnp.broadcast_to(gauss[...], (lat_dev, lat_dev)), 0.0)
    weight[...] = jnp.broadcast_to(jnp.sum(weights, axis=1, keepdims=True), weight.shape)

    none = jnp.zeros_like(chooser)
    chooser = jnp.concatenate(
        [jnp.concatenate([chooser, none], axis=1), jnp.concatenate([none, chooser], axis=1)], axis=0
    )
    for pair in range(0, lat_dev, 2):
        if pair % chunk == 0:
            large[pair // chunk].wait()
        spread = []
        for t in range(pair, pair + 2):
            rows = fourier[t].reshape(fields * levels, columns).astype(jnp.float32)
            rows = (rows * weight[t : t + 1, :]).astype(jnp.bfloat16)
            parts = []
            for slot in range(slots):
                for field in range(fields):
                    for part in range(2):
                        parts.append(rows[field * levels : (field + 1) * levels] * masks[2 * slot + part])
            spread.append(jnp.concatenate(parts, axis=0))
        chosen = mxu(chooser, jnp.concatenate(spread, axis=1), NT)
        for side in range(2):
            for tile in range(tiles):
                scratch[tile, pl.ds(pair + side, owners, stride=lat_dev), :] = chosen[
                    side * owners : (side + 1) * owners, tile * LANES : (tile + 1) * LANES
                ]

    ids = send_ids[...].astype(jnp.float32)
    in_row = jnp.floor((ids + 0.5) * (1.0 / BLOCKS_X))
    in_column = ids - in_row * BLOCKS_X
    sides = [in_row[k : k + 1] for k in range(ids.shape[0])] + [in_column[k : k + 1] for k in range(ids.shape[0])]
    extra = jnp.broadcast_to(jnp.concatenate(sides, axis=1), (8, LANES))
    group = 8

    def send(g):
        first = pl.multiple_of(g * group, group)
        return pltpu.make_async_copy(packed.at[pl.ds(first, group)], message.at[pl.ds(first, group)], out_sem.at[g])

    def finish(g, carry):
        for k in range(group):
            o = g * group + k
            parts = [scratch[tile, pl.ds(pl.multiple_of(o * lat_dev, 8), lat_dev), :] for tile in range(tiles)]
            packed[o] = jnp.concatenate(parts + [extra], axis=0).astype(jnp.bfloat16)
        send(g).start()
        return carry

    lax.fori_loop(0, owners // group, finish, 0)
    for g in range(owners // group):
        send(g).wait()


def fetch_kernel(table_in, table, room, sem):
    copy = pltpu.make_async_copy(table_in.at[0], table, sem)
    copy.start()
    copy.wait()


def spectral_kernel(
    arrived, first_table, tables_in, damping, _, spectral, message, tables, made, turned, rows_at, listed, row_of, listed_sem, in_sem, out_sem
):
    slots, per_slot, degrees = spectral.shape
    latitudes = tables.shape[1]

    def fetch(slot):
        return pltpu.make_async_copy(tables_in.at[slot], tables.at[slot - 1], in_sem.at[slot - 1])

    def fetch_one(slot, carry):
        fetch(slot).start()
        return carry

    lax.fori_loop(1, slots, fetch_one, 0)
    half = per_slot // 2
    field_rows = half // 3
    bands = arrived.shape[0]
    tiles = turned.shape[0] // LANES
    lat_dev = (arrived.shape[1] - 8) // tiles
    receivers, message_rows, message_lanes = message.shape
    lists = pltpu.make_async_copy(listed, row_of, listed_sem)

    wide = arrived[...].astype(jnp.float32)
    band = lax.broadcasted_iota(jnp.int32, (bands, LANES), 0)
    listed[...] = (wide[:, tiles * lat_dev, :].astype(jnp.int32) + band * lat_dev) * 8
    lists.start()
    unit = identity(LANES)
    for tile in range(tiles):
        columns = wide[:, tile * lat_dev : (tile + 1) * lat_dev, :].reshape(latitudes, LANES)
        turned[tile * LANES : (tile + 1) * LANES, :] = mxu(unit, columns.astype(jnp.bfloat16), NT).astype(jnp.bfloat16)

    gap = jnp.zeros((LANES - half, degrees), jnp.bfloat16)
    chunk = 256

    def one_slot(slot, table):
        own = turned[pl.ds(pl.multiple_of(slot * per_slot, 32), per_slot), :]
        spectra = mxu(own, table[...], NN)
        damped = (spectra * damping[pl.ds(slot, 1), :]).astype(jnp.bfloat16)
        spectral[slot] = damped
        sides = []
        for part in range(2):
            for field in range(3):
                at = (2 * field + part) * field_rows
                sides.append(damped[at : at + field_rows])
            sides.append(gap)
        sides = jnp.concatenate(sides, axis=0)
        for at in range(0, latitudes, chunk):
            back = mxu(table[at : at + chunk, :], sides, NT)
            for part in range(2):
                rows_at[pl.ds(at * 2 * slots + slot * 2 + part, chunk, stride=2 * slots), :] = back[
                    :, part * LANES : (part + 1) * LANES
                ]

    def later_slot(slot, carry):
        fetch(slot).wait()
        one_slot(slot, tables.at[slot - 1])
        return carry

    one_slot(0, first_table)
    lax.fori_loop(1, slots, later_slot, 0)

    lists.wait()
    lane = lax.broadcasted_iota(jnp.int32, (8, LANES), 1)
    wide_tiles = message_lanes // LANES

    group = 4
    groups = receivers // group

    def send(g):
        at = pl.multiple_of(g * group, group)
        return pltpu.make_async_copy(made.at[pl.ds(at, group)], message.at[pl.ds(at, group)], out_sem.at[g])

    def one_group(g, carry):
        for k in range(group):
            r = g * group + k
            for pair in range(message_rows // 16):
                halves = []
                for side in range(2):
                    built = [None] * wide_tiles
                    for e in range(8):
                        entry = (pair * 2 + side) * 8 + e
                        at = pl.multiple_of(row_of[entry // 2, receivers * (entry % 2) + r], 8)
                        row = rows_at[pl.ds(at, 8), :]
                        start = e * half
                        if start % LANES:
                            row = pltpu.roll(row, start % LANES, 1)
                        for tile in range(start // LANES, (start + half - 1) // LANES + 1):
                            first = start - tile * LANES
                            if built[tile] is None:
                                built[tile] = row
                            else:
                                built[tile] = jnp.where(lane >= first, row, built[tile])
                    halves.append(jnp.concatenate(built, axis=1))
                both = jnp.concatenate(halves, axis=0).astype(jnp.bfloat16)
                made[r, pair * 16 : (pair + 1) * 16, :] = both
        send(g).start()
        return carry

    lax.fori_loop(0, groups, one_group, 0)
    for g in range(groups):
        send(g).wait()


def block_kernel(
    column_of, received, zonal, vweight, blocks, lowest, highest, spread, lowest_scratch, highest_scratch
):
    owners, message_rows, message_lanes = received.shape
    unit = identity(LANES)
    half = message_lanes // 8
    groups = message_rows // 8
    entries = blocks.shape[0]
    rows, levels, _ = spread.shape
    per_entry = rows // entries
    for pair in range(groups // 2):
        wide = received[:, pair * 16 : (pair + 1) * 16, :].astype(jnp.float32)
        for side in range(2):
            group = pair * 2 + side
            own = wide[:, side * 8 : (side + 1) * 8, :].reshape(owners * 8, message_lanes).astype(jnp.bfloat16)
            turned = [
                mxu(unit, own[:, tile * LANES : (tile + 1) * LANES], NT).astype(jnp.bfloat16)
                for tile in range(message_lanes // LANES)
            ]
            turned = jnp.concatenate(turned, axis=0)
            for e in range(8):
                entry = group * 8 + e
                made = mxu(turned[e * half : (e + 1) * half], zonal[column_of[entry]], NN)
                made = made.astype(jnp.bfloat16).astype(jnp.float32)
                blocks[entry] = made
                for a in range(entry * per_entry, (entry + 1) * per_entry):
                    spread[a] = jnp.broadcast_to(vweight[:, a : a + 1], (levels, LANES))
                for field in range(3):
                    lowest_scratch[field * entries + entry : field * entries + entry + 1, :] = made[
                        field * 16 : field * 16 + 1, :
                    ]
                    highest_scratch[field * entries + entry : field * entries + entry + 1, :] = made[
                        field * 16 + 15 : field * 16 + 16, :
                    ]
    lowest[...] = lowest_scratch[...].astype(jnp.bfloat16)
    highest[...] = highest_scratch[...].astype(jnp.bfloat16)


def horizontal_kernel(stencil, blocks, hweight, horizontal):
    rows = horizontal.shape[0]
    together = 32

    def some_rows(i, carry):
        for k in range(together):
            a = i * together + k
            total = None
            for q in range(4):
                term = hweight[a, q : q + 1, :] * blocks[stencil[q, a]]
                total = term if total is None else total + term
            horizontal[a] = total
        return carry

    lax.fori_loop(0, rows // together, some_rows, 0)


def vertical_kernel(stencil, at_top, horizontal, highest, above, hweight, spread, arrival, made, over_rows, wide, out_sem):
    rows, fields, levels, _ = made.shape
    entries = wide.shape[0]
    top = at_top[0] == 1
    over_rows[...] = jnp.where(top, highest[...].astype(jnp.float32), above[...].astype(jnp.float32))
    together = 8

    def widen(i, carry):
        for k in range(together):
            entry = i * together + k
            for field in range(fields):
                wide[entry, 7 - field : 8 - field, :] = over_rows[pl.ds(field * entries + entry, 1), :]
        return carry

    lax.fori_loop(0, entries // together, widen, 0)

    row = lax.broadcasted_iota(jnp.int32, (8, LANES), 0)
    piece = 32
    pieces = rows // piece

    def send(i):
        at = pl.multiple_of(i * piece, piece)
        return pltpu.make_async_copy(made.at[pl.ds(at, piece)], arrival.at[pl.ds(at, piece)], out_sem.at[i])

    def some_rows(i, carry):
        for k in range(piece):
            a = i * piece + k
            last = None
            for q in range(4):
                term = hweight[a, q : q + 1, :] * wide[stencil[q, a]]
                last = term if last is None else last + term
            for field in range(fields):
                parts = []
                over = last if field == 0 else pltpu.roll(last, field, 0)
                for part in reversed(range(levels // 8)):
                    here = horizontal[a, field * levels + part * 8 : field * levels + (part + 1) * 8, :]
                    turned = pltpu.roll(here, 7, 0)
                    up = jnp.where(row == 7, over, turned)
                    parts.insert(0, here + spread[a, part * 8 : (part + 1) * 8, :] * (up - here))
                    over = turned
                made[a, field] = jnp.concatenate(parts, axis=0).astype(jnp.bfloat16)
        send(i).start()
        return carry

    lax.fori_loop(0, pieces, some_rows, 0)
    for i in range(pieces):
        send(i).wait()


def whole(memory):
    return pl.BlockSpec(memory_space=memory)


def per_device(fourier, gauss, legendre, owner, send_list, stencil, hweight, vweight):
    lat_count = lax.axis_size("lat")
    device_row = lax.axis_index("lat")
    lat_dev, fields, levels, columns = fourier.shape
    wave_total = columns // 2
    slot_most = legendre.shape[1]
    degrees = legendre.shape[3]
    latitudes = legendre.shape[2]
    slot_count = lat_count * slot_most
    capacity = send_list.shape[2]
    arrivals = stencil.shape[0]
    half = fields * levels
    per_slot = 2 * half
    message_lanes = slot_most * per_slot
    tiles = message_lanes // LANES
    entries = lat_count * capacity

    owners = owner[:, 0]
    wave_index = jnp.arange(wave_total, dtype=jnp.int32)
    earlier = (owners[:, None] == owners[None, :]) & (wave_index[:, None] < wave_index[None, :])
    slot_rank = jnp.sum(earlier.astype(jnp.int32), axis=0)
    slot_of = owners * slot_most + slot_rank
    wave_number = wave_index * (degrees // wave_total)
    vmem = whole(pltpu.VMEM)
    smem = whole(pltpu.SMEM)
    hbm = whole(pl.ANY)
    message_one = pl.pallas_call(
        pack_kernel,
        out_shape=jax.ShapeDtypeStruct((lat_count, tiles * lat_dev + 8, LANES), jnp.bfloat16),
        in_specs=[hbm, hbm, hbm, hbm],
        out_specs=hbm,
        scratch_shapes=[
            pltpu.VMEM((1, wave_total), jnp.int32),
            pltpu.VMEM((capacity, lat_count), jnp.int32),
            pltpu.VMEM((1, lat_dev), jnp.float32),
            pltpu.VMEM(fourier.shape, jnp.bfloat16),
            pltpu.VMEM((lat_count, tiles * lat_dev + 8, LANES), jnp.bfloat16),
            pltpu.VMEM((tiles, lat_count * lat_dev, LANES), jnp.float32),
            pltpu.VMEM((lat_dev, columns), jnp.float32),
            pltpu.SemaphoreType.DMA((lat_dev // 8 + 3,)),
            pltpu.SemaphoreType.DMA((lat_count // 8,)),
        ],
        compiler_params=pltpu.CompilerParams(vmem_limit_bytes=GRANT),
        name="pack",
    )(owner.reshape(1, wave_total), send_list[0].T, gauss.reshape(1, lat_dev), fourier)
    arrived = lax.all_to_all(message_one, "lat", split_axis=0, concat_axis=0, tiled=True)

    placed = (slot_of[:, None] == jnp.arange(slot_count, dtype=jnp.int32)[None, :]).astype(jnp.int32)
    owned = lax.dynamic_slice_in_dim(placed, device_row * slot_most, slot_most, 1)
    filled = jnp.sum(owned, axis=0) > 0
    slot_wave = jnp.sum(owned * wave_number[:, None], axis=0)
    degree_index = jnp.arange(degrees, dtype=jnp.int32)
    keep_mask = (filled[:, None] & (degree_index[None, :] >= slot_wave[:, None])).astype(jnp.float32)
    damping = keep_mask * damping_curve(degrees)[None, :]

    message_shape = (lat_count, entries // 8 * slot_most * 2, 8 * half)
    first_table, room = pl.pallas_call(
        fetch_kernel,
        out_shape=[
            jax.ShapeDtypeStruct(legendre.shape[2:], legendre.dtype),
            jax.ShapeDtypeStruct(message_shape, jnp.bfloat16),
        ],
        in_specs=[hbm],
        out_specs=[vmem, hbm],
        scratch_shapes=[pltpu.SemaphoreType.DMA],
        compiler_params=pltpu.CompilerParams(vmem_limit_bytes=48 * 2**20),
        cost_estimate=pl.CostEstimate(flops=0, bytes_accessed=legendre.size, transcendentals=0),
        name="fetch",
    )(legendre[0])
    spectral_rows, message_two = pl.pallas_call(
        spectral_kernel,
        in_specs=[vmem, vmem, hbm, vmem, hbm],
        out_specs=[vmem, hbm],
        input_output_aliases={4: 1},
        scratch_shapes=[
            pltpu.VMEM((slot_most - 1, latitudes, degrees), jnp.bfloat16),
            pltpu.VMEM(message_shape, jnp.bfloat16),
            pltpu.VMEM((message_lanes, latitudes), jnp.bfloat16),
            pltpu.VMEM((latitudes * 2 * slot_most, LANES), jnp.float32),
            pltpu.VMEM((lat_count, LANES), jnp.int32),
            pltpu.SMEM((lat_count, LANES), jnp.int32),
            pltpu.SemaphoreType.DMA,
            pltpu.SemaphoreType.DMA((slot_most - 1,)),
            pltpu.SemaphoreType.DMA((lat_count // 4,)),
        ],
        out_shape=[
            jax.ShapeDtypeStruct((slot_most, per_slot, degrees), jnp.bfloat16),
            jax.ShapeDtypeStruct(message_shape, jnp.bfloat16),
        ],
        compiler_params=pltpu.CompilerParams(vmem_limit_bytes=48 * 2**20),
        name="spectral",
    )(arrived, first_table, legendre[0], damping, room)
    received = lax.all_to_all(message_two, "lat", split_axis=0, concat_axis=0, tiled=True)

    spectral = jnp.transpose(
        spectral_rows.reshape(slot_most, fields, 2, levels, degrees), (0, 1, 3, 2, 4)
    )
    slot_waves = jnp.sum(placed * wave_number[:, None], axis=0)
    slot_waves, spectral = lax.optimization_barrier((slot_waves, spectral))
    present = (jnp.sum(placed, axis=0) > 0).astype(jnp.float32)
    points = jnp.arange(NLON, dtype=jnp.int32).reshape(BLOCKS_X, 1, 1, BLK)
    phases = slot_waves[None, :, None, None] * points % NLON
    angles = phases.astype(jnp.float32) * (2.0 * math.pi / NLON)
    norm_factor = present[None, :, None, None] / math.sqrt(wave_total)
    zonal = jnp.concatenate([jnp.cos(angles) * norm_factor, -jnp.sin(angles) * norm_factor], axis=2)
    zonal = zonal.astype(jnp.bfloat16).reshape(BLOCKS_X, slot_count * 2, BLK)
    all_columns = arrived[:, tiles * lat_dev, entries:].reshape(lat_count, capacity, lat_count)
    column_of = lax.dynamic_index_in_dim(all_columns, device_row, 2, keepdims=False)
    column_of = column_of.astype(jnp.int32).reshape(-1)
    lev_count = lax.axis_size("lev")
    at_top = (lax.axis_index("lev") == lev_count - 1).astype(jnp.int32).reshape(1)
    vertical = vweight.T
    corners = stencil.T
    received, vertical, corners, at_top = lax.optimization_barrier((received, vertical, corners, at_top))
    blocks, lowest, highest, spread = pl.pallas_call(
        block_kernel,
        out_shape=[
            jax.ShapeDtypeStruct((entries, half, BLK), jnp.float32),
            jax.ShapeDtypeStruct((fields * entries, BLK), jnp.bfloat16),
            jax.ShapeDtypeStruct((fields * entries, BLK), jnp.bfloat16),
            jax.ShapeDtypeStruct((arrivals, levels, BLK), jnp.float32),
        ],
        in_specs=[smem, vmem, vmem, vmem],
        out_specs=[vmem, vmem, vmem, vmem],
        scratch_shapes=[pltpu.VMEM((fields * entries, BLK), jnp.float32)] * 2,
        compiler_params=pltpu.CompilerParams(vmem_limit_bytes=16 * 2**20),
        name="blocks",
    )(column_of, received, zonal, vertical)

    above = lax.ppermute(lowest, "lev", [(i, i - 1) for i in range(1, lev_count)])
    horizontal = pl.pallas_call(
        horizontal_kernel,
        out_shape=jax.ShapeDtypeStruct((arrivals, half, BLK), jnp.float32),
        in_specs=[smem, vmem, vmem],
        out_specs=vmem,
        compiler_params=pltpu.CompilerParams(vmem_limit_bytes=16 * 2**20),
        cost_estimate=pl.CostEstimate(
            flops=8 * arrivals * half * BLK, bytes_accessed=4 * arrivals * half * BLK, transcendentals=0
        ),
        name="horizontal",
    )(corners, blocks, hweight)
    arrival = pl.pallas_call(
        vertical_kernel,
        out_shape=jax.ShapeDtypeStruct((arrivals, fields, levels, BLK), jnp.bfloat16),
        in_specs=[smem, smem, vmem, vmem, vmem, vmem, vmem],
        out_specs=hbm,
        scratch_shapes=[
            pltpu.VMEM((arrivals, fields, levels, BLK), jnp.bfloat16),
            pltpu.VMEM((fields * entries, BLK), jnp.float32),
            pltpu.VMEM((entries, 8, BLK), jnp.float32),
            pltpu.SemaphoreType.DMA((arrivals // 32,)),
        ],
        compiler_params=pltpu.CompilerParams(vmem_limit_bytes=16 * 2**20),
        name="vertical",
    )(corners, at_top, horizontal, highest, above, hweight, spread)
    return (spectral[None], arrival)


def solution(mesh):
    return jax.shard_map(
        per_device,
        mesh=mesh,
        in_specs=(
            P("lat", None, "lev", None),
            P("lat"),
            P("lat", None, None, None),
            P(),
            P("lat", None, None),
            P("lat", None),
            P("lat", None, None),
            P("lat", "lev"),
        ),
        out_specs=(P("lat", None, None, "lev", None, None), P("lat", None, "lev", None)),
        check_vma=False,
    )
```

```python
import math

import jax
import jax.numpy as jnp
from jax import lax
from jax.experimental import pallas as pl
from jax.experimental.pallas import tpu as pltpu
from jax.sharding import PartitionSpec as P

NLON = 2560
BLK = 128
BLOCKS_X = NLON // BLK
LANES = 128
GRANT = 56 * 2**20

diffusion = 3.0

NT = (((1,), (1,)), ((), ()))
NN = (((1,), (0,)), ((), ()))


def mxu(left, right, dims):
    return lax.dot_general(left, right, dims, preferred_element_type=jnp.float32)


def identity(size):
    rows = lax.broadcasted_iota(jnp.int32, (size, size), 0)
    columns = lax.broadcasted_iota(jnp.int32, (size, size), 1)
    return (rows == columns).astype(jnp.float32).astype(jnp.bfloat16)


def damping_curve(degrees):
    order_n = jnp.arange(degrees, dtype=jnp.float32)
    ratio = order_n * (order_n + 1.0) / float(degrees * (degrees - 1))
    return 1.0 / (1.0 + diffusion * ratio * ratio)


def pack_kernel(
    owner_in, ids_in, gauss_in, fourier_in, message, owner, send_ids, gauss, fourier, packed, scratch, weight, in_sem, out_sem
):
    lat_dev, fields, levels, columns = fourier.shape
    owners = packed.shape[0]
    tiles = scratch.shape[0]
    slots = (tiles * LANES) // (2 * fields * levels)
    chunk = 8
    pieces = lat_dev // chunk
    small = [
        pltpu.make_async_copy(source, target, in_sem.at[pieces + i])
        for i, (source, target) in enumerate(((owner_in, owner), (ids_in, send_ids), (gauss_in, gauss)))
    ]
    large = [
        pltpu.make_async_copy(
            fourier_in.at[pl.ds(i * chunk, chunk)], fourier.at[pl.ds(i * chunk, chunk)], in_sem.at[i]
        )
        for i in range(pieces)
    ]
    for copy in small + large:
        copy.start()
    for copy in small:
        copy.wait()

    waves = owner.shape[1]
    wave_at = lax.broadcasted_iota(jnp.int32, (waves, columns), 0)
    column = lax.broadcasted_iota(jnp.int32, (waves, columns), 1)
    square_row = lax.broadcasted_iota(jnp.int32, (waves, waves), 0)
    square_column = lax.broadcasted_iota(jnp.int32, (waves, waves), 1)
    listed = jnp.broadcast_to(owner[...], (waves, waves))
    upright = jnp.sum(jnp.where(square_row == square_column, listed, 0), axis=1, keepdims=True)
    upright = jnp.broadcast_to(upright, (waves, columns))
    column_owner = jnp.sum(jnp.where(wave_at == column // 2, upright, 0), axis=0, keepdims=True)
    earlier = (upright == jnp.broadcast_to(column_owner, (waves, columns))) & (wave_at < column // 2)
    column_rank = jnp.sum(jnp.where(earlier, 1, 0), axis=0, keepdims=True)
    owner_at = lax.broadcasted_iota(jnp.int32, (owners, columns), 0)
    chooser = jnp.where(owner_at == column_owner, 1.0, 0.0).astype(jnp.bfloat16)
    part_of = 2 * column_rank + lax.broadcasted_iota(jnp.int32, (1, columns), 1) % 2
    masks = [
        jnp.broadcast_to(jnp.where(part_of == i, 1.0, 0.0), (levels, columns)).astype(jnp.bfloat16)
        for i in range(2 * slots)
    ]
    turn_row = lax.broadcasted_iota(jnp.int32, (lat_dev, lat_dev), 0)
    turn_column = lax.broadcasted_iota(jnp.int32, (lat_dev, lat_dev), 1)
    weights = jnp.where(turn_row == turn_column, jnp.broadcast_to(gauss[...], (lat_dev, lat_dev)), 0.0)
    weight[...] = jnp.broadcast_to(jnp.sum(weights, axis=1, keepdims=True), weight.shape)

    none = jnp.zeros_like(chooser)
    chooser = jnp.concatenate(
        [jnp.concatenate([chooser, none], axis=1), jnp.concatenate([none, chooser], axis=1)], axis=0
    )
    for pair in range(0, lat_dev, 2):
        if pair % chunk == 0:
            large[pair // chunk].wait()
        spread = []
        for t in range(pair, pair + 2):
            rows = fourier[t].reshape(fields * levels, columns).astype(jnp.float32)
            rows = (rows * weight[t : t + 1, :]).astype(jnp.bfloat16)
            parts = []
            for slot in range(slots):
                for field in range(fields):
                    for part in range(2):
                        parts.append(rows[field * levels : (field + 1) * levels] * masks[2 * slot + part])
            spread.append(jnp.concatenate(parts, axis=0))
        chosen = mxu(chooser, jnp.concatenate(spread, axis=1), NT)
        for side in range(2):
            for tile in range(tiles):
                scratch[tile, pl.ds(pair + side, owners, stride=lat_dev), :] = chosen[
                    side * owners : (side + 1) * owners, tile * LANES : (tile + 1) * LANES
                ]

    ids = send_ids[...].astype(jnp.float32)
    in_row = jnp.floor((ids + 0.5) * (1.0 / BLOCKS_X))
    in_column = ids - in_row * BLOCKS_X
    sides = [in_row[k : k + 1] for k in range(ids.shape[0])] + [in_column[k : k + 1] for k in range(ids.shape[0])]
    extra = jnp.broadcast_to(jnp.concatenate(sides, axis=1), (8, LANES))
    group = 8

    def send(g):
        first = pl.multiple_of(g * group, group)
        return pltpu.make_async_copy(packed.at[pl.ds(first, group)], message.at[pl.ds(first, group)], out_sem.at[g])

    def finish(g, carry):
        for k in range(group):
            o = g * group + k
            parts = [scratch[tile, pl.ds(pl.multiple_of(o * lat_dev, 8), lat_dev), :] for tile in range(tiles)]
            packed[o] = jnp.concatenate(parts + [extra], axis=0).astype(jnp.bfloat16)
        send(g).start()
        return carry

    lax.fori_loop(0, owners // group, finish, 0)
    for g in range(owners // group):
        send(g).wait()


def spectral_kernel(
    arrived, tables_in, damping, spectral, message, tables, made, turned, rows_at, listed, row_of, listed_sem, in_sem, out_sem
):
    slots, per_slot, degrees = spectral.shape
    latitudes = tables.shape[1]

    def fetch(slot):
        return pltpu.make_async_copy(tables_in.at[slot], tables.at[slot], in_sem.at[slot])

    def fetch_one(slot, carry):
        fetch(slot).start()
        return carry

    lax.fori_loop(0, slots, fetch_one, 0)
    half = per_slot // 2
    field_rows = half // 3
    bands = arrived.shape[0]
    tiles = turned.shape[0] // LANES
    lat_dev = (arrived.shape[1] - 8) // tiles
    receivers, message_rows, message_lanes = message.shape
    lists = pltpu.make_async_copy(listed, row_of, listed_sem)

    wide = arrived[...].astype(jnp.float32)
    unit = identity(LANES)
    band = lax.broadcasted_iota(jnp.int32, listed.shape, 1)
    rows = wide[:, tiles * lat_dev, :].astype(jnp.bfloat16)
    rows = jnp.concatenate([rows, jnp.zeros((LANES - bands, LANES), jnp.bfloat16)], axis=0)
    rows = mxu(unit[: listed.shape[0]], rows, NT).astype(jnp.int32)
    listed[...] = (rows + jnp.where(band < bands, band, 0) * lat_dev) * 8
    lists.start()
    for tile in range(tiles):
        columns = wide[:, tile * lat_dev : (tile + 1) * lat_dev, :].reshape(latitudes, LANES)
        turned[tile * LANES : (tile + 1) * LANES, :] = mxu(unit, columns.astype(jnp.bfloat16), NT).astype(jnp.bfloat16)

    gap = jnp.zeros((LANES - half, degrees), jnp.bfloat16)
    chunk = 256

    def one_slot(slot, carry):
        fetch(slot).wait()
        own = turned[pl.ds(pl.multiple_of(slot * per_slot, 32), per_slot), :]
        spectra = mxu(own, tables[slot], NN)
        damped = (spectra * damping[pl.ds(slot, 1), :]).astype(jnp.bfloat16)
        spectral[slot] = damped
        sides = []
        for part in range(2):
            for field in range(3):
                at = (2 * field + part) * field_rows
                sides.append(damped[at : at + field_rows])
            sides.append(gap)
        sides = jnp.concatenate(sides, axis=0)
        for at in range(0, latitudes, chunk):
            back = mxu(tables[slot, at : at + chunk, :], sides, NT)
            for part in range(2):
                rows_at[pl.ds(at * 2 * slots + slot * 2 + part, chunk, stride=2 * slots), :] = back[
                    :, part * LANES : (part + 1) * LANES
                ]
        return carry

    lax.fori_loop(0, slots, one_slot, 0)

    lists.wait()
    lane = lax.broadcasted_iota(jnp.int32, (8, LANES), 1)
    wide_tiles = message_lanes // LANES

    group = 4
    groups = receivers // group

    def send(g):
        at = pl.multiple_of(g * group, group)
        return pltpu.make_async_copy(made.at[pl.ds(at, group)], message.at[pl.ds(at, group)], out_sem.at[g])

    def one_group(g, carry):
        for k in range(group):
            r = g * group + k
            for pair in range(message_rows // 16):
                halves = []
                for side in range(2):
                    built = [None] * wide_tiles
                    for e in range(8):
                        entry = (pair * 2 + side) * 8 + e
                        at = pl.multiple_of(row_of[receivers * (entry % 2) + r, entry // 2], 8)
                        row = rows_at[pl.ds(at, 8), :]
                        start = e * half
                        if start % LANES:
                            row = pltpu.roll(row, start % LANES, 1)
                        for tile in range(start // LANES, (start + half - 1) // LANES + 1):
                            first = start - tile * LANES
                            if built[tile] is None:
                                built[tile] = row
                            else:
                                built[tile] = jnp.where(lane >= first, row, built[tile])
                    halves.append(jnp.concatenate(built, axis=1))
                both = jnp.concatenate(halves, axis=0).astype(jnp.bfloat16)
                made[r, pair * 16 : (pair + 1) * 16, :] = both
        send(g).start()
        return carry

    lax.fori_loop(0, groups, one_group, 0)
    for g in range(groups):
        send(g).wait()


def block_kernel(
    column_of, received, zonal, vweight, blocks, lowest, highest, spread, lowest_scratch, highest_scratch
):
    owners, message_rows, message_lanes = received.shape
    unit = identity(LANES)
    half = message_lanes // 8
    groups = message_rows // 8
    entries = blocks.shape[0]
    rows, levels, _ = spread.shape
    per_entry = rows // entries
    for pair in range(groups // 2):
        wide = received[:, pair * 16 : (pair + 1) * 16, :].astype(jnp.float32)
        for side in range(2):
            group = pair * 2 + side
            own = wide[:, side * 8 : (side + 1) * 8, :].reshape(owners * 8, message_lanes).astype(jnp.bfloat16)
            turned = [
                mxu(unit, own[:, tile * LANES : (tile + 1) * LANES], NT).astype(jnp.bfloat16)
                for tile in range(message_lanes // LANES)
            ]
            turned = jnp.concatenate(turned, axis=0)
            for e in range(8):
                entry = group * 8 + e
                made = mxu(turned[e * half : (e + 1) * half], zonal[column_of[entry]], NN)
                made = made.astype(jnp.bfloat16).astype(jnp.float32)
                blocks[entry] = made
                for a in range(entry * per_entry, (entry + 1) * per_entry):
                    spread[a] = jnp.broadcast_to(vweight[:, a : a + 1], (levels, LANES))
                for field in range(3):
                    lowest_scratch[field * entries + entry : field * entries + entry + 1, :] = made[
                        field * 16 : field * 16 + 1, :
                    ]
                    highest_scratch[field * entries + entry : field * entries + entry + 1, :] = made[
                        field * 16 + 15 : field * 16 + 16, :
                    ]
    lowest[...] = lowest_scratch[...].astype(jnp.bfloat16)
    highest[...] = highest_scratch[...].astype(jnp.bfloat16)


def horizontal_kernel(stencil, blocks, hweight, horizontal):
    rows = horizontal.shape[0]
    together = stencil.shape[1] // 4

    def some_rows(i, carry):
        for k in range(together):
            a = i * together + k
            total = None
            for q in range(4):
                term = hweight[a, q : q + 1, :] * blocks[stencil[i, k * 4 + q]]
                total = term if total is None else total + term
            horizontal[a] = total
        return carry

    lax.fori_loop(0, rows // together, some_rows, 0)


def vertical_kernel(stencil, at_top, horizontal, highest, above, hweight, spread, arrival, made, over_rows, wide, out_sem):
    rows, fields, levels, _ = made.shape
    entries = wide.shape[0]
    top = at_top[0] == 1
    over_rows[...] = jnp.where(top, highest[...].astype(jnp.float32), above[...].astype(jnp.float32))
    together = 8

    def widen(i, carry):
        for k in range(together):
            entry = i * together + k
            for field in range(fields):
                wide[entry, 7 - field : 8 - field, :] = over_rows[pl.ds(field * entries + entry, 1), :]
        return carry

    lax.fori_loop(0, entries // together, widen, 0)

    row = lax.broadcasted_iota(jnp.int32, (8, LANES), 0)
    piece = stencil.shape[1] // 4
    pieces = rows // piece

    def send(i):
        at = pl.multiple_of(i * piece, piece)
        return pltpu.make_async_copy(made.at[pl.ds(at, piece)], arrival.at[pl.ds(at, piece)], out_sem.at[i])

    def some_rows(i, carry):
        for k in range(piece):
            a = i * piece + k
            last = None
            for q in range(4):
                term = hweight[a, q : q + 1, :] * wide[stencil[i, k * 4 + q]]
                last = term if last is None else last + term
            for field in range(fields):
                parts = []
                over = last if field == 0 else pltpu.roll(last, field, 0)
                for part in reversed(range(levels // 8)):
                    here = horizontal[a, field * levels + part * 8 : field * levels + (part + 1) * 8, :]
                    turned = pltpu.roll(here, 7, 0)
                    up = jnp.where(row == 7, over, turned)
                    parts.insert(0, here + spread[a, part * 8 : (part + 1) * 8, :] * (up - here))
                    over = turned
                made[a, field] = jnp.concatenate(parts, axis=0).astype(jnp.bfloat16)
        send(i).start()
        return carry

    lax.fori_loop(0, pieces, some_rows, 0)
    for i in range(pieces):
        send(i).wait()


def whole(memory):
    return pl.BlockSpec(memory_space=memory)


def per_device(fourier, gauss, legendre, owner, send_list, stencil, hweight, vweight):
    lat_count = lax.axis_size("lat")
    device_row = lax.axis_index("lat")
    lat_dev, fields, levels, columns = fourier.shape
    wave_total = columns // 2
    slot_most = legendre.shape[1]
    degrees = legendre.shape[3]
    latitudes = legendre.shape[2]
    slot_count = lat_count * slot_most
    capacity = send_list.shape[2]
    arrivals = stencil.shape[0]
    half = fields * levels
    per_slot = 2 * half
    message_lanes = slot_most * per_slot
    tiles = message_lanes // LANES
    entries = lat_count * capacity

    owners = owner[:, 0]
    wave_index = jnp.arange(wave_total, dtype=jnp.int32)
    earlier = (owners[:, None] == owners[None, :]) & (wave_index[:, None] < wave_index[None, :])
    slot_rank = jnp.sum(earlier.astype(jnp.int32), axis=0)
    slot_of = owners * slot_most + slot_rank
    wave_number = wave_index * (degrees // wave_total)
    vmem = whole(pltpu.VMEM)
    smem = whole(pltpu.SMEM)
    hbm = whole(pl.ANY)
    message_one = pl.pallas_call(
        pack_kernel,
        out_shape=jax.ShapeDtypeStruct((lat_count, tiles * lat_dev + 8, LANES), jnp.bfloat16),
        in_specs=[hbm, hbm, hbm, hbm],
        out_specs=hbm,
        scratch_shapes=[
            pltpu.VMEM((1, wave_total), jnp.int32),
            pltpu.VMEM((capacity, lat_count), jnp.int32),
            pltpu.VMEM((1, lat_dev), jnp.float32),
            pltpu.VMEM(fourier.shape, jnp.bfloat16),
            pltpu.VMEM((lat_count, tiles * lat_dev + 8, LANES), jnp.bfloat16),
            pltpu.VMEM((tiles, lat_count * lat_dev, LANES), jnp.float32),
            pltpu.VMEM((lat_dev, columns), jnp.float32),
            pltpu.SemaphoreType.DMA((lat_dev // 8 + 3,)),
            pltpu.SemaphoreType.DMA((lat_count // 8,)),
        ],
        compiler_params=pltpu.CompilerParams(vmem_limit_bytes=GRANT),
        name="pack",
    )(owner.reshape(1, wave_total), send_list[0].T, gauss.reshape(1, lat_dev), fourier)
    arrived = lax.all_to_all(message_one, "lat", split_axis=0, concat_axis=0, tiled=True)

    placed = (slot_of[:, None] == jnp.arange(slot_count, dtype=jnp.int32)[None, :]).astype(jnp.int32)
    owned = lax.dynamic_slice_in_dim(placed, device_row * slot_most, slot_most, 1)
    filled = jnp.sum(owned, axis=0) > 0
    slot_wave = jnp.sum(owned * wave_number[:, None], axis=0)
    degree_index = jnp.arange(degrees, dtype=jnp.int32)
    keep_mask = (filled[:, None] & (degree_index[None, :] >= slot_wave[:, None])).astype(jnp.float32)
    damping = keep_mask * damping_curve(degrees)[None, :]

    message_shape = (lat_count, entries // 8 * slot_most * 2, 8 * half)
    spectral_rows, message_two = pl.pallas_call(
        spectral_kernel,
        in_specs=[vmem, hbm, vmem],
        out_specs=[vmem, hbm],
        scratch_shapes=[
            pltpu.VMEM((slot_most, latitudes, degrees), jnp.bfloat16),
            pltpu.VMEM(message_shape, jnp.bfloat16),
            pltpu.VMEM((message_lanes, latitudes), jnp.bfloat16),
            pltpu.VMEM((latitudes * 2 * slot_most, LANES), jnp.float32),
            pltpu.VMEM((entries, LANES), jnp.int32),
            pltpu.SMEM((entries, LANES), jnp.int32),
            pltpu.SemaphoreType.DMA,
            pltpu.SemaphoreType.DMA((slot_most,)),
            pltpu.SemaphoreType.DMA((lat_count // 4,)),
        ],
        out_shape=[
            jax.ShapeDtypeStruct((slot_most, per_slot, degrees), jnp.bfloat16),
            jax.ShapeDtypeStruct(message_shape, jnp.bfloat16),
        ],
        compiler_params=pltpu.CompilerParams(vmem_limit_bytes=52 * 2**20),
        name="spectral",
    )(arrived, legendre[0], damping)
    received = lax.all_to_all(message_two, "lat", split_axis=0, concat_axis=0, tiled=True)

    spectral = jnp.transpose(
        spectral_rows.reshape(slot_most, fields, 2, levels, degrees), (0, 1, 3, 2, 4)
    )
    slot_waves = jnp.sum(placed * wave_number[:, None], axis=0)
    slot_waves, spectral = lax.optimization_barrier((slot_waves, spectral))
    present = (jnp.sum(placed, axis=0) > 0).astype(jnp.float32)
    points = jnp.arange(NLON, dtype=jnp.int32).reshape(BLOCKS_X, 1, 1, BLK)
    phases = slot_waves[None, :, None, None] * points % NLON
    angles = phases.astype(jnp.float32) * (2.0 * math.pi / NLON)
    norm_factor = present[None, :, None, None] / math.sqrt(wave_total)
    zonal = jnp.concatenate([jnp.cos(angles) * norm_factor, -jnp.sin(angles) * norm_factor], axis=2)
    zonal = zonal.astype(jnp.bfloat16).reshape(BLOCKS_X, slot_count * 2, BLK)
    all_columns = arrived[:, tiles * lat_dev, entries:].reshape(lat_count, capacity, lat_count)
    column_of = lax.dynamic_index_in_dim(all_columns, device_row, 2, keepdims=False)
    column_of = column_of.astype(jnp.int32).reshape(-1)
    lev_count = lax.axis_size("lev")
    at_top = (lax.axis_index("lev") == lev_count - 1).astype(jnp.int32).reshape(1)
    vertical = vweight.T
    corners = stencil.reshape(arrivals // 32, 128)
    received, vertical, corners, at_top = lax.optimization_barrier((received, vertical, corners, at_top))
    blocks, lowest, highest, spread = pl.pallas_call(
        block_kernel,
        out_shape=[
            jax.ShapeDtypeStruct((entries, half, BLK), jnp.float32),
            jax.ShapeDtypeStruct((fields * entries, BLK), jnp.bfloat16),
            jax.ShapeDtypeStruct((fields * entries, BLK), jnp.bfloat16),
            jax.ShapeDtypeStruct((arrivals, levels, BLK), jnp.float32),
        ],
        in_specs=[smem, vmem, vmem, vmem],
        out_specs=[vmem, vmem, vmem, vmem],
        scratch_shapes=[pltpu.VMEM((fields * entries, BLK), jnp.float32)] * 2,
        compiler_params=pltpu.CompilerParams(vmem_limit_bytes=16 * 2**20),
        name="blocks",
    )(column_of, received, zonal, vertical)

    above = lax.ppermute(lowest, "lev", [(i, i - 1) for i in range(1, lev_count)])
    horizontal = pl.pallas_call(
        horizontal_kernel,
        out_shape=jax.ShapeDtypeStruct((arrivals, half, BLK), jnp.float32),
        in_specs=[smem, vmem, vmem],
        out_specs=vmem,
        compiler_params=pltpu.CompilerParams(vmem_limit_bytes=16 * 2**20),
        cost_estimate=pl.CostEstimate(
            flops=8 * arrivals * half * BLK, bytes_accessed=4 * arrivals * half * BLK, transcendentals=0
        ),
        name="horizontal",
    )(corners, blocks, hweight)
    arrival = pl.pallas_call(
        vertical_kernel,
        out_shape=jax.ShapeDtypeStruct((arrivals, fields, levels, BLK), jnp.bfloat16),
        in_specs=[smem, smem, vmem, vmem, vmem, vmem, vmem],
        out_specs=hbm,
        scratch_shapes=[
            pltpu.VMEM((arrivals, fields, levels, BLK), jnp.bfloat16),
            pltpu.VMEM((fields * entries, BLK), jnp.float32),
            pltpu.VMEM((entries, 8, BLK), jnp.float32),
            pltpu.SemaphoreType.DMA((arrivals // 32,)),
        ],
        compiler_params=pltpu.CompilerParams(vmem_limit_bytes=16 * 2**20),
        name="vertical",
    )(corners, at_top, horizontal, highest, above, hweight, spread)
    return (spectral[None], arrival)


def solution(mesh):
    return jax.shard_map(
        per_device,
        mesh=mesh,
        in_specs=(
            P("lat", None, "lev", None),
            P("lat"),
            P("lat", None, None, None),
            P(),
            P("lat", None, None),
            P("lat", None),
            P("lat", None, None),
            P("lat", "lev"),
        ),
        out_specs=(P("lat", None, None, "lev", None, None), P("lat", None, "lev", None)),
        check_vma=False,
    )
```

```python
import functools
import math

import jax
import jax.numpy as jnp
from jax import lax
from jax.experimental import pallas as pl
from jax.experimental.pallas import tpu as pltpu
from jax.sharding import PartitionSpec as P

NLON = 2560
BLK = 128
BLOCKS_X = NLON // BLK
LANES = 128
GRANT = 56 * 2**20

diffusion = 3.0

NT = (((1,), (1,)), ((), ()))
NN = (((1,), (0,)), ((), ()))


def mxu(left, right, dims):
    return lax.dot_general(left, right, dims, preferred_element_type=jnp.float32)


def identity(size):
    rows = lax.broadcasted_iota(jnp.int32, (size, size), 0)
    columns = lax.broadcasted_iota(jnp.int32, (size, size), 1)
    return (rows == columns).astype(jnp.float32).astype(jnp.bfloat16)


def damping_curve(degrees):
    order_n = jnp.arange(degrees, dtype=jnp.float32)
    ratio = order_n * (order_n + 1.0) / float(degrees * (degrees - 1))
    return 1.0 / (1.0 + diffusion * ratio * ratio)


def pack_kernel(
    owner_in, ids_in, gauss_in, fourier_in, message, owner, send_ids, gauss, fourier, packed, scratch, weight, in_sem, out_sem
):
    lat_dev, fields, levels, columns = fourier.shape
    owners = packed.shape[0]
    tiles = scratch.shape[0]
    slots = (tiles * LANES) // (2 * fields * levels)
    chunk = 8
    pieces = lat_dev // chunk
    small = [
        pltpu.make_async_copy(source, target, in_sem.at[pieces + i])
        for i, (source, target) in enumerate(((owner_in, owner), (ids_in, send_ids), (gauss_in, gauss)))
    ]
    large = [
        pltpu.make_async_copy(
            fourier_in.at[pl.ds(i * chunk, chunk)], fourier.at[pl.ds(i * chunk, chunk)], in_sem.at[i]
        )
        for i in range(pieces)
    ]
    for copy in small + large:
        copy.start()
    for copy in small:
        copy.wait()

    waves = owner.shape[1]
    wave_at = lax.broadcasted_iota(jnp.int32, (waves, columns), 0)
    column = lax.broadcasted_iota(jnp.int32, (waves, columns), 1)
    square_row = lax.broadcasted_iota(jnp.int32, (waves, waves), 0)
    square_column = lax.broadcasted_iota(jnp.int32, (waves, waves), 1)
    listed = jnp.broadcast_to(owner[...], (waves, waves))
    upright = jnp.sum(jnp.where(square_row == square_column, listed, 0), axis=1, keepdims=True)
    upright = jnp.broadcast_to(upright, (waves, columns))
    column_owner = jnp.sum(jnp.where(wave_at == column // 2, upright, 0), axis=0, keepdims=True)
    earlier = (upright == jnp.broadcast_to(column_owner, (waves, columns))) & (wave_at < column // 2)
    column_rank = jnp.sum(jnp.where(earlier, 1, 0), axis=0, keepdims=True)
    owner_at = lax.broadcasted_iota(jnp.int32, (owners, columns), 0)
    chooser = jnp.where(owner_at == column_owner, 1.0, 0.0).astype(jnp.bfloat16)
    part_of = 2 * column_rank + lax.broadcasted_iota(jnp.int32, (1, columns), 1) % 2
    masks = [
        jnp.broadcast_to(jnp.where(part_of == i, 1.0, 0.0), (levels, columns)).astype(jnp.bfloat16)
        for i in range(2 * slots)
    ]
    turn_row = lax.broadcasted_iota(jnp.int32, (lat_dev, lat_dev), 0)
    turn_column = lax.broadcasted_iota(jnp.int32, (lat_dev, lat_dev), 1)
    weights = jnp.where(turn_row == turn_column, jnp.broadcast_to(gauss[...], (lat_dev, lat_dev)), 0.0)
    weight[...] = jnp.broadcast_to(jnp.sum(weights, axis=1, keepdims=True), weight.shape)

    none = jnp.zeros_like(chooser)
    chooser = jnp.concatenate(
        [jnp.concatenate([chooser, none], axis=1), jnp.concatenate([none, chooser], axis=1)], axis=0
    )
    for pair in range(0, lat_dev, 2):
        if pair % chunk == 0:
            large[pair // chunk].wait()
        spread = []
        for t in range(pair, pair + 2):
            rows = fourier[t].reshape(fields * levels, columns).astype(jnp.float32)
            rows = (rows * weight[t : t + 1, :]).astype(jnp.bfloat16)
            parts = []
            for slot in range(slots):
                for field in range(fields):
                    for part in range(2):
                        parts.append(rows[field * levels : (field + 1) * levels] * masks[2 * slot + part])
            spread.append(jnp.concatenate(parts, axis=0))
        chosen = mxu(chooser, jnp.concatenate(spread, axis=1), NT)
        for side in range(2):
            for tile in range(tiles):
                scratch[tile, pl.ds(pair + side, owners, stride=lat_dev), :] = chosen[
                    side * owners : (side + 1) * owners, tile * LANES : (tile + 1) * LANES
                ]

    ids = send_ids[...].astype(jnp.float32)
    in_row = jnp.floor((ids + 0.5) * (1.0 / BLOCKS_X))
    in_column = ids - in_row * BLOCKS_X
    sides = [in_row[k : k + 1] for k in range(ids.shape[0])] + [in_column[k : k + 1] for k in range(ids.shape[0])]
    extra = jnp.broadcast_to(jnp.concatenate(sides, axis=1), (8, LANES))
    group = 8

    def send(g):
        first = pl.multiple_of(g * group, group)
        return pltpu.make_async_copy(packed.at[pl.ds(first, group)], message.at[pl.ds(first, group)], out_sem.at[g])

    def finish(g, carry):
        for k in range(group):
            o = g * group + k
            parts = [scratch[tile, pl.ds(pl.multiple_of(o * lat_dev, 8), lat_dev), :] for tile in range(tiles)]
            packed[o] = jnp.concatenate(parts + [extra], axis=0).astype(jnp.bfloat16)
        send(g).start()
        return carry

    lax.fori_loop(0, owners // group, finish, 0)
    for g in range(owners // group):
        send(g).wait()


def spectral_kernel(
    arrived, tables_in, damping, spectral, message, tables, made, turned, rows_at, listed, row_of, listed_sem, in_sem, out_sem
):
    slots, per_slot, degrees = spectral.shape
    latitudes = tables.shape[1]

    def fetch(slot):
        return pltpu.make_async_copy(tables_in.at[slot], tables.at[slot], in_sem.at[slot])

    def fetch_one(slot, carry):
        fetch(slot).start()
        return carry

    lax.fori_loop(0, slots, fetch_one, 0)
    half = per_slot // 2
    field_rows = half // 3
    bands = arrived.shape[0]
    tiles = turned.shape[0] // LANES
    lat_dev = (arrived.shape[1] - 8) // tiles
    receivers, message_rows, message_lanes = message.shape
    lists = pltpu.make_async_copy(listed, row_of, listed_sem)

    wide = arrived[...].astype(jnp.float32)
    unit = identity(LANES)
    band = lax.broadcasted_iota(jnp.int32, listed.shape, 1)
    rows = wide[:, tiles * lat_dev, :].astype(jnp.bfloat16)
    rows = jnp.concatenate([rows, jnp.zeros((LANES - bands, LANES), jnp.bfloat16)], axis=0)
    rows = mxu(unit[: listed.shape[0]], rows, NT).astype(jnp.int32)
    listed[...] = (rows + jnp.where(band < bands, band, 0) * lat_dev) * 8
    lists.start()
    for tile in range(tiles):
        columns = wide[:, tile * lat_dev : (tile + 1) * lat_dev, :].reshape(latitudes, LANES)
        turned[tile * LANES : (tile + 1) * LANES, :] = mxu(unit, columns.astype(jnp.bfloat16), NT).astype(jnp.bfloat16)

    gap = jnp.zeros((LANES - half, degrees), jnp.bfloat16)
    chunk = 256

    def one_slot(slot, carry):
        fetch(slot).wait()
        own = turned[pl.ds(pl.multiple_of(slot * per_slot, 32), per_slot), :]
        spectra = mxu(own, tables[slot], NN)
        damped = (spectra * damping[pl.ds(slot, 1), :]).astype(jnp.bfloat16)
        spectral[slot] = damped
        sides = []
        for part in range(2):
            for field in range(3):
                at = (2 * field + part) * field_rows
                sides.append(damped[at : at + field_rows])
            sides.append(gap)
        sides = jnp.concatenate(sides, axis=0)
        for at in range(0, latitudes, chunk):
            back = mxu(tables[slot, at : at + chunk, :], sides, NT)
            for part in range(2):
                rows_at[pl.ds(at * 2 * slots + slot * 2 + part, chunk, stride=2 * slots), :] = back[
                    :, part * LANES : (part + 1) * LANES
                ]
        return carry

    lax.fori_loop(0, slots, one_slot, 0)

    lists.wait()
    lane = lax.broadcasted_iota(jnp.int32, (8, LANES), 1)
    wide_tiles = message_lanes // LANES

    group = 4
    groups = receivers // group

    def send(g):
        at = pl.multiple_of(g * group, group)
        return pltpu.make_async_copy(made.at[pl.ds(at, group)], message.at[pl.ds(at, group)], out_sem.at[g])

    def one_group(g, carry):
        for k in range(group):
            r = g * group + k
            for pair in range(message_rows // 16):
                halves = []
                for side in range(2):
                    built = [None] * wide_tiles
                    for e in range(8):
                        entry = (pair * 2 + side) * 8 + e
                        at = pl.multiple_of(row_of[receivers * (entry % 2) + r, entry // 2], 8)
                        row = rows_at[pl.ds(at, 8), :]
                        start = e * half
                        if start % LANES:
                            row = pltpu.roll(row, start % LANES, 1)
                        for tile in range(start // LANES, (start + half - 1) // LANES + 1):
                            first = start - tile * LANES
                            if built[tile] is None:
                                built[tile] = row
                            else:
                                built[tile] = jnp.where(lane >= first, row, built[tile])
                    halves.append(jnp.concatenate(built, axis=1))
                both = jnp.concatenate(halves, axis=0).astype(jnp.bfloat16)
                made[r, pair * 16 : (pair + 1) * 16, :] = both
        send(g).start()
        return carry

    lax.fori_loop(0, groups, one_group, 0)
    for g in range(groups):
        send(g).wait()


def horizontal_rows(stencil, blocks, hweight, horizontal):
    together = stencil.shape[1] // 4

    def some_rows(i, carry):
        for k in range(together):
            a = i * together + k
            total = None
            for q in range(4):
                term = hweight[a, q : q + 1, :] * blocks[stencil[i, k * 4 + q]]
                total = term if total is None else total + term
            horizontal[a] = total
        return carry

    lax.fori_loop(0, stencil.shape[0], some_rows, 0)


def block_kernel(
    column_of, stencil, flags, received, zonal, vweight, hweight, blocks, lowest, highest, spread, horizontal,
    lowest_scratch, highest_scratch,
):
    owners, message_rows, message_lanes = received.shape
    unit = identity(LANES)
    half = message_lanes // 8
    groups = message_rows // 8
    entries = blocks.shape[0]
    rows, levels, _ = spread.shape
    per_entry = rows // entries
    for pair in range(groups // 2):
        wide = received[:, pair * 16 : (pair + 1) * 16, :].astype(jnp.float32)
        for side in range(2):
            group = pair * 2 + side
            own = wide[:, side * 8 : (side + 1) * 8, :].reshape(owners * 8, message_lanes).astype(jnp.bfloat16)
            turned = [
                mxu(unit, own[:, tile * LANES : (tile + 1) * LANES], NT).astype(jnp.bfloat16)
                for tile in range(message_lanes // LANES)
            ]
            turned = jnp.concatenate(turned, axis=0)
            for e in range(8):
                entry = group * 8 + e
                made = mxu(turned[e * half : (e + 1) * half], zonal[column_of[entry]], NN)
                made = made.astype(jnp.bfloat16).astype(jnp.float32)
                blocks[entry] = made
                for a in range(entry * per_entry, (entry + 1) * per_entry):
                    spread[a] = jnp.broadcast_to(vweight[:, a : a + 1], (levels, LANES))
                for field in range(3):
                    lowest_scratch[field * entries + entry : field * entries + entry + 1, :] = made[
                        field * 16 : field * 16 + 1, :
                    ]
                    highest_scratch[field * entries + entry : field * entries + entry + 1, :] = made[
                        field * 16 + 15 : field * 16 + 16, :
                    ]
    lowest[...] = lowest_scratch[...].astype(jnp.bfloat16)
    highest[...] = highest_scratch[...].astype(jnp.bfloat16)

    @pl.when(flags[1] == 1)
    def _():
        horizontal_rows(stencil, blocks, hweight, horizontal)


def horizontal_kernel(stencil, flags, blocks, hweight, horizontal):
    @pl.when(flags[1] == 0)
    def _():
        horizontal_rows(stencil, blocks, hweight, horizontal)


def vertical_kernel(
    stencil, flags, early, late, highest, above, hweight, spread, arrival, made, over_rows, wide, out_sem
):
    rows, fields, levels, _ = made.shape
    entries = wide.shape[0]
    top = flags[0] == 1
    over_rows[...] = jnp.where(top, highest[...].astype(jnp.float32), above[...].astype(jnp.float32))
    together = 8

    def widen(i, carry):
        for k in range(together):
            entry = i * together + k
            for field in range(fields):
                wide[entry, 7 - field : 8 - field, :] = over_rows[pl.ds(field * entries + entry, 1), :]
        return carry

    lax.fori_loop(0, entries // together, widen, 0)

    row = lax.broadcasted_iota(jnp.int32, (8, LANES), 0)
    piece = stencil.shape[1] // 4
    pieces = rows // piece

    def send(i):
        at = pl.multiple_of(i * piece, piece)
        return pltpu.make_async_copy(made.at[pl.ds(at, piece)], arrival.at[pl.ds(at, piece)], out_sem.at[i])

    def some_rows(horizontal, i, carry):
        for k in range(piece):
            a = i * piece + k
            last = None
            for q in range(4):
                term = hweight[a, q : q + 1, :] * wide[stencil[i, k * 4 + q]]
                last = term if last is None else last + term
            for field in range(fields):
                parts = []
                over = last if field == 0 else pltpu.roll(last, field, 0)
                for part in reversed(range(levels // 8)):
                    here = horizontal[a, field * levels + part * 8 : field * levels + (part + 1) * 8, :]
                    turned = pltpu.roll(here, 7, 0)
                    up = jnp.where(row == 7, over, turned)
                    parts.insert(0, here + spread[a, part * 8 : (part + 1) * 8, :] * (up - here))
                    over = turned
                made[a, field] = jnp.concatenate(parts, axis=0).astype(jnp.bfloat16)
        send(i).start()
        return carry

    @pl.when(flags[1] == 1)
    def _():
        lax.fori_loop(0, pieces, functools.partial(some_rows, early), 0)

    @pl.when(flags[1] == 0)
    def _():
        lax.fori_loop(0, pieces, functools.partial(some_rows, late), 0)

    for i in range(pieces):
        send(i).wait()


def whole(memory):
    return pl.BlockSpec(memory_space=memory)


def per_device(fourier, gauss, legendre, owner, send_list, stencil, hweight, vweight):
    lat_count = lax.axis_size("lat")
    device_row = lax.axis_index("lat")
    lat_dev, fields, levels, columns = fourier.shape
    wave_total = columns // 2
    slot_most = legendre.shape[1]
    degrees = legendre.shape[3]
    latitudes = legendre.shape[2]
    slot_count = lat_count * slot_most
    capacity = send_list.shape[2]
    arrivals = stencil.shape[0]
    half = fields * levels
    per_slot = 2 * half
    message_lanes = slot_most * per_slot
    tiles = message_lanes // LANES
    entries = lat_count * capacity

    owners = owner[:, 0]
    wave_index = jnp.arange(wave_total, dtype=jnp.int32)
    earlier = (owners[:, None] == owners[None, :]) & (wave_index[:, None] < wave_index[None, :])
    slot_rank = jnp.sum(earlier.astype(jnp.int32), axis=0)
    slot_of = owners * slot_most + slot_rank
    wave_number = wave_index * (degrees // wave_total)
    vmem = whole(pltpu.VMEM)
    smem = whole(pltpu.SMEM)
    hbm = whole(pl.ANY)
    message_one = pl.pallas_call(
        pack_kernel,
        out_shape=jax.ShapeDtypeStruct((lat_count, tiles * lat_dev + 8, LANES), jnp.bfloat16),
        in_specs=[hbm, hbm, hbm, hbm],
        out_specs=hbm,
        scratch_shapes=[
            pltpu.VMEM((1, wave_total), jnp.int32),
            pltpu.VMEM((capacity, lat_count), jnp.int32),
            pltpu.VMEM((1, lat_dev), jnp.float32),
            pltpu.VMEM(fourier.shape, jnp.bfloat16),
            pltpu.VMEM((lat_count, tiles * lat_dev + 8, LANES), jnp.bfloat16),
            pltpu.VMEM((tiles, lat_count * lat_dev, LANES), jnp.float32),
            pltpu.VMEM((lat_dev, columns), jnp.float32),
            pltpu.SemaphoreType.DMA((lat_dev // 8 + 3,)),
            pltpu.SemaphoreType.DMA((lat_count // 8,)),
        ],
        compiler_params=pltpu.CompilerParams(vmem_limit_bytes=GRANT),
        name="pack",
    )(owner.reshape(1, wave_total), send_list[0].T, gauss.reshape(1, lat_dev), fourier)
    arrived = lax.all_to_all(message_one, "lat", split_axis=0, concat_axis=0, tiled=True)

    placed = (slot_of[:, None] == jnp.arange(slot_count, dtype=jnp.int32)[None, :]).astype(jnp.int32)
    owned = lax.dynamic_slice_in_dim(placed, device_row * slot_most, slot_most, 1)
    filled = jnp.sum(owned, axis=0) > 0
    slot_wave = jnp.sum(owned * wave_number[:, None], axis=0)
    degree_index = jnp.arange(degrees, dtype=jnp.int32)
    keep_mask = (filled[:, None] & (degree_index[None, :] >= slot_wave[:, None])).astype(jnp.float32)
    damping = keep_mask * damping_curve(degrees)[None, :]

    message_shape = (lat_count, entries // 8 * slot_most * 2, 8 * half)
    spectral_rows, message_two = pl.pallas_call(
        spectral_kernel,
        in_specs=[vmem, hbm, vmem],
        out_specs=[vmem, hbm],
        scratch_shapes=[
            pltpu.VMEM((slot_most, latitudes, degrees), jnp.bfloat16),
            pltpu.VMEM(message_shape, jnp.bfloat16),
            pltpu.VMEM((message_lanes, latitudes), jnp.bfloat16),
            pltpu.VMEM((latitudes * 2 * slot_most, LANES), jnp.float32),
            pltpu.VMEM((entries, LANES), jnp.int32),
            pltpu.SMEM((entries, LANES), jnp.int32),
            pltpu.SemaphoreType.DMA,
            pltpu.SemaphoreType.DMA((slot_most,)),
            pltpu.SemaphoreType.DMA((lat_count // 4,)),
        ],
        out_shape=[
            jax.ShapeDtypeStruct((slot_most, per_slot, degrees), jnp.bfloat16),
            jax.ShapeDtypeStruct(message_shape, jnp.bfloat16),
        ],
        compiler_params=pltpu.CompilerParams(vmem_limit_bytes=52 * 2**20),
        name="spectral",
    )(arrived, legendre[0], damping)
    received = lax.all_to_all(message_two, "lat", split_axis=0, concat_axis=0, tiled=True)

    spectral = jnp.transpose(
        spectral_rows.reshape(slot_most, fields, 2, levels, degrees), (0, 1, 3, 2, 4)
    )
    slot_waves = jnp.sum(placed * wave_number[:, None], axis=0)
    slot_waves, spectral = lax.optimization_barrier((slot_waves, spectral))
    present = (jnp.sum(placed, axis=0) > 0).astype(jnp.float32)
    points = jnp.arange(NLON, dtype=jnp.int32).reshape(BLOCKS_X, 1, 1, BLK)
    phases = slot_waves[None, :, None, None] * points % NLON
    angles = phases.astype(jnp.float32) * (2.0 * math.pi / NLON)
    norm_factor = present[None, :, None, None] / math.sqrt(wave_total)
    zonal = jnp.concatenate([jnp.cos(angles) * norm_factor, -jnp.sin(angles) * norm_factor], axis=2)
    zonal = zonal.astype(jnp.bfloat16).reshape(BLOCKS_X, slot_count * 2, BLK)
    all_columns = arrived[:, tiles * lat_dev, entries:].reshape(lat_count, capacity, lat_count)
    column_of = lax.dynamic_index_in_dim(all_columns, device_row, 2, keepdims=False)
    column_of = column_of.astype(jnp.int32).reshape(-1)
    lev_count = lax.axis_size("lev")
    level_group = lax.axis_index("lev")
    flags = jnp.stack([(level_group == lev_count - 1).astype(jnp.int32), (level_group % 2).astype(jnp.int32)])
    vertical = vweight.T
    corners = stencil.reshape(arrivals // 32, 128)
    received, vertical, corners, flags = lax.optimization_barrier((received, vertical, corners, flags))
    blocks, lowest, highest, spread, early = pl.pallas_call(
        block_kernel,
        out_shape=[
            jax.ShapeDtypeStruct((entries, half, BLK), jnp.float32),
            jax.ShapeDtypeStruct((fields * entries, BLK), jnp.bfloat16),
            jax.ShapeDtypeStruct((fields * entries, BLK), jnp.bfloat16),
            jax.ShapeDtypeStruct((arrivals, levels, BLK), jnp.float32),
            jax.ShapeDtypeStruct((arrivals, half, BLK), jnp.float32),
        ],
        in_specs=[smem, smem, smem, vmem, vmem, vmem, vmem],
        out_specs=[vmem, vmem, vmem, vmem, vmem],
        scratch_shapes=[pltpu.VMEM((fields * entries, BLK), jnp.float32)] * 2,
        compiler_params=pltpu.CompilerParams(vmem_limit_bytes=16 * 2**20),
        name="blocks",
    )(column_of, corners, flags, received, zonal, vertical, hweight)

    above = lax.ppermute(lowest, "lev", [(i, i - 1) for i in range(1, lev_count)])
    late = pl.pallas_call(
        horizontal_kernel,
        out_shape=jax.ShapeDtypeStruct((arrivals, half, BLK), jnp.float32),
        in_specs=[smem, smem, vmem, vmem],
        out_specs=vmem,
        compiler_params=pltpu.CompilerParams(vmem_limit_bytes=16 * 2**20),
        cost_estimate=pl.CostEstimate(
            flops=8 * arrivals * half * BLK, bytes_accessed=4 * arrivals * half * BLK, transcendentals=0
        ),
        name="horizontal",
    )(corners, flags, blocks, hweight)
    arrival = pl.pallas_call(
        vertical_kernel,
        out_shape=jax.ShapeDtypeStruct((arrivals, fields, levels, BLK), jnp.bfloat16),
        in_specs=[smem, smem, vmem, vmem, vmem, vmem, vmem, vmem],
        out_specs=hbm,
        scratch_shapes=[
            pltpu.VMEM((arrivals, fields, levels, BLK), jnp.bfloat16),
            pltpu.VMEM((fields * entries, BLK), jnp.float32),
            pltpu.VMEM((entries, 8, BLK), jnp.float32),
            pltpu.SemaphoreType.DMA((arrivals // 32,)),
        ],
        compiler_params=pltpu.CompilerParams(vmem_limit_bytes=16 * 2**20),
        name="vertical",
    )(corners, flags, early, late, highest, above, hweight, spread)
    return (spectral[None], arrival)


def solution(mesh):
    return jax.shard_map(
        per_device,
        mesh=mesh,
        in_specs=(
            P("lat", None, "lev", None),
            P("lat"),
            P("lat", None, None, None),
            P(),
            P("lat", None, None),
            P("lat", None),
            P("lat", None, None),
            P("lat", "lev"),
        ),
        out_specs=(P("lat", None, None, "lev", None, None), P("lat", None, "lev", None)),
        check_vma=False,
    )
```

```python
import math

import jax
import jax.numpy as jnp
from jax import lax
from jax.experimental import pallas as pl
from jax.experimental.pallas import tpu as pltpu
from jax.sharding import PartitionSpec as P

NLON = 2560
BLK = 128
BLOCKS_X = NLON // BLK
LANES = 128
GRANT = 56 * 2**20

diffusion = 3.0

NT = (((1,), (1,)), ((), ()))
NN = (((1,), (0,)), ((), ()))


def mxu(left, right, dims):
    return lax.dot_general(left, right, dims, preferred_element_type=jnp.float32)


def identity(size):
    rows = lax.broadcasted_iota(jnp.int32, (size, size), 0)
    columns = lax.broadcasted_iota(jnp.int32, (size, size), 1)
    return (rows == columns).astype(jnp.float32).astype(jnp.bfloat16)


def damping_curve(degrees):
    order_n = jnp.arange(degrees, dtype=jnp.float32)
    ratio = order_n * (order_n + 1.0) / float(degrees * (degrees - 1))
    return 1.0 / (1.0 + diffusion * ratio * ratio)


def pack_kernel(
    owner_in, ids_in, gauss_in, fourier_in, message, owner, send_ids, gauss, fourier, packed, scratch, weight, in_sem, out_sem
):
    lat_dev, fields, levels, columns = fourier.shape
    owners = packed.shape[0]
    tiles = scratch.shape[0]
    slots = (tiles * LANES) // (2 * fields * levels)
    chunk = 8
    pieces = lat_dev // chunk
    small = [
        pltpu.make_async_copy(source, target, in_sem.at[pieces + i])
        for i, (source, target) in enumerate(((owner_in, owner), (ids_in, send_ids), (gauss_in, gauss)))
    ]
    large = [
        pltpu.make_async_copy(
            fourier_in.at[pl.ds(i * chunk, chunk)], fourier.at[pl.ds(i * chunk, chunk)], in_sem.at[i]
        )
        for i in range(pieces)
    ]
    for copy in small + large:
        copy.start()
    for copy in small:
        copy.wait()

    waves = owner.shape[1]
    wave_at = lax.broadcasted_iota(jnp.int32, (waves, columns), 0)
    column = lax.broadcasted_iota(jnp.int32, (waves, columns), 1)
    square_row = lax.broadcasted_iota(jnp.int32, (waves, waves), 0)
    square_column = lax.broadcasted_iota(jnp.int32, (waves, waves), 1)
    listed = jnp.broadcast_to(owner[...], (waves, waves))
    upright = jnp.sum(jnp.where(square_row == square_column, listed, 0), axis=1, keepdims=True)
    upright = jnp.broadcast_to(upright, (waves, columns))
    column_owner = jnp.sum(jnp.where(wave_at == column // 2, upright, 0), axis=0, keepdims=True)
    earlier = (upright == jnp.broadcast_to(column_owner, (waves, columns))) & (wave_at < column // 2)
    column_rank = jnp.sum(jnp.where(earlier, 1, 0), axis=0, keepdims=True)
    owner_at = lax.broadcasted_iota(jnp.int32, (owners, columns), 0)
    chooser = jnp.where(owner_at == column_owner, 1.0, 0.0).astype(jnp.bfloat16)
    part_of = 2 * column_rank + lax.broadcasted_iota(jnp.int32, (1, columns), 1) % 2
    masks = [
        jnp.broadcast_to(jnp.where(part_of == i, 1.0, 0.0), (levels, columns)).astype(jnp.bfloat16)
        for i in range(2 * slots)
    ]
    turn_row = lax.broadcasted_iota(jnp.int32, (lat_dev, lat_dev), 0)
    turn_column = lax.broadcasted_iota(jnp.int32, (lat_dev, lat_dev), 1)
    weights = jnp.where(turn_row == turn_column, jnp.broadcast_to(gauss[...], (lat_dev, lat_dev)), 0.0)
    weight[...] = jnp.broadcast_to(jnp.sum(weights, axis=1, keepdims=True), weight.shape)

    none = jnp.zeros_like(chooser)
    chooser = jnp.concatenate(
        [jnp.concatenate([chooser, none], axis=1), jnp.concatenate([none, chooser], axis=1)], axis=0
    )
    for pair in range(0, lat_dev, 2):
        if pair % chunk == 0:
            large[pair // chunk].wait()
        spread = []
        for t in range(pair, pair + 2):
            rows = fourier[t].reshape(fields * levels, columns).astype(jnp.float32)
            rows = (rows * weight[t : t + 1, :]).astype(jnp.bfloat16)
            parts = []
            for slot in range(slots):
                for field in range(fields):
                    for part in range(2):
                        parts.append(rows[field * levels : (field + 1) * levels] * masks[2 * slot + part])
            spread.append(jnp.concatenate(parts, axis=0))
        chosen = mxu(chooser, jnp.concatenate(spread, axis=1), NT)
        for side in range(2):
            for tile in range(tiles):
                scratch[tile, pl.ds(pair + side, owners, stride=lat_dev), :] = chosen[
                    side * owners : (side + 1) * owners, tile * LANES : (tile + 1) * LANES
                ]

    ids = send_ids[...].astype(jnp.float32)
    in_row = jnp.floor((ids + 0.5) * (1.0 / BLOCKS_X))
    in_column = ids - in_row * BLOCKS_X
    sides = [in_row[k : k + 1] for k in range(ids.shape[0])] + [in_column[k : k + 1] for k in range(ids.shape[0])]
    extra = jnp.broadcast_to(jnp.concatenate(sides, axis=1), (8, LANES))
    group = 8

    def send(g):
        first = pl.multiple_of(g * group, group)
        return pltpu.make_async_copy(packed.at[pl.ds(first, group)], message.at[pl.ds(first, group)], out_sem.at[g])

    def finish(g, carry):
        for k in range(group):
            o = g * group + k
            parts = [scratch[tile, pl.ds(pl.multiple_of(o * lat_dev, 8), lat_dev), :] for tile in range(tiles)]
            packed[o] = jnp.concatenate(parts + [extra], axis=0).astype(jnp.bfloat16)
        send(g).start()
        return carry

    lax.fori_loop(0, owners // group, finish, 0)
    for g in range(owners // group):
        send(g).wait()


def spectral_kernel(
    arrived, tables_in, damping, spectral, message, tables, made, turned, rows_at, listed, row_of, listed_sem, in_sem, out_sem
):
    slots, per_slot, degrees = spectral.shape
    latitudes = tables.shape[1]

    def fetch(slot):
        return pltpu.make_async_copy(tables_in.at[slot], tables.at[slot], in_sem.at[slot])

    def fetch_one(slot, carry):
        fetch(slot).start()
        return carry

    lax.fori_loop(0, slots, fetch_one, 0)
    half = per_slot // 2
    field_rows = half // 3
    bands = arrived.shape[0]
    tiles = turned.shape[0] // LANES
    lat_dev = (arrived.shape[1] - 8) // tiles
    receivers, message_rows, message_lanes = message.shape
    lists = pltpu.make_async_copy(listed, row_of, listed_sem)

    wide = arrived[...].astype(jnp.float32)
    unit = identity(LANES)
    band = lax.broadcasted_iota(jnp.int32, listed.shape, 1)
    rows = wide[:, tiles * lat_dev, :].astype(jnp.bfloat16)
    rows = jnp.concatenate([rows, jnp.zeros((LANES - bands, LANES), jnp.bfloat16)], axis=0)
    rows = mxu(unit[: listed.shape[0]], rows, NT).astype(jnp.int32)
    listed[...] = (rows + jnp.where(band < bands, band, 0) * lat_dev) * 8
    lists.start()
    for tile in range(tiles):
        columns = wide[:, tile * lat_dev : (tile + 1) * lat_dev, :].reshape(latitudes, LANES)
        turned[tile * LANES : (tile + 1) * LANES, :] = mxu(unit, columns.astype(jnp.bfloat16), NT).astype(jnp.bfloat16)

    gap = jnp.zeros((LANES - half, degrees), jnp.bfloat16)
    chunk = 256

    def one_slot(slot, carry):
        fetch(slot).wait()
        own = turned[pl.ds(pl.multiple_of(slot * per_slot, 32), per_slot), :]
        spectra = mxu(own, tables[slot], NN)
        damped = (spectra * damping[pl.ds(slot, 1), :]).astype(jnp.bfloat16)
        spectral[slot] = damped
        sides = []
        for part in range(2):
            for field in range(3):
                at = (2 * field + part) * field_rows
                sides.append(damped[at : at + field_rows])
            sides.append(gap)
        sides = jnp.concatenate(sides, axis=0)
        for at in range(0, latitudes, chunk):
            back = mxu(tables[slot, at : at + chunk, :], sides, NT)
            for part in range(2):
                rows_at[pl.ds(at * 2 * slots + slot * 2 + part, chunk, stride=2 * slots), :] = back[
                    :, part * LANES : (part + 1) * LANES
                ]
        return carry

    lax.fori_loop(0, slots, one_slot, 0)

    lists.wait()
    lane = lax.broadcasted_iota(jnp.int32, (8, LANES), 1)
    wide_tiles = message_lanes // LANES

    group = 4
    groups = receivers // group

    def send(g):
        at = pl.multiple_of(g * group, group)
        return pltpu.make_async_copy(made.at[pl.ds(at, group)], message.at[pl.ds(at, group)], out_sem.at[g])

    def one_group(g, carry):
        for k in range(group):
            r = g * group + k
            for pair in range(message_rows // 16):
                halves = []
                for side in range(2):
                    built = [None] * wide_tiles
                    for e in range(8):
                        entry = (pair * 2 + side) * 8 + e
                        at = pl.multiple_of(row_of[receivers * (entry % 2) + r, entry // 2], 8)
                        row = rows_at[pl.ds(at, 8), :]
                        start = e * half
                        if start % LANES:
                            row = pltpu.roll(row, start % LANES, 1)
                        for tile in range(start // LANES, (start + half - 1) // LANES + 1):
                            first = start - tile * LANES
                            if built[tile] is None:
                                built[tile] = row
                            else:
                                built[tile] = jnp.where(lane >= first, row, built[tile])
                    halves.append(jnp.concatenate(built, axis=1))
                both = jnp.concatenate(halves, axis=0).astype(jnp.bfloat16)
                made[r, pair * 16 : (pair + 1) * 16, :] = both
        send(g).start()
        return carry

    lax.fori_loop(0, groups, one_group, 0)
    for g in range(groups):
        send(g).wait()


def block_kernel(
    column_of, received, zonal, vweight, blocks, lowest, highest, spread, lowest_scratch, highest_scratch
):
    owners, message_rows, message_lanes = received.shape
    unit = identity(LANES)
    half = message_lanes // 8
    groups = message_rows // 8
    entries = blocks.shape[0]
    rows, levels, _ = spread.shape
    per_entry = rows // entries
    for pair in range(groups // 2):
        wide = received[:, pair * 16 : (pair + 1) * 16, :].astype(jnp.float32)
        for side in range(2):
            group = pair * 2 + side
            own = wide[:, side * 8 : (side + 1) * 8, :].reshape(owners * 8, message_lanes).astype(jnp.bfloat16)
            turned = [
                mxu(unit, own[:, tile * LANES : (tile + 1) * LANES], NT).astype(jnp.bfloat16)
                for tile in range(message_lanes // LANES)
            ]
            turned = jnp.concatenate(turned, axis=0)
            for e in range(8):
                entry = group * 8 + e
                made = mxu(turned[e * half : (e + 1) * half], zonal[column_of[entry]], NN)
                made = made.astype(jnp.bfloat16).astype(jnp.float32)
                blocks[entry] = made
                for a in range(entry * per_entry, (entry + 1) * per_entry):
                    spread[a] = jnp.broadcast_to(vweight[:, a : a + 1], (levels, LANES))
                for field in range(3):
                    lowest_scratch[field * entries + entry : field * entries + entry + 1, :] = made[
                        field * 16 : field * 16 + 1, :
                    ]
                    highest_scratch[field * entries + entry : field * entries + entry + 1, :] = made[
                        field * 16 + 15 : field * 16 + 16, :
                    ]
    lowest[...] = lowest_scratch[...].astype(jnp.bfloat16)
    highest[...] = highest_scratch[...].astype(jnp.bfloat16)


def horizontal_kernel(stencil, blocks, hweight, spread, partial, tops):
    _, fields, levels, _ = partial.shape
    together = stencil.shape[1] // 4
    row = lax.broadcasted_iota(jnp.int32, (8, LANES), 0)

    def some_rows(i, carry):
        for k in range(together):
            a = i * together + k
            total = None
            for q in range(4):
                term = hweight[a, q : q + 1, :] * blocks[stencil[i, k * 4 + q]]
                total = term if total is None else total + term
            lower = spread[a, 0:8, :]
            upper = spread[a, 8:16, :]
            top = None
            for field in range(fields):
                first = total[field * levels : field * levels + 8]
                second = total[field * levels + 8 : field * levels + 16]
                turned = pltpu.roll(second, 7, 0)
                up = jnp.where(row == 7, turned, pltpu.roll(first, 7, 0))
                low = first + lower * (up - first)
                high = jnp.where(row == 7, 0.0, second + upper * (turned - second))
                partial[a, field] = jnp.concatenate([low, high], axis=0).astype(jnp.bfloat16)
                placed = second if field == 0 else turned if field == 1 else pltpu.roll(second, 8 - field, 0)
                top = placed if top is None else jnp.where(row == 7 - field, placed, top)
            tops[a] = top
        return carry

    lax.fori_loop(0, stencil.shape[0], some_rows, 0)


def vertical_kernel(
    stencil, at_top, partial, tops, highest, above, hweight, spread, arrival, made, over_rows, wide, out_sem
):
    rows, fields, levels, _ = made.shape
    entries = wide.shape[0]
    top = at_top[0] == 1
    over_rows[...] = jnp.where(top, highest[...].astype(jnp.float32), above[...].astype(jnp.float32))
    together = 8

    def widen(i, carry):
        for k in range(together):
            entry = i * together + k
            for field in range(fields):
                wide[entry, 7 - field : 8 - field, :] = over_rows[pl.ds(field * entries + entry, 1), :]
        return carry

    lax.fori_loop(0, entries // together, widen, 0)

    row = lax.broadcasted_iota(jnp.int32, (8, LANES), 0)
    piece = stencil.shape[1] // 4
    pieces = rows // piece

    def send(i):
        at = pl.multiple_of(i * piece, piece)
        return pltpu.make_async_copy(made.at[pl.ds(at, piece)], arrival.at[pl.ds(at, piece)], out_sem.at[i])

    def some_rows(i, carry):
        for k in range(piece):
            a = i * piece + k
            last = None
            for q in range(4):
                term = hweight[a, q : q + 1, :] * wide[stencil[i, k * 4 + q]]
                last = term if last is None else last + term
            here = tops[a]
            top = here + spread[a, levels - 1 : levels, :] * (last - here)
            for field in range(fields):
                placed = top if field == 0 else pltpu.roll(top, field, 0)
                placed = jnp.where(row == 7, placed, 0.0)
                patch = jnp.concatenate([jnp.zeros_like(placed), placed], axis=0).astype(jnp.bfloat16)
                made[a, field] = partial[a, field] + patch
        send(i).start()
        return carry

    lax.fori_loop(0, pieces, some_rows, 0)
    for i in range(pieces):
        send(i).wait()


def whole(memory):
    return pl.BlockSpec(memory_space=memory)


def per_device(fourier, gauss, legendre, owner, send_list, stencil, hweight, vweight):
    lat_count = lax.axis_size("lat")
    device_row = lax.axis_index("lat")
    lat_dev, fields, levels, columns = fourier.shape
    wave_total = columns // 2
    slot_most = legendre.shape[1]
    degrees = legendre.shape[3]
    latitudes = legendre.shape[2]
    slot_count = lat_count * slot_most
    capacity = send_list.shape[2]
    arrivals = stencil.shape[0]
    half = fields * levels
    per_slot = 2 * half
    message_lanes = slot_most * per_slot
    tiles = message_lanes // LANES
    entries = lat_count * capacity

    owners = owner[:, 0]
    wave_index = jnp.arange(wave_total, dtype=jnp.int32)
    earlier = (owners[:, None] == owners[None, :]) & (wave_index[:, None] < wave_index[None, :])
    slot_rank = jnp.sum(earlier.astype(jnp.int32), axis=0)
    slot_of = owners * slot_most + slot_rank
    wave_number = wave_index * (degrees // wave_total)
    vmem = whole(pltpu.VMEM)
    smem = whole(pltpu.SMEM)
    hbm = whole(pl.ANY)
    message_one = pl.pallas_call(
        pack_kernel,
        out_shape=jax.ShapeDtypeStruct((lat_count, tiles * lat_dev + 8, LANES), jnp.bfloat16),
        in_specs=[hbm, hbm, hbm, hbm],
        out_specs=hbm,
        scratch_shapes=[
            pltpu.VMEM((1, wave_total), jnp.int32),
            pltpu.VMEM((capacity, lat_count), jnp.int32),
            pltpu.VMEM((1, lat_dev), jnp.float32),
            pltpu.VMEM(fourier.shape, jnp.bfloat16),
            pltpu.VMEM((lat_count, tiles * lat_dev + 8, LANES), jnp.bfloat16),
            pltpu.VMEM((tiles, lat_count * lat_dev, LANES), jnp.float32),
            pltpu.VMEM((lat_dev, columns), jnp.float32),
            pltpu.SemaphoreType.DMA((lat_dev // 8 + 3,)),
            pltpu.SemaphoreType.DMA((lat_count // 8,)),
        ],
        compiler_params=pltpu.CompilerParams(vmem_limit_bytes=GRANT),
        name="pack",
    )(owner.reshape(1, wave_total), send_list[0].T, gauss.reshape(1, lat_dev), fourier)
    arrived = lax.all_to_all(message_one, "lat", split_axis=0, concat_axis=0, tiled=True)

    placed = (slot_of[:, None] == jnp.arange(slot_count, dtype=jnp.int32)[None, :]).astype(jnp.int32)
    owned = lax.dynamic_slice_in_dim(placed, device_row * slot_most, slot_most, 1)
    filled = jnp.sum(owned, axis=0) > 0
    slot_wave = jnp.sum(owned * wave_number[:, None], axis=0)
    degree_index = jnp.arange(degrees, dtype=jnp.int32)
    keep_mask = (filled[:, None] & (degree_index[None, :] >= slot_wave[:, None])).astype(jnp.float32)
    damping = keep_mask * damping_curve(degrees)[None, :]

    message_shape = (lat_count, entries // 8 * slot_most * 2, 8 * half)
    spectral_rows, message_two = pl.pallas_call(
        spectral_kernel,
        in_specs=[vmem, hbm, vmem],
        out_specs=[vmem, hbm],
        scratch_shapes=[
            pltpu.VMEM((slot_most, latitudes, degrees), jnp.bfloat16),
            pltpu.VMEM(message_shape, jnp.bfloat16),
            pltpu.VMEM((message_lanes, latitudes), jnp.bfloat16),
            pltpu.VMEM((latitudes * 2 * slot_most, LANES), jnp.float32),
            pltpu.VMEM((entries, LANES), jnp.int32),
            pltpu.SMEM((entries, LANES), jnp.int32),
            pltpu.SemaphoreType.DMA,
            pltpu.SemaphoreType.DMA((slot_most,)),
            pltpu.SemaphoreType.DMA((lat_count // 4,)),
        ],
        out_shape=[
            jax.ShapeDtypeStruct((slot_most, per_slot, degrees), jnp.bfloat16),
            jax.ShapeDtypeStruct(message_shape, jnp.bfloat16),
        ],
        compiler_params=pltpu.CompilerParams(vmem_limit_bytes=52 * 2**20),
        name="spectral",
    )(arrived, legendre[0], damping)
    received = lax.all_to_all(message_two, "lat", split_axis=0, concat_axis=0, tiled=True)

    spectral = jnp.transpose(
        spectral_rows.reshape(slot_most, fields, 2, levels, degrees), (0, 1, 3, 2, 4)
    )
    slot_waves = jnp.sum(placed * wave_number[:, None], axis=0)
    slot_waves, spectral = lax.optimization_barrier((slot_waves, spectral))
    present = (jnp.sum(placed, axis=0) > 0).astype(jnp.float32)
    points = jnp.arange(NLON, dtype=jnp.int32).reshape(BLOCKS_X, 1, 1, BLK)
    phases = slot_waves[None, :, None, None] * points % NLON
    angles = phases.astype(jnp.float32) * (2.0 * math.pi / NLON)
    norm_factor = present[None, :, None, None] / math.sqrt(wave_total)
    zonal = jnp.concatenate([jnp.cos(angles) * norm_factor, -jnp.sin(angles) * norm_factor], axis=2)
    zonal = zonal.astype(jnp.bfloat16).reshape(BLOCKS_X, slot_count * 2, BLK)
    all_columns = arrived[:, tiles * lat_dev, entries:].reshape(lat_count, capacity, lat_count)
    column_of = lax.dynamic_index_in_dim(all_columns, device_row, 2, keepdims=False)
    column_of = column_of.astype(jnp.int32).reshape(-1)
    lev_count = lax.axis_size("lev")
    at_top = (lax.axis_index("lev") == lev_count - 1).astype(jnp.int32).reshape(1)
    vertical = vweight.T
    corners = stencil.reshape(arrivals // 32, 128)
    received, vertical, corners, at_top = lax.optimization_barrier((received, vertical, corners, at_top))
    blocks, lowest, highest, spread = pl.pallas_call(
        block_kernel,
        out_shape=[
            jax.ShapeDtypeStruct((entries, half, BLK), jnp.float32),
            jax.ShapeDtypeStruct((fields * entries, BLK), jnp.bfloat16),
            jax.ShapeDtypeStruct((fields * entries, BLK), jnp.bfloat16),
            jax.ShapeDtypeStruct((arrivals, levels, BLK), jnp.float32),
        ],
        in_specs=[smem, vmem, vmem, vmem],
        out_specs=[vmem, vmem, vmem, vmem],
        scratch_shapes=[pltpu.VMEM((fields * entries, BLK), jnp.float32)] * 2,
        compiler_params=pltpu.CompilerParams(vmem_limit_bytes=16 * 2**20),
        name="blocks",
    )(column_of, received, zonal, vertical)

    above = lax.ppermute(lowest, "lev", [(i, i - 1) for i in range(1, lev_count)])
    partial, tops = pl.pallas_call(
        horizontal_kernel,
        out_shape=[
            jax.ShapeDtypeStruct((arrivals, fields, levels, BLK), jnp.bfloat16),
            jax.ShapeDtypeStruct((arrivals, 8, BLK), jnp.float32),
        ],
        in_specs=[smem, vmem, vmem, vmem],
        out_specs=[vmem, vmem],
        compiler_params=pltpu.CompilerParams(vmem_limit_bytes=16 * 2**20),
        cost_estimate=pl.CostEstimate(
            flops=8 * arrivals * half * BLK, bytes_accessed=4 * arrivals * half * BLK, transcendentals=0
        ),
        name="horizontal",
    )(corners, blocks, hweight, spread)
    arrival = pl.pallas_call(
        vertical_kernel,
        out_shape=jax.ShapeDtypeStruct((arrivals, fields, levels, BLK), jnp.bfloat16),
        in_specs=[smem, smem, vmem, vmem, vmem, vmem, vmem, vmem],
        out_specs=hbm,
        scratch_shapes=[
            pltpu.VMEM((arrivals, fields, levels, BLK), jnp.bfloat16),
            pltpu.VMEM((fields * entries, BLK), jnp.float32),
            pltpu.VMEM((entries, 8, BLK), jnp.float32),
            pltpu.SemaphoreType.DMA((arrivals // 32,)),
        ],
        compiler_params=pltpu.CompilerParams(vmem_limit_bytes=16 * 2**20),
        name="vertical",
    )(corners, at_top, partial, tops, highest, above, hweight, spread)
    return (spectral[None], arrival)


def solution(mesh):
    return jax.shard_map(
        per_device,
        mesh=mesh,
        in_specs=(
            P("lat", None, "lev", None),
            P("lat"),
            P("lat", None, None, None),
            P(),
            P("lat", None, None),
            P("lat", None),
            P("lat", None, None),
            P("lat", "lev"),
        ),
        out_specs=(P("lat", None, None, "lev", None, None), P("lat", None, "lev", None)),
        check_vma=False,
    )
```

```python
import math

import jax
import jax.numpy as jnp
from jax import lax
from jax.experimental import pallas as pl
from jax.experimental.pallas import tpu as pltpu
from jax.sharding import PartitionSpec as P

NLON = 2560
BLK = 128
BLOCKS_X = NLON // BLK
LANES = 128
GRANT = 56 * 2**20

diffusion = 3.0

NT = (((1,), (1,)), ((), ()))
NN = (((1,), (0,)), ((), ()))


def mxu(left, right, dims):
    return lax.dot_general(left, right, dims, preferred_element_type=jnp.float32)


def identity(size):
    rows = lax.broadcasted_iota(jnp.int32, (size, size), 0)
    columns = lax.broadcasted_iota(jnp.int32, (size, size), 1)
    return (rows == columns).astype(jnp.float32).astype(jnp.bfloat16)


def damping_curve(degrees):
    order_n = jnp.arange(degrees, dtype=jnp.float32)
    ratio = order_n * (order_n + 1.0) / float(degrees * (degrees - 1))
    return 1.0 / (1.0 + diffusion * ratio * ratio)


def pack_kernel(
    owner_in, ids_in, gauss_in, fourier_in, message, owner, send_ids, gauss, fourier, packed, scratch, weight, in_sem, out_sem
):
    lat_dev, fields, levels, columns = fourier.shape
    owners = packed.shape[0]
    tiles = scratch.shape[0]
    slots = (tiles * LANES) // (2 * fields * levels)
    chunk = 8
    pieces = lat_dev // chunk
    small = [
        pltpu.make_async_copy(source, target, in_sem.at[pieces + i])
        for i, (source, target) in enumerate(((owner_in, owner), (ids_in, send_ids), (gauss_in, gauss)))
    ]
    large = [
        pltpu.make_async_copy(
            fourier_in.at[pl.ds(i * chunk, chunk)], fourier.at[pl.ds(i * chunk, chunk)], in_sem.at[i]
        )
        for i in range(pieces)
    ]
    for copy in small + large:
        copy.start()
    for copy in small:
        copy.wait()

    waves = owner.shape[1]
    wave_at = lax.broadcasted_iota(jnp.int32, (waves, columns), 0)
    column = lax.broadcasted_iota(jnp.int32, (waves, columns), 1)
    square_row = lax.broadcasted_iota(jnp.int32, (waves, waves), 0)
    square_column = lax.broadcasted_iota(jnp.int32, (waves, waves), 1)
    listed = jnp.broadcast_to(owner[...], (waves, waves))
    upright = jnp.sum(jnp.where(square_row == square_column, listed, 0), axis=1, keepdims=True)
    upright = jnp.broadcast_to(upright, (waves, columns))
    column_owner = jnp.sum(jnp.where(wave_at == column // 2, upright, 0), axis=0, keepdims=True)
    earlier = (upright == jnp.broadcast_to(column_owner, (waves, columns))) & (wave_at < column // 2)
    column_rank = jnp.sum(jnp.where(earlier, 1, 0), axis=0, keepdims=True)
    owner_at = lax.broadcasted_iota(jnp.int32, (owners, columns), 0)
    chooser = jnp.where(owner_at == column_owner, 1.0, 0.0).astype(jnp.bfloat16)
    part_of = 2 * column_rank + lax.broadcasted_iota(jnp.int32, (1, columns), 1) % 2
    masks = [
        jnp.broadcast_to(jnp.where(part_of == i, 1.0, 0.0), (levels, columns)).astype(jnp.bfloat16)
        for i in range(2 * slots)
    ]
    turn_row = lax.broadcasted_iota(jnp.int32, (lat_dev, lat_dev), 0)
    turn_column = lax.broadcasted_iota(jnp.int32, (lat_dev, lat_dev), 1)
    weights = jnp.where(turn_row == turn_column, jnp.broadcast_to(gauss[...], (lat_dev, lat_dev)), 0.0)
    weight[...] = jnp.broadcast_to(jnp.sum(weights, axis=1, keepdims=True), weight.shape)

    none = jnp.zeros_like(chooser)
    chooser = jnp.concatenate(
        [jnp.concatenate([chooser, none], axis=1), jnp.concatenate([none, chooser], axis=1)], axis=0
    )
    for pair in range(0, lat_dev, 2):
        if pair % chunk == 0:
            large[pair // chunk].wait()
        spread = []
        for t in range(pair, pair + 2):
            rows = fourier[t].reshape(fields * levels, columns).astype(jnp.float32)
            rows = (rows * weight[t : t + 1, :]).astype(jnp.bfloat16)
            parts = []
            for slot in range(slots):
                for field in range(fields):
                    for part in range(2):
                        parts.append(rows[field * levels : (field + 1) * levels] * masks[2 * slot + part])
            spread.append(jnp.concatenate(parts, axis=0))
        chosen = mxu(chooser, jnp.concatenate(spread, axis=1), NT)
        for side in range(2):
            for tile in range(tiles):
                scratch[tile, pl.ds(pair + side, owners, stride=lat_dev), :] = chosen[
                    side * owners : (side + 1) * owners, tile * LANES : (tile + 1) * LANES
                ]

    ids = send_ids[...].astype(jnp.float32)
    in_row = jnp.floor((ids + 0.5) * (1.0 / BLOCKS_X))
    in_column = ids - in_row * BLOCKS_X
    sides = [in_row[k : k + 1] for k in range(ids.shape[0])] + [in_column[k : k + 1] for k in range(ids.shape[0])]
    extra = jnp.broadcast_to(jnp.concatenate(sides, axis=1), (8, LANES))
    group = 8

    def send(g):
        first = pl.multiple_of(g * group, group)
        return pltpu.make_async_copy(packed.at[pl.ds(first, group)], message.at[pl.ds(first, group)], out_sem.at[g])

    def finish(g, carry):
        for k in range(group):
            o = g * group + k
            parts = [scratch[tile, pl.ds(pl.multiple_of(o * lat_dev, 8), lat_dev), :] for tile in range(tiles)]
            packed[o] = jnp.concatenate(parts + [extra], axis=0).astype(jnp.bfloat16)
        send(g).start()
        return carry

    lax.fori_loop(0, owners // group, finish, 0)
    for g in range(owners // group):
        send(g).wait()


def spectral_kernel(
    arrived, tables_in, damping, spectral, message, tables, made, turned, rows_at, listed, row_of, listed_sem, in_sem, out_sem
):
    slots, per_slot, degrees = spectral.shape
    latitudes = tables.shape[1]

    def fetch(slot):
        return pltpu.make_async_copy(tables_in.at[slot], tables.at[slot], in_sem.at[slot])

    def fetch_one(slot, carry):
        fetch(slot).start()
        return carry

    lax.fori_loop(0, slots, fetch_one, 0)
    half = per_slot // 2
    field_rows = half // 3
    bands = arrived.shape[0]
    tiles = turned.shape[0] // LANES
    lat_dev = (arrived.shape[1] - 8) // tiles
    receivers, message_rows, message_lanes = message.shape
    lists = pltpu.make_async_copy(listed, row_of, listed_sem)

    wide = arrived[...].astype(jnp.float32)
    unit = identity(LANES)
    band = lax.broadcasted_iota(jnp.int32, listed.shape, 1)
    rows = wide[:, tiles * lat_dev, :].astype(jnp.bfloat16)
    rows = jnp.concatenate([rows, jnp.zeros((LANES - bands, LANES), jnp.bfloat16)], axis=0)
    rows = mxu(unit[: listed.shape[0]], rows, NT).astype(jnp.int32)
    listed[...] = (rows + jnp.where(band < bands, band, 0) * lat_dev) * 8
    lists.start()
    for tile in range(tiles):
        columns = wide[:, tile * lat_dev : (tile + 1) * lat_dev, :].reshape(latitudes, LANES)
        turned[tile * LANES : (tile + 1) * LANES, :] = jnp.transpose(columns).astype(jnp.bfloat16)

    gap = jnp.zeros((LANES - half, degrees), jnp.bfloat16)
    chunk = 256

    def one_slot(slot, carry):
        fetch(slot).wait()
        own = turned[pl.ds(pl.multiple_of(slot * per_slot, 32), per_slot), :]
        spectra = mxu(own, tables[slot], NN)
        damped = (spectra * damping[pl.ds(slot, 1), :]).astype(jnp.bfloat16)
        spectral[slot] = damped
        sides = []
        for part in range(2):
            for field in range(3):
                at = (2 * field + part) * field_rows
                sides.append(damped[at : at + field_rows])
            sides.append(gap)
        sides = jnp.concatenate(sides, axis=0)
        for at in range(0, latitudes, chunk):
            back = mxu(tables[slot, at : at + chunk, :], sides, NT)
            for part in range(2):
                rows_at[pl.ds(at * 2 * slots + slot * 2 + part, chunk, stride=2 * slots), :] = back[
                    :, part * LANES : (part + 1) * LANES
                ]
        return carry

    lax.fori_loop(0, slots, one_slot, 0)

    lists.wait()
    lane = lax.broadcasted_iota(jnp.int32, (8, LANES), 1)
    wide_tiles = message_lanes // LANES

    group = 4
    groups = receivers // group

    def send(g):
        at = pl.multiple_of(g * group, group)
        return pltpu.make_async_copy(made.at[pl.ds(at, group)], message.at[pl.ds(at, group)], out_sem.at[g])

    def one_group(g, carry):
        for k in range(group):
            r = g * group + k
            for pair in range(message_rows // 16):
                halves = []
                for side in range(2):
                    built = [None] * wide_tiles
                    for e in range(8):
                        entry = (pair * 2 + side) * 8 + e
                        at = pl.multiple_of(row_of[receivers * (entry % 2) + r, entry // 2], 8)
                        row = rows_at[pl.ds(at, 8), :]
                        start = e * half
                        if start % LANES:
                            row = pltpu.roll(row, start % LANES, 1)
                        for tile in range(start // LANES, (start + half - 1) // LANES + 1):
                            first = start - tile * LANES
                            if built[tile] is None:
                                built[tile] = row
                            else:
                                built[tile] = jnp.where(lane >= first, row, built[tile])
                    halves.append(jnp.concatenate(built, axis=1))
                both = jnp.concatenate(halves, axis=0).astype(jnp.bfloat16)
                made[r, pair * 16 : (pair + 1) * 16, :] = both
        send(g).start()
        return carry

    lax.fori_loop(0, groups, one_group, 0)
    for g in range(groups):
        send(g).wait()


def block_kernel(
    column_of, received, zonal, vweight, blocks, lowest, highest, spread, lowest_scratch, highest_scratch
):
    owners, message_rows, message_lanes = received.shape
    half = message_lanes // 8
    groups = message_rows // 8
    entries = blocks.shape[0]
    rows, levels, _ = spread.shape
    per_entry = rows // entries
    for pair in range(groups // 2):
        wide = received[:, pair * 16 : (pair + 1) * 16, :].astype(jnp.float32)
        for side in range(2):
            group = pair * 2 + side
            own = wide[:, side * 8 : (side + 1) * 8, :].reshape(owners * 8, message_lanes)
            turned = [
                jnp.transpose(own[:, tile * LANES : (tile + 1) * LANES]).astype(jnp.bfloat16)
                for tile in range(message_lanes // LANES)
            ]
            turned = jnp.concatenate(turned, axis=0)
            for e in range(8):
                entry = group * 8 + e
                made = mxu(turned[e * half : (e + 1) * half], zonal[column_of[entry]], NN)
                made = made.astype(jnp.bfloat16).astype(jnp.float32)
                blocks[entry] = made
                for a in range(entry * per_entry, (entry + 1) * per_entry):
                    spread[a] = jnp.broadcast_to(vweight[:, a : a + 1], (levels, LANES))
                for field in range(3):
                    lowest_scratch[field * entries + entry : field * entries + entry + 1, :] = made[
                        field * 16 : field * 16 + 1, :
                    ]
                    highest_scratch[field * entries + entry : field * entries + entry + 1, :] = made[
                        field * 16 + 15 : field * 16 + 16, :
                    ]
    lowest[...] = lowest_scratch[...].astype(jnp.bfloat16)
    highest[...] = highest_scratch[...].astype(jnp.bfloat16)


def horizontal_kernel(stencil, blocks, hweight, spread, partial, tops):
    _, fields, levels, _ = partial.shape
    together = stencil.shape[1] // 4
    row = lax.broadcasted_iota(jnp.int32, (8, LANES), 0)

    def some_rows(i, carry):
        for k in range(together):
            a = i * together + k
            total = None
            for q in range(4):
                term = hweight[a, q : q + 1, :] * blocks[stencil[i, k * 4 + q]]
                total = term if total is None else total + term
            lower = spread[a, 0:8, :]
            upper = spread[a, 8:16, :]
            top = None
            for field in range(fields):
                first = total[field * levels : field * levels + 8]
                second = total[field * levels + 8 : field * levels + 16]
                turned = pltpu.roll(second, 7, 0)
                up = jnp.where(row == 7, turned, pltpu.roll(first, 7, 0))
                low = first + lower * (up - first)
                high = jnp.where(row == 7, 0.0, second + upper * (turned - second))
                partial[a, field] = jnp.concatenate([low, high], axis=0).astype(jnp.bfloat16)
                placed = second if field == 0 else turned if field == 1 else pltpu.roll(second, 8 - field, 0)
                top = placed if top is None else jnp.where(row == 7 - field, placed, top)
            tops[a] = top
        return carry

    lax.fori_loop(0, stencil.shape[0], some_rows, 0)


def vertical_kernel(
    stencil, at_top, partial, tops, highest, above, hweight, spread, arrival, made, over_rows, wide, out_sem
):
    rows, fields, levels, _ = made.shape
    entries = wide.shape[0]
    top = at_top[0] == 1
    over_rows[...] = jnp.where(top, highest[...].astype(jnp.float32), above[...].astype(jnp.float32))
    together = 8

    def widen(i, carry):
        for k in range(together):
            entry = i * together + k
            for field in range(fields):
                wide[entry, 7 - field : 8 - field, :] = over_rows[pl.ds(field * entries + entry, 1), :]
        return carry

    lax.fori_loop(0, entries // together, widen, 0)

    row = lax.broadcasted_iota(jnp.int32, (8, LANES), 0)
    piece = stencil.shape[1] // 4
    pieces = rows // piece

    def send(i):
        at = pl.multiple_of(i * piece, piece)
        return pltpu.make_async_copy(made.at[pl.ds(at, piece)], arrival.at[pl.ds(at, piece)], out_sem.at[i])

    def some_rows(i, carry):
        for k in range(piece):
            a = i * piece + k
            last = None
            for q in range(4):
                term = hweight[a, q : q + 1, :] * wide[stencil[i, k * 4 + q]]
                last = term if last is None else last + term
            here = tops[a]
            top = here + spread[a, levels - 1 : levels, :] * (last - here)
            for field in range(fields):
                placed = top if field == 0 else pltpu.roll(top, field, 0)
                placed = jnp.where(row == 7, placed, 0.0)
                patch = jnp.concatenate([jnp.zeros_like(placed), placed], axis=0).astype(jnp.bfloat16)
                made[a, field] = partial[a, field] + patch
        send(i).start()
        return carry

    lax.fori_loop(0, pieces, some_rows, 0)
    for i in range(pieces):
        send(i).wait()


def whole(memory):
    return pl.BlockSpec(memory_space=memory)


def per_device(fourier, gauss, legendre, owner, send_list, stencil, hweight, vweight):
    lat_count = lax.axis_size("lat")
    device_row = lax.axis_index("lat")
    lat_dev, fields, levels, columns = fourier.shape
    wave_total = columns // 2
    slot_most = legendre.shape[1]
    degrees = legendre.shape[3]
    latitudes = legendre.shape[2]
    slot_count = lat_count * slot_most
    capacity = send_list.shape[2]
    arrivals = stencil.shape[0]
    half = fields * levels
    per_slot = 2 * half
    message_lanes = slot_most * per_slot
    tiles = message_lanes // LANES
    entries = lat_count * capacity

    owners = owner[:, 0]
    wave_index = jnp.arange(wave_total, dtype=jnp.int32)
    earlier = (owners[:, None] == owners[None, :]) & (wave_index[:, None] < wave_index[None, :])
    slot_rank = jnp.sum(earlier.astype(jnp.int32), axis=0)
    slot_of = owners * slot_most + slot_rank
    wave_number = wave_index * (degrees // wave_total)
    vmem = whole(pltpu.VMEM)
    smem = whole(pltpu.SMEM)
    hbm = whole(pl.ANY)
    message_one = pl.pallas_call(
        pack_kernel,
        out_shape=jax.ShapeDtypeStruct((lat_count, tiles * lat_dev + 8, LANES), jnp.bfloat16),
        in_specs=[hbm, hbm, hbm, hbm],
        out_specs=hbm,
        scratch_shapes=[
            pltpu.VMEM((1, wave_total), jnp.int32),
            pltpu.VMEM((capacity, lat_count), jnp.int32),
            pltpu.VMEM((1, lat_dev), jnp.float32),
            pltpu.VMEM(fourier.shape, jnp.bfloat16),
            pltpu.VMEM((lat_count, tiles * lat_dev + 8, LANES), jnp.bfloat16),
            pltpu.VMEM((tiles, lat_count * lat_dev, LANES), jnp.float32),
            pltpu.VMEM((lat_dev, columns), jnp.float32),
            pltpu.SemaphoreType.DMA((lat_dev // 8 + 3,)),
            pltpu.SemaphoreType.DMA((lat_count // 8,)),
        ],
        compiler_params=pltpu.CompilerParams(vmem_limit_bytes=GRANT),
        name="pack",
    )(owner.reshape(1, wave_total), send_list[0].T, gauss.reshape(1, lat_dev), fourier)
    arrived = lax.all_to_all(message_one, "lat", split_axis=0, concat_axis=0, tiled=True)

    placed = (slot_of[:, None] == jnp.arange(slot_count, dtype=jnp.int32)[None, :]).astype(jnp.int32)
    owned = lax.dynamic_slice_in_dim(placed, device_row * slot_most, slot_most, 1)
    filled = jnp.sum(owned, axis=0) > 0
    slot_wave = jnp.sum(owned * wave_number[:, None], axis=0)
    degree_index = jnp.arange(degrees, dtype=jnp.int32)
    keep_mask = (filled[:, None] & (degree_index[None, :] >= slot_wave[:, None])).astype(jnp.float32)
    damping = keep_mask * damping_curve(degrees)[None, :]

    message_shape = (lat_count, entries // 8 * slot_most * 2, 8 * half)
    spectral_rows, message_two = pl.pallas_call(
        spectral_kernel,
        in_specs=[vmem, hbm, vmem],
        out_specs=[vmem, hbm],
        scratch_shapes=[
            pltpu.VMEM((slot_most, latitudes, degrees), jnp.bfloat16),
            pltpu.VMEM(message_shape, jnp.bfloat16),
            pltpu.VMEM((message_lanes, latitudes), jnp.bfloat16),
            pltpu.VMEM((latitudes * 2 * slot_most, LANES), jnp.float32),
            pltpu.VMEM((entries, LANES), jnp.int32),
            pltpu.SMEM((entries, LANES), jnp.int32),
            pltpu.SemaphoreType.DMA,
            pltpu.SemaphoreType.DMA((slot_most,)),
            pltpu.SemaphoreType.DMA((lat_count // 4,)),
        ],
        out_shape=[
            jax.ShapeDtypeStruct((slot_most, per_slot, degrees), jnp.bfloat16),
            jax.ShapeDtypeStruct(message_shape, jnp.bfloat16),
        ],
        compiler_params=pltpu.CompilerParams(vmem_limit_bytes=52 * 2**20),
        name="spectral",
    )(arrived, legendre[0], damping)
    received = lax.all_to_all(message_two, "lat", split_axis=0, concat_axis=0, tiled=True)

    spectral = jnp.transpose(
        spectral_rows.reshape(slot_most, fields, 2, levels, degrees), (0, 1, 3, 2, 4)
    )
    slot_waves = jnp.sum(placed * wave_number[:, None], axis=0)
    slot_waves, spectral = lax.optimization_barrier((slot_waves, spectral))
    present = (jnp.sum(placed, axis=0) > 0).astype(jnp.float32)
    points = jnp.arange(NLON, dtype=jnp.int32).reshape(BLOCKS_X, 1, 1, BLK)
    phases = slot_waves[None, :, None, None] * points % NLON
    angles = phases.astype(jnp.float32) * (2.0 * math.pi / NLON)
    norm_factor = present[None, :, None, None] / math.sqrt(wave_total)
    zonal = jnp.concatenate([jnp.cos(angles) * norm_factor, -jnp.sin(angles) * norm_factor], axis=2)
    zonal = zonal.astype(jnp.bfloat16).reshape(BLOCKS_X, slot_count * 2, BLK)
    all_columns = arrived[:, tiles * lat_dev, entries:].reshape(lat_count, capacity, lat_count)
    column_of = lax.dynamic_index_in_dim(all_columns, device_row, 2, keepdims=False)
    column_of = column_of.astype(jnp.int32).reshape(-1)
    lev_count = lax.axis_size("lev")
    at_top = (lax.axis_index("lev") == lev_count - 1).astype(jnp.int32).reshape(1)
    vertical = vweight.T
    corners = stencil.reshape(arrivals // 32, 128)
    received, vertical, corners, at_top = lax.optimization_barrier((received, vertical, corners, at_top))
    blocks, lowest, highest, spread = pl.pallas_call(
        block_kernel,
        out_shape=[
            jax.ShapeDtypeStruct((entries, half, BLK), jnp.float32),
            jax.ShapeDtypeStruct((fields * entries, BLK), jnp.bfloat16),
            jax.ShapeDtypeStruct((fields * entries, BLK), jnp.bfloat16),
            jax.ShapeDtypeStruct((arrivals, levels, BLK), jnp.float32),
        ],
        in_specs=[smem, vmem, vmem, vmem],
        out_specs=[vmem, vmem, vmem, vmem],
        scratch_shapes=[pltpu.VMEM((fields * entries, BLK), jnp.float32)] * 2,
        compiler_params=pltpu.CompilerParams(vmem_limit_bytes=16 * 2**20),
        name="blocks",
    )(column_of, received, zonal, vertical)

    above = lax.ppermute(lowest, "lev", [(i, i - 1) for i in range(1, lev_count)])
    partial, tops = pl.pallas_call(
        horizontal_kernel,
        out_shape=[
            jax.ShapeDtypeStruct((arrivals, fields, levels, BLK), jnp.bfloat16),
            jax.ShapeDtypeStruct((arrivals, 8, BLK), jnp.float32),
        ],
        in_specs=[smem, vmem, vmem, vmem],
        out_specs=[vmem, vmem],
        compiler_params=pltpu.CompilerParams(vmem_limit_bytes=16 * 2**20),
        cost_estimate=pl.CostEstimate(
            flops=8 * arrivals * half * BLK, bytes_accessed=4 * arrivals * half * BLK, transcendentals=0
        ),
        name="horizontal",
    )(corners, blocks, hweight, spread)
    arrival = pl.pallas_call(
        vertical_kernel,
        out_shape=jax.ShapeDtypeStruct((arrivals, fields, levels, BLK), jnp.bfloat16),
        in_specs=[smem, smem, vmem, vmem, vmem, vmem, vmem, vmem],
        out_specs=hbm,
        scratch_shapes=[
            pltpu.VMEM((arrivals, fields, levels, BLK), jnp.bfloat16),
            pltpu.VMEM((fields * entries, BLK), jnp.float32),
            pltpu.VMEM((entries, 8, BLK), jnp.float32),
            pltpu.SemaphoreType.DMA((arrivals // 32,)),
        ],
        compiler_params=pltpu.CompilerParams(vmem_limit_bytes=16 * 2**20),
        name="vertical",
    )(corners, at_top, partial, tops, highest, above, hweight, spread)
    return (spectral[None], arrival)


def solution(mesh):
    return jax.shard_map(
        per_device,
        mesh=mesh,
        in_specs=(
            P("lat", None, "lev", None),
            P("lat"),
            P("lat", None, None, None),
            P(),
            P("lat", None, None),
            P("lat", None),
            P("lat", None, None),
            P("lat", "lev"),
        ),
        out_specs=(P("lat", None, None, "lev", None, None), P("lat", None, "lev", None)),
        check_vma=False,
    )
```

```python
import math

import jax
import jax.numpy as jnp
from jax import lax
from jax.experimental import pallas as pl
from jax.experimental.pallas import tpu as pltpu
from jax.sharding import PartitionSpec as P

NLON = 2560
BLK = 128
BLOCKS_X = NLON // BLK
LANES = 128
GRANT = 56 * 2**20

diffusion = 3.0

NT = (((1,), (1,)), ((), ()))
NN = (((1,), (0,)), ((), ()))


def mxu(left, right, dims):
    return lax.dot_general(left, right, dims, preferred_element_type=jnp.float32)


def identity(size):
    rows = lax.broadcasted_iota(jnp.int32, (size, size), 0)
    columns = lax.broadcasted_iota(jnp.int32, (size, size), 1)
    return (rows == columns).astype(jnp.float32).astype(jnp.bfloat16)


def damping_curve(degrees):
    order_n = jnp.arange(degrees, dtype=jnp.float32)
    ratio = order_n * (order_n + 1.0) / float(degrees * (degrees - 1))
    return 1.0 / (1.0 + diffusion * ratio * ratio)


def pack_kernel(
    owner_in, ids_in, gauss_in, fourier_in, message, owner, send_ids, gauss, fourier, packed, scratch, weight, in_sem, out_sem
):
    lat_dev, fields, levels, columns = fourier.shape
    owners = packed.shape[0]
    tiles = scratch.shape[0]
    slots = (tiles * LANES) // (2 * fields * levels)
    chunk = 8
    pieces = lat_dev // chunk
    small = [
        pltpu.make_async_copy(source, target, in_sem.at[pieces + i])
        for i, (source, target) in enumerate(((owner_in, owner), (ids_in, send_ids), (gauss_in, gauss)))
    ]
    large = [
        pltpu.make_async_copy(
            fourier_in.at[pl.ds(i * chunk, chunk)], fourier.at[pl.ds(i * chunk, chunk)], in_sem.at[i]
        )
        for i in range(pieces)
    ]
    for copy in small + large:
        copy.start()
    for copy in small:
        copy.wait()

    waves = owner.shape[1]
    wave_at = lax.broadcasted_iota(jnp.int32, (waves, columns), 0)
    column = lax.broadcasted_iota(jnp.int32, (waves, columns), 1)
    square_row = lax.broadcasted_iota(jnp.int32, (waves, waves), 0)
    square_column = lax.broadcasted_iota(jnp.int32, (waves, waves), 1)
    listed = jnp.broadcast_to(owner[...], (waves, waves))
    upright = jnp.sum(jnp.where(square_row == square_column, listed, 0), axis=1, keepdims=True)
    upright = jnp.broadcast_to(upright, (waves, columns))
    column_owner = jnp.sum(jnp.where(wave_at == column // 2, upright, 0), axis=0, keepdims=True)
    earlier = (upright == jnp.broadcast_to(column_owner, (waves, columns))) & (wave_at < column // 2)
    column_rank = jnp.sum(jnp.where(earlier, 1, 0), axis=0, keepdims=True)
    owner_at = lax.broadcasted_iota(jnp.int32, (owners, columns), 0)
    chooser = jnp.where(owner_at == column_owner, 1.0, 0.0).astype(jnp.bfloat16)
    part_of = 2 * column_rank + lax.broadcasted_iota(jnp.int32, (1, columns), 1) % 2
    masks = [
        jnp.broadcast_to(jnp.where(part_of == i, 1.0, 0.0), (levels, columns)).astype(jnp.bfloat16)
        for i in range(2 * slots)
    ]
    turn_row = lax.broadcasted_iota(jnp.int32, (lat_dev, lat_dev), 0)
    turn_column = lax.broadcasted_iota(jnp.int32, (lat_dev, lat_dev), 1)
    weights = jnp.where(turn_row == turn_column, jnp.broadcast_to(gauss[...], (lat_dev, lat_dev)), 0.0)
    weight[...] = jnp.broadcast_to(jnp.sum(weights, axis=1, keepdims=True), weight.shape)

    none = jnp.zeros_like(chooser)
    chooser = jnp.concatenate(
        [jnp.concatenate([chooser, none], axis=1), jnp.concatenate([none, chooser], axis=1)], axis=0
    )
    for pair in range(0, lat_dev, 2):
        if pair % chunk == 0:
            large[pair // chunk].wait()
        spread = []
        for t in range(pair, pair + 2):
            rows = fourier[t].reshape(fields * levels, columns).astype(jnp.float32)
            rows = (rows * weight[t : t + 1, :]).astype(jnp.bfloat16)
            parts = []
            for slot in range(slots):
                for field in range(fields):
                    for part in range(2):
                        parts.append(rows[field * levels : (field + 1) * levels] * masks[2 * slot + part])
            spread.append(jnp.concatenate(parts, axis=0))
        chosen = mxu(chooser, jnp.concatenate(spread, axis=1), NT)
        for side in range(2):
            for tile in range(tiles):
                scratch[tile, pl.ds(pair + side, owners, stride=lat_dev), :] = chosen[
                    side * owners : (side + 1) * owners, tile * LANES : (tile + 1) * LANES
                ]

    ids = send_ids[...].astype(jnp.float32)
    in_row = jnp.floor((ids + 0.5) * (1.0 / BLOCKS_X))
    in_column = ids - in_row * BLOCKS_X
    sides = [in_row[k : k + 1] for k in range(ids.shape[0])] + [in_column[k : k + 1] for k in range(ids.shape[0])]
    extra = jnp.broadcast_to(jnp.concatenate(sides, axis=1), (8, LANES))
    group = 8

    def send(g):
        first = pl.multiple_of(g * group, group)
        return pltpu.make_async_copy(packed.at[pl.ds(first, group)], message.at[pl.ds(first, group)], out_sem.at[g])

    def finish(g, carry):
        for k in range(group):
            o = g * group + k
            parts = [scratch[tile, pl.ds(pl.multiple_of(o * lat_dev, 8), lat_dev), :] for tile in range(tiles)]
            packed[o] = jnp.concatenate(parts + [extra], axis=0).astype(jnp.bfloat16)
        send(g).start()
        return carry

    lax.fori_loop(0, owners // group, finish, 0)
    for g in range(owners // group):
        send(g).wait()


def spectral_kernel(
    arrived, tables_in, damping, spectral, message, tables, made, turned, rows_at, listed, row_of, listed_sem, in_sem, out_sem
):
    slots, per_slot, degrees = spectral.shape
    latitudes = tables.shape[1]

    def fetch(slot):
        return pltpu.make_async_copy(tables_in.at[slot], tables.at[slot], in_sem.at[slot])

    def fetch_one(slot, carry):
        fetch(slot).start()
        return carry

    lax.fori_loop(0, slots, fetch_one, 0)
    half = per_slot // 2
    field_rows = half // 3
    bands = arrived.shape[0]
    tiles = turned.shape[0] // LANES
    lat_dev = (arrived.shape[1] - 8) // tiles
    receivers, message_rows, message_lanes = message.shape
    lists = pltpu.make_async_copy(listed, row_of, listed_sem)

    wide = arrived[...].astype(jnp.float32)
    unit = identity(LANES)
    band = lax.broadcasted_iota(jnp.int32, listed.shape, 1)
    rows = wide[:, tiles * lat_dev, :].astype(jnp.bfloat16)
    rows = jnp.concatenate([rows, jnp.zeros((LANES - bands, LANES), jnp.bfloat16)], axis=0)
    rows = mxu(unit[: listed.shape[0]], rows, NT).astype(jnp.int32)
    listed[...] = (rows + jnp.where(band < bands, band, 0) * lat_dev) * 8
    lists.start()
    for tile in range(tiles):
        columns = wide[:, tile * lat_dev : (tile + 1) * lat_dev, :].reshape(latitudes, LANES)
        turned[tile * LANES : (tile + 1) * LANES, :] = jnp.transpose(columns).astype(jnp.bfloat16)

    gap = jnp.zeros((LANES - half, degrees), jnp.bfloat16)
    chunk = 256

    def one_slot(slot, carry):
        fetch(slot).wait()
        own = turned[pl.ds(pl.multiple_of(slot * per_slot, 32), per_slot), :]
        spectra = mxu(own, tables[slot], NN)
        damped = (spectra * damping[pl.ds(slot, 1), :]).astype(jnp.bfloat16)
        spectral[slot] = damped
        sides = []
        for part in range(2):
            for field in range(3):
                at = (2 * field + part) * field_rows
                sides.append(damped[at : at + field_rows])
            sides.append(gap)
        sides = jnp.concatenate(sides, axis=0)
        for at in range(0, latitudes, chunk):
            back = mxu(tables[slot, at : at + chunk, :], sides, NT)
            for part in range(2):
                rows_at[pl.ds(at * 2 * slots + slot * 2 + part, chunk, stride=2 * slots), :] = back[
                    :, part * LANES : (part + 1) * LANES
                ]
        return carry

    lax.fori_loop(0, slots, one_slot, 0)

    lists.wait()
    lane = lax.broadcasted_iota(jnp.int32, (8, LANES), 1)
    wide_tiles = message_lanes // LANES

    group = 4
    groups = receivers // group

    def send(g):
        at = pl.multiple_of(g * group, group)
        return pltpu.make_async_copy(made.at[pl.ds(at, group)], message.at[pl.ds(at, group)], out_sem.at[g])

    def one_group(g, carry):
        for k in range(group):
            r = g * group + k
            for pair in range(message_rows // 16):
                halves = []
                for side in range(2):
                    built = [None] * wide_tiles
                    for e in range(8):
                        entry = (pair * 2 + side) * 8 + e
                        at = pl.multiple_of(row_of[receivers * (entry % 2) + r, entry // 2], 8)
                        row = rows_at[pl.ds(at, 8), :]
                        start = e * half
                        if start % LANES:
                            row = pltpu.roll(row, start % LANES, 1)
                        for tile in range(start // LANES, (start + half - 1) // LANES + 1):
                            first = start - tile * LANES
                            if built[tile] is None:
                                built[tile] = row
                            else:
                                built[tile] = jnp.where(lane >= first, row, built[tile])
                    halves.append(jnp.concatenate(built, axis=1))
                both = jnp.concatenate(halves, axis=0).astype(jnp.bfloat16)
                made[r, pair * 16 : (pair + 1) * 16, :] = both
        send(g).start()
        return carry

    lax.fori_loop(0, groups, one_group, 0)
    for g in range(groups):
        send(g).wait()


def block_kernel(
    column_of, received, zonal, vweight, blocks, lowest, highest, spread, lowest_scratch, highest_scratch
):
    owners, message_rows, message_lanes = received.shape
    half = message_lanes // 8
    groups = message_rows // 8
    entries = blocks.shape[0]
    rows, levels, _ = spread.shape
    per_entry = rows // entries
    for pair in range(groups // 2):
        wide = received[:, pair * 16 : (pair + 1) * 16, :].astype(jnp.float32)
        for side in range(2):
            group = pair * 2 + side
            own = wide[:, side * 8 : (side + 1) * 8, :].reshape(owners * 8, message_lanes)
            turned = [
                jnp.transpose(own[:, tile * LANES : (tile + 1) * LANES]).astype(jnp.bfloat16)
                for tile in range(message_lanes // LANES)
            ]
            turned = jnp.concatenate(turned, axis=0)
            for e in range(8):
                entry = group * 8 + e
                made = mxu(turned[e * half : (e + 1) * half], zonal[column_of[entry]], NN)
                made = made.astype(jnp.bfloat16).astype(jnp.float32)
                blocks[entry] = made
                for a in range(entry * per_entry, (entry + 1) * per_entry):
                    spread[a] = jnp.broadcast_to(vweight[:, a : a + 1], (levels, LANES))
                for field in range(3):
                    lowest_scratch[field * entries + entry : field * entries + entry + 1, :] = made[
                        field * 16 : field * 16 + 1, :
                    ]
                    highest_scratch[field * entries + entry : field * entries + entry + 1, :] = made[
                        field * 16 + 15 : field * 16 + 16, :
                    ]
    lowest[...] = lowest_scratch[...].astype(jnp.bfloat16)
    highest[...] = highest_scratch[...].astype(jnp.bfloat16)


def horizontal_kernel(stencil, blocks, hweight, horizontal):
    rows = horizontal.shape[0]
    together = stencil.shape[1] // 4

    def some_rows(i, carry):
        for k in range(together):
            a = i * together + k
            total = None
            for q in range(4):
                term = hweight[a, q : q + 1, :] * blocks[stencil[i, k * 4 + q]]
                total = term if total is None else total + term
            horizontal[a] = total
        return carry

    lax.fori_loop(0, rows // together, some_rows, 0)


def vertical_kernel(stencil, at_top, horizontal, highest, above, hweight, spread, arrival, made, over_rows, wide, out_sem):
    rows, fields, levels, _ = made.shape
    entries = wide.shape[0]
    top = at_top[0] == 1
    over_rows[...] = jnp.where(top, highest[...].astype(jnp.float32), above[...].astype(jnp.float32))
    together = 8

    def widen(i, carry):
        for k in range(together):
            entry = i * together + k
            for field in range(fields):
                wide[entry, 7 - field : 8 - field, :] = over_rows[pl.ds(field * entries + entry, 1), :]
        return carry

    lax.fori_loop(0, entries // together, widen, 0)

    row = lax.broadcasted_iota(jnp.int32, (8, LANES), 0)
    piece = stencil.shape[1] // 4
    pieces = rows // piece

    def send(i):
        at = pl.multiple_of(i * piece, piece)
        return pltpu.make_async_copy(made.at[pl.ds(at, piece)], arrival.at[pl.ds(at, piece)], out_sem.at[i])

    def some_rows(i, carry):
        for k in range(piece):
            a = i * piece + k
            last = None
            for q in range(4):
                term = hweight[a, q : q + 1, :] * wide[stencil[i, k * 4 + q]]
                last = term if last is None else last + term
            for field in range(fields):
                parts = []
                over = last if field == 0 else pltpu.roll(last, field, 0)
                for part in reversed(range(levels // 8)):
                    here = horizontal[a, field * levels + part * 8 : field * levels + (part + 1) * 8, :]
                    turned = pltpu.roll(here, 7, 0)
                    up = jnp.where(row == 7, over, turned)
                    parts.insert(0, here + spread[a, part * 8 : (part + 1) * 8, :] * (up - here))
                    over = turned
                made[a, field] = jnp.concatenate(parts, axis=0).astype(jnp.bfloat16)
        send(i).start()
        return carry

    lax.fori_loop(0, pieces, some_rows, 0)
    for i in range(pieces):
        send(i).wait()


def whole(memory):
    return pl.BlockSpec(memory_space=memory)


def per_device(fourier, gauss, legendre, owner, send_list, stencil, hweight, vweight):
    lat_count = lax.axis_size("lat")
    device_row = lax.axis_index("lat")
    lat_dev, fields, levels, columns = fourier.shape
    wave_total = columns // 2
    slot_most = legendre.shape[1]
    degrees = legendre.shape[3]
    latitudes = legendre.shape[2]
    slot_count = lat_count * slot_most
    capacity = send_list.shape[2]
    arrivals = stencil.shape[0]
    half = fields * levels
    per_slot = 2 * half
    message_lanes = slot_most * per_slot
    tiles = message_lanes // LANES
    entries = lat_count * capacity

    owners = owner[:, 0]
    wave_index = jnp.arange(wave_total, dtype=jnp.int32)
    earlier = (owners[:, None] == owners[None, :]) & (wave_index[:, None] < wave_index[None, :])
    slot_rank = jnp.sum(earlier.astype(jnp.int32), axis=0)
    slot_of = owners * slot_most + slot_rank
    wave_number = wave_index * (degrees // wave_total)
    vmem = whole(pltpu.VMEM)
    smem = whole(pltpu.SMEM)
    hbm = whole(pl.ANY)
    message_one = pl.pallas_call(
        pack_kernel,
        out_shape=jax.ShapeDtypeStruct((lat_count, tiles * lat_dev + 8, LANES), jnp.bfloat16),
        in_specs=[hbm, hbm, hbm, hbm],
        out_specs=hbm,
        scratch_shapes=[
            pltpu.VMEM((1, wave_total), jnp.int32),
            pltpu.VMEM((capacity, lat_count), jnp.int32),
            pltpu.VMEM((1, lat_dev), jnp.float32),
            pltpu.VMEM(fourier.shape, jnp.bfloat16),
            pltpu.VMEM((lat_count, tiles * lat_dev + 8, LANES), jnp.bfloat16),
            pltpu.VMEM((tiles, lat_count * lat_dev, LANES), jnp.float32),
            pltpu.VMEM((lat_dev, columns), jnp.float32),
            pltpu.SemaphoreType.DMA((lat_dev // 8 + 3,)),
            pltpu.SemaphoreType.DMA((lat_count // 8,)),
        ],
        compiler_params=pltpu.CompilerParams(vmem_limit_bytes=GRANT),
        name="pack",
    )(owner.reshape(1, wave_total), send_list[0].T, gauss.reshape(1, lat_dev), fourier)
    arrived = lax.all_to_all(message_one, "lat", split_axis=0, concat_axis=0, tiled=True)

    placed = (slot_of[:, None] == jnp.arange(slot_count, dtype=jnp.int32)[None, :]).astype(jnp.int32)
    owned = lax.dynamic_slice_in_dim(placed, device_row * slot_most, slot_most, 1)
    filled = jnp.sum(owned, axis=0) > 0
    slot_wave = jnp.sum(owned * wave_number[:, None], axis=0)
    degree_index = jnp.arange(degrees, dtype=jnp.int32)
    keep_mask = (filled[:, None] & (degree_index[None, :] >= slot_wave[:, None])).astype(jnp.float32)
    damping = keep_mask * damping_curve(degrees)[None, :]

    message_shape = (lat_count, entries // 8 * slot_most * 2, 8 * half)
    spectral_rows, message_two = pl.pallas_call(
        spectral_kernel,
        in_specs=[vmem, hbm, vmem],
        out_specs=[vmem, hbm],
        scratch_shapes=[
            pltpu.VMEM((slot_most, latitudes, degrees), jnp.bfloat16),
            pltpu.VMEM(message_shape, jnp.bfloat16),
            pltpu.VMEM((message_lanes, latitudes), jnp.bfloat16),
            pltpu.VMEM((latitudes * 2 * slot_most, LANES), jnp.float32),
            pltpu.VMEM((entries, LANES), jnp.int32),
            pltpu.SMEM((entries, LANES), jnp.int32),
            pltpu.SemaphoreType.DMA,
            pltpu.SemaphoreType.DMA((slot_most,)),
            pltpu.SemaphoreType.DMA((lat_count // 4,)),
        ],
        out_shape=[
            jax.ShapeDtypeStruct((slot_most, per_slot, degrees), jnp.bfloat16),
            jax.ShapeDtypeStruct(message_shape, jnp.bfloat16),
        ],
        compiler_params=pltpu.CompilerParams(vmem_limit_bytes=52 * 2**20),
        name="spectral",
    )(arrived, legendre[0], damping)
    received = lax.all_to_all(message_two, "lat", split_axis=0, concat_axis=0, tiled=True)

    spectral = jnp.transpose(
        spectral_rows.reshape(slot_most, fields, 2, levels, degrees), (0, 1, 3, 2, 4)
    )
    slot_waves = jnp.sum(placed * wave_number[:, None], axis=0)
    slot_waves, spectral = lax.optimization_barrier((slot_waves, spectral))
    present = (jnp.sum(placed, axis=0) > 0).astype(jnp.float32)
    points = jnp.arange(NLON, dtype=jnp.int32).reshape(BLOCKS_X, 1, 1, BLK)
    phases = slot_waves[None, :, None, None] * points % NLON
    angles = phases.astype(jnp.float32) * (2.0 * math.pi / NLON)
    norm_factor = present[None, :, None, None] / math.sqrt(wave_total)
    zonal = jnp.concatenate([jnp.cos(angles) * norm_factor, -jnp.sin(angles) * norm_factor], axis=2)
    zonal = zonal.astype(jnp.bfloat16).reshape(BLOCKS_X, slot_count * 2, BLK)
    all_columns = arrived[:, tiles * lat_dev, entries:].reshape(lat_count, capacity, lat_count)
    column_of = lax.dynamic_index_in_dim(all_columns, device_row, 2, keepdims=False)
    column_of = column_of.astype(jnp.int32).reshape(-1)
    lev_count = lax.axis_size("lev")
    at_top = (lax.axis_index("lev") == lev_count - 1).astype(jnp.int32).reshape(1)
    vertical = vweight.T
    corners = stencil.reshape(arrivals // 32, 128)
    received, vertical, corners, at_top = lax.optimization_barrier((received, vertical, corners, at_top))
    blocks, lowest, highest, spread = pl.pallas_call(
        block_kernel,
        out_shape=[
            jax.ShapeDtypeStruct((entries, half, BLK), jnp.float32),
            jax.ShapeDtypeStruct((fields * entries, BLK), jnp.bfloat16),
            jax.ShapeDtypeStruct((fields * entries, BLK), jnp.bfloat16),
            jax.ShapeDtypeStruct((arrivals, levels, BLK), jnp.float32),
        ],
        in_specs=[smem, vmem, vmem, vmem],
        out_specs=[vmem, vmem, vmem, vmem],
        scratch_shapes=[pltpu.VMEM((fields * entries, BLK), jnp.float32)] * 2,
        compiler_params=pltpu.CompilerParams(vmem_limit_bytes=16 * 2**20),
        name="blocks",
    )(column_of, received, zonal, vertical)

    above = lax.ppermute(lowest, "lev", [(i, i - 1) for i in range(1, lev_count)])
    horizontal = pl.pallas_call(
        horizontal_kernel,
        out_shape=jax.ShapeDtypeStruct((arrivals, half, BLK), jnp.float32),
        in_specs=[smem, vmem, vmem],
        out_specs=vmem,
        compiler_params=pltpu.CompilerParams(vmem_limit_bytes=16 * 2**20),
        cost_estimate=pl.CostEstimate(
            flops=8 * arrivals * half * BLK, bytes_accessed=4 * arrivals * half * BLK, transcendentals=0
        ),
        name="horizontal",
    )(corners, blocks, hweight)
    arrival = pl.pallas_call(
        vertical_kernel,
        out_shape=jax.ShapeDtypeStruct((arrivals, fields, levels, BLK), jnp.bfloat16),
        in_specs=[smem, smem, vmem, vmem, vmem, vmem, vmem],
        out_specs=hbm,
        scratch_shapes=[
            pltpu.VMEM((arrivals, fields, levels, BLK), jnp.bfloat16),
            pltpu.VMEM((fields * entries, BLK), jnp.float32),
            pltpu.VMEM((entries, 8, BLK), jnp.float32),
            pltpu.SemaphoreType.DMA((arrivals // 32,)),
        ],
        compiler_params=pltpu.CompilerParams(vmem_limit_bytes=16 * 2**20),
        name="vertical",
    )(corners, at_top, horizontal, highest, above, hweight, spread)
    return (spectral[None], arrival)


def solution(mesh):
    return jax.shard_map(
        per_device,
        mesh=mesh,
        in_specs=(
            P("lat", None, "lev", None),
            P("lat"),
            P("lat", None, None, None),
            P(),
            P("lat", None, None),
            P("lat", None),
            P("lat", None, None),
            P("lat", "lev"),
        ),
        out_specs=(P("lat", None, None, "lev", None, None), P("lat", None, "lev", None)),
        check_vma=False,
    )
```

```python
import math

import jax
import jax.numpy as jnp
from jax import lax
from jax.experimental import pallas as pl
from jax.experimental.pallas import tpu as pltpu
from jax.sharding import PartitionSpec as P

NLON = 2560
BLK = 128
BLOCKS_X = NLON // BLK
LANES = 128
GRANT = 56 * 2**20

diffusion = 3.0

NT = (((1,), (1,)), ((), ()))
NN = (((1,), (0,)), ((), ()))


def mxu(left, right, dims):
    return lax.dot_general(left, right, dims, preferred_element_type=jnp.float32)


def identity(size):
    rows = lax.broadcasted_iota(jnp.int32, (size, size), 0)
    columns = lax.broadcasted_iota(jnp.int32, (size, size), 1)
    return (rows == columns).astype(jnp.float32).astype(jnp.bfloat16)


def damping_curve(degrees):
    order_n = jnp.arange(degrees, dtype=jnp.float32)
    ratio = order_n * (order_n + 1.0) / float(degrees * (degrees - 1))
    return 1.0 / (1.0 + diffusion * ratio * ratio)


def pack_kernel(
    owner_in, ids_in, gauss_in, fourier_in, message, owner, send_ids, gauss, fourier, packed, scratch, weight, in_sem, out_sem
):
    lat_dev, fields, levels, columns = fourier.shape
    owners = packed.shape[0]
    tiles = scratch.shape[0]
    slots = (tiles * LANES) // (2 * fields * levels)
    chunk = 8
    pieces = lat_dev // chunk
    small = [
        pltpu.make_async_copy(source, target, in_sem.at[pieces + i])
        for i, (source, target) in enumerate(((owner_in, owner), (ids_in, send_ids), (gauss_in, gauss)))
    ]
    large = [
        pltpu.make_async_copy(
            fourier_in.at[pl.ds(i * chunk, chunk)], fourier.at[pl.ds(i * chunk, chunk)], in_sem.at[i]
        )
        for i in range(pieces)
    ]
    for copy in small + large:
        copy.start()
    for copy in small:
        copy.wait()

    waves = owner.shape[1]
    wave_at = lax.broadcasted_iota(jnp.int32, (waves, columns), 0)
    column = lax.broadcasted_iota(jnp.int32, (waves, columns), 1)
    square_row = lax.broadcasted_iota(jnp.int32, (waves, waves), 0)
    square_column = lax.broadcasted_iota(jnp.int32, (waves, waves), 1)
    listed = jnp.broadcast_to(owner[...], (waves, waves))
    upright = jnp.sum(jnp.where(square_row == square_column, listed, 0), axis=1, keepdims=True)
    upright = jnp.broadcast_to(upright, (waves, columns))
    column_owner = jnp.sum(jnp.where(wave_at == column // 2, upright, 0), axis=0, keepdims=True)
    earlier = (upright == jnp.broadcast_to(column_owner, (waves, columns))) & (wave_at < column // 2)
    column_rank = jnp.sum(jnp.where(earlier, 1, 0), axis=0, keepdims=True)
    owner_at = lax.broadcasted_iota(jnp.int32, (owners, columns), 0)
    chooser = jnp.where(owner_at == column_owner, 1.0, 0.0).astype(jnp.bfloat16)
    part_of = 2 * column_rank + lax.broadcasted_iota(jnp.int32, (1, columns), 1) % 2
    masks = [
        jnp.broadcast_to(jnp.where(part_of == i, 1.0, 0.0), (levels, columns)).astype(jnp.bfloat16)
        for i in range(2 * slots)
    ]
    turn_row = lax.broadcasted_iota(jnp.int32, (lat_dev, lat_dev), 0)
    turn_column = lax.broadcasted_iota(jnp.int32, (lat_dev, lat_dev), 1)
    weights = jnp.where(turn_row == turn_column, jnp.broadcast_to(gauss[...], (lat_dev, lat_dev)), 0.0)
    weight[...] = jnp.broadcast_to(jnp.sum(weights, axis=1, keepdims=True), weight.shape)

    none = jnp.zeros_like(chooser)
    chooser = jnp.concatenate(
        [jnp.concatenate([chooser, none], axis=1), jnp.concatenate([none, chooser], axis=1)], axis=0
    )
    for pair in range(0, lat_dev, 2):
        if pair % chunk == 0:
            large[pair // chunk].wait()
        spread = []
        for t in range(pair, pair + 2):
            rows = fourier[t].reshape(fields * levels, columns).astype(jnp.float32)
            rows = (rows * weight[t : t + 1, :]).astype(jnp.bfloat16)
            parts = []
            for slot in range(slots):
                for field in range(fields):
                    for part in range(2):
                        parts.append(rows[field * levels : (field + 1) * levels] * masks[2 * slot + part])
            spread.append(jnp.concatenate(parts, axis=0))
        chosen = mxu(chooser, jnp.concatenate(spread, axis=1), NT)
        for side in range(2):
            for tile in range(tiles):
                scratch[tile, pl.ds(pair + side, owners, stride=lat_dev), :] = chosen[
                    side * owners : (side + 1) * owners, tile * LANES : (tile + 1) * LANES
                ]

    ids = send_ids[...].astype(jnp.float32)
    in_row = jnp.floor((ids + 0.5) * (1.0 / BLOCKS_X))
    in_column = ids - in_row * BLOCKS_X
    sides = [in_row[k : k + 1] for k in range(ids.shape[0])] + [in_column[k : k + 1] for k in range(ids.shape[0])]
    extra = jnp.broadcast_to(jnp.concatenate(sides, axis=1), (8, LANES))
    group = 8

    def send(g):
        first = pl.multiple_of(g * group, group)
        return pltpu.make_async_copy(packed.at[pl.ds(first, group)], message.at[pl.ds(first, group)], out_sem.at[g])

    def finish(g, carry):
        for k in range(group):
            o = g * group + k
            parts = [scratch[tile, pl.ds(pl.multiple_of(o * lat_dev, 8), lat_dev), :] for tile in range(tiles)]
            packed[o] = jnp.concatenate(parts + [extra], axis=0).astype(jnp.bfloat16)
        send(g).start()
        return carry

    lax.fori_loop(0, owners // group, finish, 0)
    for g in range(owners // group):
        send(g).wait()


def spectral_kernel(
    arrived, tables_in, damping, spectral, message, tables, made, turned, rows_at, listed, row_of, listed_sem, in_sem, out_sem
):
    slots, per_slot, degrees = spectral.shape
    latitudes = tables.shape[1]

    def fetch(slot):
        return pltpu.make_async_copy(tables_in.at[slot], tables.at[slot], in_sem.at[slot])

    def fetch_one(slot, carry):
        fetch(slot).start()
        return carry

    lax.fori_loop(0, slots, fetch_one, 0)
    half = per_slot // 2
    field_rows = half // 3
    bands = arrived.shape[0]
    tiles = turned.shape[0] // LANES
    lat_dev = (arrived.shape[1] - 8) // tiles
    receivers, message_rows, message_lanes = message.shape
    lists = pltpu.make_async_copy(listed, row_of, listed_sem)

    wide = arrived[...].astype(jnp.float32)
    unit = identity(LANES)
    band = lax.broadcasted_iota(jnp.int32, listed.shape, 1)
    rows = wide[:, tiles * lat_dev, :].astype(jnp.bfloat16)
    rows = jnp.concatenate([rows, jnp.zeros((LANES - bands, LANES), jnp.bfloat16)], axis=0)
    rows = mxu(unit[: listed.shape[0]], rows, NT).astype(jnp.int32)
    listed[...] = (rows + jnp.where(band < bands, band, 0) * lat_dev) * 8
    lists.start()
    for tile in range(tiles):
        columns = wide[:, tile * lat_dev : (tile + 1) * lat_dev, :].reshape(latitudes, LANES)
        turned[tile * LANES : (tile + 1) * LANES, :] = jnp.transpose(columns).astype(jnp.bfloat16)

    gap = jnp.zeros((LANES - half, degrees), jnp.bfloat16)
    chunk = 256

    def one_slot(slot, carry):
        fetch(slot).wait()
        own = turned[pl.ds(pl.multiple_of(slot * per_slot, 32), per_slot), :]
        spectra = mxu(own, tables[slot], NN)
        damped = (spectra * damping[pl.ds(slot, 1), :]).astype(jnp.bfloat16)
        spectral[slot] = damped
        sides = []
        for part in range(2):
            for field in range(3):
                at = (2 * field + part) * field_rows
                sides.append(damped[at : at + field_rows])
            sides.append(gap)
        sides = jnp.concatenate(sides, axis=0)
        for at in range(0, latitudes, chunk):
            back = mxu(tables[slot, at : at + chunk, :], sides, NT)
            for part in range(2):
                rows_at[pl.ds(at * 2 * slots + slot * 2 + part, chunk, stride=2 * slots), :] = back[
                    :, part * LANES : (part + 1) * LANES
                ]
        return carry

    lax.fori_loop(0, slots, one_slot, 0)

    lists.wait()
    lane = lax.broadcasted_iota(jnp.int32, (8, LANES), 1)
    wide_tiles = message_lanes // LANES

    group = 4
    groups = receivers // group

    def send(g):
        at = pl.multiple_of(g * group, group)
        return pltpu.make_async_copy(made.at[pl.ds(at, group)], message.at[pl.ds(at, group)], out_sem.at[g])

    def one_group(g, carry):
        for k in range(group):
            r = g * group + k
            for pair in range(message_rows // 16):
                halves = []
                for side in range(2):
                    built = [None] * wide_tiles
                    for e in range(8):
                        entry = (pair * 2 + side) * 8 + e
                        at = pl.multiple_of(row_of[receivers * (entry % 2) + r, entry // 2], 8)
                        row = rows_at[pl.ds(at, 8), :]
                        start = e * half
                        if start % LANES:
                            row = pltpu.roll(row, start % LANES, 1)
                        for tile in range(start // LANES, (start + half - 1) // LANES + 1):
                            first = start - tile * LANES
                            if built[tile] is None:
                                built[tile] = row
                            else:
                                built[tile] = jnp.where(lane >= first, row, built[tile])
                    halves.append(jnp.concatenate(built, axis=1))
                both = jnp.concatenate(halves, axis=0).astype(jnp.bfloat16)
                made[r, pair * 16 : (pair + 1) * 16, :] = both
        send(g).start()
        return carry

    lax.fori_loop(0, groups, one_group, 0)
    for g in range(groups):
        send(g).wait()


def block_kernel(
    column_of, received, zonal, vweight, blocks, lowest, highest, spread, lowest_scratch, highest_scratch
):
    owners, message_rows, message_lanes = received.shape
    half = message_lanes // 8
    groups = message_rows // 8
    entries = blocks.shape[0]
    rows, levels, _ = spread.shape
    per_entry = rows // entries
    for pair in range(groups // 2):
        wide = received[:, pair * 16 : (pair + 1) * 16, :].astype(jnp.float32)
        for side in range(2):
            group = pair * 2 + side
            own = wide[:, side * 8 : (side + 1) * 8, :].reshape(owners * 8, message_lanes)
            turned = [
                jnp.transpose(own[:, tile * LANES : (tile + 1) * LANES]).astype(jnp.bfloat16)
                for tile in range(message_lanes // LANES)
            ]
            turned = jnp.concatenate(turned, axis=0)
            for e in range(8):
                entry = group * 8 + e
                made = mxu(turned[e * half : (e + 1) * half], zonal[column_of[entry]], NN)
                made = made.astype(jnp.bfloat16).astype(jnp.float32)
                blocks[entry] = made
                for a in range(entry * per_entry, (entry + 1) * per_entry):
                    spread[a] = jnp.broadcast_to(vweight[:, a : a + 1], (levels, LANES))
                for field in range(3):
                    lowest_scratch[field * entries + entry : field * entries + entry + 1, :] = made[
                        field * 16 : field * 16 + 1, :
                    ]
                    highest_scratch[field * entries + entry : field * entries + entry + 1, :] = made[
                        field * 16 + 15 : field * 16 + 16, :
                    ]
    lowest[...] = lowest_scratch[...].astype(jnp.bfloat16)
    highest[...] = highest_scratch[...].astype(jnp.bfloat16)


def horizontal_kernel(stencil, blocks, hweight, horizontal):
    rows = horizontal.shape[0]
    together = stencil.shape[1] // 4

    def some_rows(i, carry):
        for k in range(together):
            a = i * together + k
            total = None
            for q in range(4):
                term = hweight[a, q : q + 1, :] * blocks[stencil[i, k * 4 + q]]
                total = term if total is None else total + term
            horizontal[a] = total
        return carry

    lax.fori_loop(0, rows // together, some_rows, 0)


def vertical_kernel(stencil, at_top, horizontal, highest, above, hweight, spread, arrival, made, over_rows, wide, out_sem):
    rows, fields, levels, _ = made.shape
    entries = wide.shape[0]
    top = at_top[0] == 1
    over_rows[...] = jnp.where(top, highest[...].astype(jnp.float32), above[...].astype(jnp.float32))
    together = 8

    def widen(i, carry):
        for k in range(together):
            entry = i * together + k
            for field in range(fields):
                wide[entry, 7 - field : 8 - field, :] = over_rows[pl.ds(field * entries + entry, 1), :]
        return carry

    lax.fori_loop(0, entries // together, widen, 0)

    row = lax.broadcasted_iota(jnp.int32, (8, LANES), 0)
    piece = stencil.shape[1] // 4
    pieces = rows // piece

    def send(i):
        at = pl.multiple_of(i * piece, piece)
        return pltpu.make_async_copy(made.at[pl.ds(at, piece)], arrival.at[pl.ds(at, piece)], out_sem.at[i])

    def some_rows(i, carry):
        for k in range(piece):
            a = i * piece + k
            last = None
            for q in range(4):
                term = hweight[a, q : q + 1, :] * wide[stencil[i, k * 4 + q]]
                last = term if last is None else last + term
            for field in range(fields):
                parts = []
                over = last if field == 0 else pltpu.roll(last, field, 0)
                for part in reversed(range(levels // 8)):
                    here = horizontal[a, field * levels + part * 8 : field * levels + (part + 1) * 8, :]
                    turned = pltpu.roll(here, 7, 0)
                    up = jnp.where(row == 7, over, turned)
                    parts.insert(0, here + spread[a, part * 8 : (part + 1) * 8, :] * (up - here))
                    over = turned
                made[a, field] = jnp.concatenate(parts, axis=0).astype(jnp.bfloat16)
        send(i).start()
        return carry

    lax.fori_loop(0, pieces, some_rows, 0)
    for i in range(pieces):
        send(i).wait()


def whole(memory):
    return pl.BlockSpec(memory_space=memory)


def per_device(fourier, gauss, legendre, owner, send_list, stencil, hweight, vweight):
    lat_count = lax.axis_size("lat")
    device_row = lax.axis_index("lat")
    lat_dev, fields, levels, columns = fourier.shape
    wave_total = columns // 2
    slot_most = legendre.shape[1]
    degrees = legendre.shape[3]
    latitudes = legendre.shape[2]
    slot_count = lat_count * slot_most
    capacity = send_list.shape[2]
    arrivals = stencil.shape[0]
    half = fields * levels
    per_slot = 2 * half
    message_lanes = slot_most * per_slot
    tiles = message_lanes // LANES
    entries = lat_count * capacity

    owners = owner[:, 0]
    wave_index = jnp.arange(wave_total, dtype=jnp.int32)
    earlier = (owners[:, None] == owners[None, :]) & (wave_index[:, None] < wave_index[None, :])
    slot_rank = jnp.sum(earlier.astype(jnp.int32), axis=0)
    slot_of = owners * slot_most + slot_rank
    wave_number = wave_index * (degrees // wave_total)
    vmem = whole(pltpu.VMEM)
    smem = whole(pltpu.SMEM)
    hbm = whole(pl.ANY)
    message_one = pl.pallas_call(
        pack_kernel,
        out_shape=jax.ShapeDtypeStruct((lat_count, tiles * lat_dev + 8, LANES), jnp.bfloat16),
        in_specs=[hbm, hbm, hbm, hbm],
        out_specs=hbm,
        scratch_shapes=[
            pltpu.VMEM((1, wave_total), jnp.int32),
            pltpu.VMEM((capacity, lat_count), jnp.int32),
            pltpu.VMEM((1, lat_dev), jnp.float32),
            pltpu.VMEM(fourier.shape, jnp.bfloat16),
            pltpu.VMEM((lat_count, tiles * lat_dev + 8, LANES), jnp.bfloat16),
            pltpu.VMEM((tiles, (lat_count + 1) * lat_dev, LANES), jnp.float32),
            pltpu.VMEM((lat_dev, columns), jnp.float32),
            pltpu.SemaphoreType.DMA((lat_dev // 8 + 3,)),
            pltpu.SemaphoreType.DMA((lat_count // 8,)),
        ],
        compiler_params=pltpu.CompilerParams(vmem_limit_bytes=GRANT),
        name="pack",
    )(owner.reshape(1, wave_total), send_list[0].T, gauss.reshape(1, lat_dev), fourier)
    arrived = lax.all_to_all(message_one, "lat", split_axis=0, concat_axis=0, tiled=True)

    placed = (slot_of[:, None] == jnp.arange(slot_count, dtype=jnp.int32)[None, :]).astype(jnp.int32)
    owned = lax.dynamic_slice_in_dim(placed, device_row * slot_most, slot_most, 1)
    filled = jnp.sum(owned, axis=0) > 0
    slot_wave = jnp.sum(owned * wave_number[:, None], axis=0)
    degree_index = jnp.arange(degrees, dtype=jnp.int32)
    keep_mask = (filled[:, None] & (degree_index[None, :] >= slot_wave[:, None])).astype(jnp.float32)
    damping = keep_mask * damping_curve(degrees)[None, :]

    message_shape = (lat_count, entries // 8 * slot_most * 2, 8 * half)
    spectral_rows, message_two = pl.pallas_call(
        spectral_kernel,
        in_specs=[vmem, hbm, vmem],
        out_specs=[vmem, hbm],
        scratch_shapes=[
            pltpu.VMEM((slot_most, latitudes, degrees), jnp.bfloat16),
            pltpu.VMEM(message_shape, jnp.bfloat16),
            pltpu.VMEM((message_lanes, latitudes), jnp.bfloat16),
            pltpu.VMEM(((latitudes + 1) * 2 * slot_most, LANES), jnp.float32),
            pltpu.VMEM((entries, LANES), jnp.int32),
            pltpu.SMEM((entries, LANES), jnp.int32),
            pltpu.SemaphoreType.DMA,
            pltpu.SemaphoreType.DMA((slot_most,)),
            pltpu.SemaphoreType.DMA((lat_count // 4,)),
        ],
        out_shape=[
            jax.ShapeDtypeStruct((slot_most, per_slot, degrees), jnp.bfloat16),
            jax.ShapeDtypeStruct(message_shape, jnp.bfloat16),
        ],
        compiler_params=pltpu.CompilerParams(vmem_limit_bytes=52 * 2**20),
        name="spectral",
    )(arrived, legendre[0], damping)
    received = lax.all_to_all(message_two, "lat", split_axis=0, concat_axis=0, tiled=True)

    spectral = jnp.transpose(
        spectral_rows.reshape(slot_most, fields, 2, levels, degrees), (0, 1, 3, 2, 4)
    )
    slot_waves = jnp.sum(placed * wave_number[:, None], axis=0)
    slot_waves, spectral = lax.optimization_barrier((slot_waves, spectral))
    present = (jnp.sum(placed, axis=0) > 0).astype(jnp.float32)
    points = jnp.arange(NLON, dtype=jnp.int32).reshape(BLOCKS_X, 1, 1, BLK)
    phases = slot_waves[None, :, None, None] * points % NLON
    angles = phases.astype(jnp.float32) * (2.0 * math.pi / NLON)
    norm_factor = present[None, :, None, None] / math.sqrt(wave_total)
    zonal = jnp.concatenate([jnp.cos(angles) * norm_factor, -jnp.sin(angles) * norm_factor], axis=2)
    zonal = zonal.astype(jnp.bfloat16).reshape(BLOCKS_X, slot_count * 2, BLK)
    all_columns = arrived[:, tiles * lat_dev, entries:].reshape(lat_count, capacity, lat_count)
    column_of = lax.dynamic_index_in_dim(all_columns, device_row, 2, keepdims=False)
    column_of = column_of.astype(jnp.int32).reshape(-1)
    lev_count = lax.axis_size("lev")
    at_top = (lax.axis_index("lev") == lev_count - 1).astype(jnp.int32).reshape(1)
    vertical = vweight.T
    corners = stencil.reshape(arrivals // 32, 128)
    received, vertical, corners, at_top = lax.optimization_barrier((received, vertical, corners, at_top))
    blocks, lowest, highest, spread = pl.pallas_call(
        block_kernel,
        out_shape=[
            jax.ShapeDtypeStruct((entries, half, BLK), jnp.float32),
            jax.ShapeDtypeStruct((fields * entries, BLK), jnp.bfloat16),
            jax.ShapeDtypeStruct((fields * entries, BLK), jnp.bfloat16),
            jax.ShapeDtypeStruct((arrivals, levels, BLK), jnp.float32),
        ],
        in_specs=[smem, vmem, vmem, vmem],
        out_specs=[vmem, vmem, vmem, vmem],
        scratch_shapes=[pltpu.VMEM((fields * entries, BLK), jnp.float32)] * 2,
        compiler_params=pltpu.CompilerParams(vmem_limit_bytes=16 * 2**20),
        name="blocks",
    )(column_of, received, zonal, vertical)

    above = lax.ppermute(lowest, "lev", [(i, i - 1) for i in range(1, lev_count)])
    horizontal = pl.pallas_call(
        horizontal_kernel,
        out_shape=jax.ShapeDtypeStruct((arrivals, half, BLK), jnp.float32),
        in_specs=[smem, vmem, vmem],
        out_specs=vmem,
        compiler_params=pltpu.CompilerParams(vmem_limit_bytes=16 * 2**20),
        cost_estimate=pl.CostEstimate(
            flops=8 * arrivals * half * BLK, bytes_accessed=4 * arrivals * half * BLK, transcendentals=0
        ),
        name="horizontal",
    )(corners, blocks, hweight)
    arrival = pl.pallas_call(
        vertical_kernel,
        out_shape=jax.ShapeDtypeStruct((arrivals, fields, levels, BLK), jnp.bfloat16),
        in_specs=[smem, smem, vmem, vmem, vmem, vmem, vmem],
        out_specs=hbm,
        scratch_shapes=[
            pltpu.VMEM((arrivals, fields, levels, BLK), jnp.bfloat16),
            pltpu.VMEM((fields * entries, BLK), jnp.float32),
            pltpu.VMEM((entries, 8, BLK), jnp.float32),
            pltpu.SemaphoreType.DMA((arrivals // 32,)),
        ],
        compiler_params=pltpu.CompilerParams(vmem_limit_bytes=16 * 2**20),
        name="vertical",
    )(corners, at_top, horizontal, highest, above, hweight, spread)
    return (spectral[None], arrival)


def solution(mesh):
    return jax.shard_map(
        per_device,
        mesh=mesh,
        in_specs=(
            P("lat", None, "lev", None),
            P("lat"),
            P("lat", None, None, None),
            P(),
            P("lat", None, None),
            P("lat", None),
            P("lat", None, None),
            P("lat", "lev"),
        ),
        out_specs=(P("lat", None, None, "lev", None, None), P("lat", None, "lev", None)),
        check_vma=False,
    )
```

```python
import math

import jax
import jax.numpy as jnp
from jax import lax
from jax.experimental import pallas as pl
from jax.experimental.pallas import tpu as pltpu
from jax.sharding import PartitionSpec as P

NLON = 2560
BLK = 128
BLOCKS_X = NLON // BLK
LANES = 128
GRANT = 56 * 2**20

diffusion = 3.0

NT = (((1,), (1,)), ((), ()))
NN = (((1,), (0,)), ((), ()))


def mxu(left, right, dims):
    return lax.dot_general(left, right, dims, preferred_element_type=jnp.float32)


def identity(size):
    rows = lax.broadcasted_iota(jnp.int32, (size, size), 0)
    columns = lax.broadcasted_iota(jnp.int32, (size, size), 1)
    return (rows == columns).astype(jnp.float32).astype(jnp.bfloat16)


def damping_curve(degrees):
    order_n = jnp.arange(degrees, dtype=jnp.float32)
    ratio = order_n * (order_n + 1.0) / float(degrees * (degrees - 1))
    return 1.0 / (1.0 + diffusion * ratio * ratio)


def pack_kernel(
    owner_in, ids_in, gauss_in, fourier_in, message, owner, send_ids, gauss, fourier, packed, scratch, weight, in_sem, out_sem
):
    lat_dev, fields, levels, columns = fourier.shape
    owners = packed.shape[0]
    tiles = scratch.shape[0]
    slots = (tiles * LANES) // (2 * fields * levels)
    chunk = 8
    pieces = lat_dev // chunk
    small = [
        pltpu.make_async_copy(source, target, in_sem.at[pieces + i])
        for i, (source, target) in enumerate(((owner_in, owner), (ids_in, send_ids), (gauss_in, gauss)))
    ]
    large = [
        pltpu.make_async_copy(
            fourier_in.at[pl.ds(i * chunk, chunk)], fourier.at[pl.ds(i * chunk, chunk)], in_sem.at[i]
        )
        for i in range(pieces)
    ]
    for copy in small + large:
        copy.start()
    for copy in small:
        copy.wait()

    waves = owner.shape[1]
    wave_at = lax.broadcasted_iota(jnp.int32, (waves, columns), 0)
    column = lax.broadcasted_iota(jnp.int32, (waves, columns), 1)
    square_row = lax.broadcasted_iota(jnp.int32, (waves, waves), 0)
    square_column = lax.broadcasted_iota(jnp.int32, (waves, waves), 1)
    listed = jnp.broadcast_to(owner[...], (waves, waves))
    upright = jnp.sum(jnp.where(square_row == square_column, listed, 0), axis=1, keepdims=True)
    upright = jnp.broadcast_to(upright, (waves, columns))
    column_owner = jnp.sum(jnp.where(wave_at == column // 2, upright, 0), axis=0, keepdims=True)
    earlier = (upright == jnp.broadcast_to(column_owner, (waves, columns))) & (wave_at < column // 2)
    column_rank = jnp.sum(jnp.where(earlier, 1, 0), axis=0, keepdims=True)
    owner_at = lax.broadcasted_iota(jnp.int32, (owners, columns), 0)
    chooser = jnp.where(owner_at == column_owner, 1.0, 0.0).astype(jnp.bfloat16)
    part_of = 2 * column_rank + lax.broadcasted_iota(jnp.int32, (1, columns), 1) % 2
    masks = [
        jnp.broadcast_to(jnp.where(part_of == i, 1.0, 0.0), (levels, columns)).astype(jnp.bfloat16)
        for i in range(2 * slots)
    ]
    turn_row = lax.broadcasted_iota(jnp.int32, (lat_dev, lat_dev), 0)
    turn_column = lax.broadcasted_iota(jnp.int32, (lat_dev, lat_dev), 1)
    weights = jnp.where(turn_row == turn_column, jnp.broadcast_to(gauss[...], (lat_dev, lat_dev)), 0.0)
    weight[...] = jnp.broadcast_to(jnp.sum(weights, axis=1, keepdims=True), weight.shape)

    none = jnp.zeros_like(chooser)
    chooser = jnp.concatenate(
        [jnp.concatenate([chooser, none], axis=1), jnp.concatenate([none, chooser], axis=1)], axis=0
    )
    for pair in range(0, lat_dev, 2):
        if pair % chunk == 0:
            large[pair // chunk].wait()
        spread = []
        for t in range(pair, pair + 2):
            rows = fourier[t].reshape(fields * levels, columns).astype(jnp.float32)
            rows = (rows * weight[t : t + 1, :]).astype(jnp.bfloat16)
            parts = []
            for slot in range(slots):
                for field in range(fields):
                    for part in range(2):
                        parts.append(rows[field * levels : (field + 1) * levels] * masks[2 * slot + part])
            spread.append(jnp.concatenate(parts, axis=0))
        chosen = mxu(chooser, jnp.concatenate(spread, axis=1), NT)
        for side in range(2):
            for tile in range(tiles):
                scratch[tile, pl.ds(pair + side, owners, stride=lat_dev), :] = chosen[
                    side * owners : (side + 1) * owners, tile * LANES : (tile + 1) * LANES
                ]

    ids = send_ids[...].astype(jnp.float32)
    in_row = jnp.floor((ids + 0.5) * (1.0 / BLOCKS_X))
    in_column = ids - in_row * BLOCKS_X
    sides = [in_row[k : k + 1] for k in range(ids.shape[0])] + [in_column[k : k + 1] for k in range(ids.shape[0])]
    extra = jnp.broadcast_to(jnp.concatenate(sides, axis=1), (8, LANES))
    group = 8

    def send(g):
        first = pl.multiple_of(g * group, group)
        return pltpu.make_async_copy(packed.at[pl.ds(first, group)], message.at[pl.ds(first, group)], out_sem.at[g])

    def finish(g, carry):
        for k in range(group):
            o = g * group + k
            parts = [scratch[tile, pl.ds(pl.multiple_of(o * lat_dev, 8), lat_dev), :] for tile in range(tiles)]
            packed[o] = jnp.concatenate(parts + [extra], axis=0).astype(jnp.bfloat16)
        send(g).start()
        return carry

    lax.fori_loop(0, owners // group, finish, 0)
    for g in range(owners // group):
        send(g).wait()


def spectral_kernel(
    arrived, tables_in, damping, spectral, message, tables, made, turned, rows_at, listed, row_of, listed_sem, in_sem, out_sem
):
    slots, per_slot, degrees = spectral.shape
    latitudes = tables.shape[1]

    def fetch(slot):
        return pltpu.make_async_copy(tables_in.at[slot], tables.at[slot], in_sem.at[slot])

    def fetch_one(slot, carry):
        fetch(slot).start()
        return carry

    lax.fori_loop(0, slots, fetch_one, 0)
    half = per_slot // 2
    field_rows = half // 3
    bands = arrived.shape[0]
    tiles = turned.shape[0] // LANES
    lat_dev = (arrived.shape[1] - 8) // tiles
    receivers, message_rows, message_lanes = message.shape
    lists = pltpu.make_async_copy(listed, row_of, listed_sem)

    wide = arrived[...].astype(jnp.float32)
    unit = identity(LANES)
    band = lax.broadcasted_iota(jnp.int32, listed.shape, 1)
    rows = wide[:, tiles * lat_dev, :].astype(jnp.bfloat16)
    rows = jnp.concatenate([rows, jnp.zeros((LANES - bands, LANES), jnp.bfloat16)], axis=0)
    rows = mxu(unit[: listed.shape[0]], rows, NT).astype(jnp.int32)
    listed[...] = (rows + jnp.where(band < bands, band, 0) * lat_dev) * 8
    lists.start()
    for tile in range(tiles):
        columns = wide[:, tile * lat_dev : (tile + 1) * lat_dev, :].reshape(latitudes, LANES)
        turned[tile * LANES : (tile + 1) * LANES, :] = jnp.transpose(columns).astype(jnp.bfloat16)

    gap = jnp.zeros((LANES - half, degrees), jnp.bfloat16)
    chunk = 256

    def one_slot(slot, carry):
        fetch(slot).wait()
        own = turned[pl.ds(pl.multiple_of(slot * per_slot, 32), per_slot), :]
        spectra = mxu(own, tables[slot], NN)
        damped = (spectra * damping[pl.ds(slot, 1), :]).astype(jnp.bfloat16)
        spectral[slot] = damped
        sides = []
        for part in range(2):
            for field in range(3):
                at = (2 * field + part) * field_rows
                sides.append(damped[at : at + field_rows])
            sides.append(gap)
        sides = jnp.concatenate(sides, axis=0)
        for at in range(0, latitudes, chunk):
            back = mxu(tables[slot, at : at + chunk, :], sides, NT)
            for part in range(2):
                rows_at[pl.ds(at * 2 * slots + slot * 2 + part, chunk, stride=2 * slots), :] = back[
                    :, part * LANES : (part + 1) * LANES
                ]
        return carry

    lax.fori_loop(0, slots, one_slot, 0)

    lists.wait()
    lane = lax.broadcasted_iota(jnp.int32, (8, LANES), 1)
    wide_tiles = message_lanes // LANES

    group = 4
    groups = receivers // group

    def send(g):
        at = pl.multiple_of(g * group, group)
        return pltpu.make_async_copy(made.at[pl.ds(at, group)], message.at[pl.ds(at, group)], out_sem.at[g])

    def one_group(g, carry):
        for k in range(group):
            r = g * group + k
            for pair in range(message_rows // 16):
                halves = []
                for side in range(2):
                    built = [None] * wide_tiles
                    for e in range(8):
                        entry = (pair * 2 + side) * 8 + e
                        at = pl.multiple_of(row_of[receivers * (entry % 2) + r, entry // 2], 8)
                        row = rows_at[pl.ds(at, 8), :]
                        start = e * half
                        if start % LANES:
                            row = pltpu.roll(row, start % LANES, 1)
                        for tile in range(start // LANES, (start + half - 1) // LANES + 1):
                            first = start - tile * LANES
                            if built[tile] is None:
                                built[tile] = row
                            else:
                                built[tile] = jnp.where(lane >= first, row, built[tile])
                    halves.append(jnp.concatenate(built, axis=1))
                both = jnp.concatenate(halves, axis=0).astype(jnp.bfloat16)
                made[r, pair * 16 : (pair + 1) * 16, :] = both
        send(g).start()
        return carry

    lax.fori_loop(0, groups, one_group, 0)
    for g in range(groups):
        send(g).wait()


def block_kernel(
    column_of, received, zonal, vweight, blocks, lowest, highest, spread, lowest_scratch, highest_scratch
):
    owners, message_rows, message_lanes = received.shape
    half = message_lanes // 8
    groups = message_rows // 8
    entries = blocks.shape[0]
    rows, levels, _ = spread.shape
    per_entry = rows // entries
    for pair in range(groups // 2):
        wide = received[:, pair * 16 : (pair + 1) * 16, :].astype(jnp.float32)
        for side in range(2):
            group = pair * 2 + side
            own = wide[:, side * 8 : (side + 1) * 8, :].reshape(owners * 8, message_lanes)
            turned = [
                jnp.transpose(own[:, tile * LANES : (tile + 1) * LANES]).astype(jnp.bfloat16)
                for tile in range(message_lanes // LANES)
            ]
            turned = jnp.concatenate(turned, axis=0)
            for e in range(8):
                entry = group * 8 + e
                made = mxu(turned[e * half : (e + 1) * half], zonal[column_of[entry]], NN)
                made = made.astype(jnp.bfloat16).astype(jnp.float32)
                blocks[entry] = made
                for a in range(entry * per_entry, (entry + 1) * per_entry):
                    spread[a] = jnp.broadcast_to(vweight[:, a : a + 1], (levels, LANES))
                for field in range(3):
                    lowest_scratch[entry * 3 + 2 - field : entry * 3 + 3 - field, :] = made[
                        field * 16 : field * 16 + 1, :
                    ]
                    highest_scratch[entry * 3 + 2 - field : entry * 3 + 3 - field, :] = made[
                        field * 16 + 15 : field * 16 + 16, :
                    ]
    lowest[...] = lowest_scratch[...].astype(jnp.bfloat16)
    highest[...] = highest_scratch[...].astype(jnp.bfloat16)


def horizontal_kernel(stencil, blocks, hweight, horizontal):
    rows = horizontal.shape[0]
    together = stencil.shape[1] // 4

    def some_rows(i, carry):
        for k in range(together):
            a = i * together + k
            total = None
            for q in range(4):
                term = hweight[a, q : q + 1, :] * blocks[stencil[i, k * 4 + q]]
                total = term if total is None else total + term
            horizontal[a] = total
        return carry

    lax.fori_loop(0, rows // together, some_rows, 0)


def vertical_kernel(stencil, at_top, horizontal, highest, above, hweight, spread, arrival, made, over_rows, out_sem):
    rows, fields, levels, _ = made.shape
    top = at_top[0] == 1
    count = above.shape[0]
    over_rows[8 : 8 + count, :] = jnp.where(top, highest[...].astype(jnp.float32), above[...].astype(jnp.float32))
    row = lax.broadcasted_iota(jnp.int32, (8, LANES), 0)
    piece = stencil.shape[1] // 4
    pieces = rows // piece

    def send(i):
        at = pl.multiple_of(i * piece, piece)
        return pltpu.make_async_copy(made.at[pl.ds(at, piece)], arrival.at[pl.ds(at, piece)], out_sem.at[i])

    def some_rows(i, carry):
        for k in range(piece):
            a = i * piece + k
            last = None
            for q in range(4):
                term = hweight[a, q : q + 1, :] * over_rows[pl.ds(stencil[i, k * 4 + q] * 3 + 3, 8), :]
                last = term if last is None else last + term
            for field in range(fields):
                parts = []
                over = last if field == 0 else pltpu.roll(last, field, 0)
                for part in reversed(range(levels // 8)):
                    here = horizontal[a, field * levels + part * 8 : field * levels + (part + 1) * 8, :]
                    turned = pltpu.roll(here, 7, 0)
                    up = jnp.where(row == 7, over, turned)
                    parts.insert(0, here + spread[a, part * 8 : (part + 1) * 8, :] * (up - here))
                    over = turned
                made[a, field] = jnp.concatenate(parts, axis=0).astype(jnp.bfloat16)
        send(i).start()
        return carry

    lax.fori_loop(0, pieces, some_rows, 0)
    for i in range(pieces):
        send(i).wait()


def whole(memory):
    return pl.BlockSpec(memory_space=memory)


def per_device(fourier, gauss, legendre, owner, send_list, stencil, hweight, vweight):
    lat_count = lax.axis_size("lat")
    device_row = lax.axis_index("lat")
    lat_dev, fields, levels, columns = fourier.shape
    wave_total = columns // 2
    slot_most = legendre.shape[1]
    degrees = legendre.shape[3]
    latitudes = legendre.shape[2]
    slot_count = lat_count * slot_most
    capacity = send_list.shape[2]
    arrivals = stencil.shape[0]
    half = fields * levels
    per_slot = 2 * half
    message_lanes = slot_most * per_slot
    tiles = message_lanes // LANES
    entries = lat_count * capacity

    owners = owner[:, 0]
    wave_index = jnp.arange(wave_total, dtype=jnp.int32)
    earlier = (owners[:, None] == owners[None, :]) & (wave_index[:, None] < wave_index[None, :])
    slot_rank = jnp.sum(earlier.astype(jnp.int32), axis=0)
    slot_of = owners * slot_most + slot_rank
    wave_number = wave_index * (degrees // wave_total)
    vmem = whole(pltpu.VMEM)
    smem = whole(pltpu.SMEM)
    hbm = whole(pl.ANY)
    message_one = pl.pallas_call(
        pack_kernel,
        out_shape=jax.ShapeDtypeStruct((lat_count, tiles * lat_dev + 8, LANES), jnp.bfloat16),
        in_specs=[hbm, hbm, hbm, hbm],
        out_specs=hbm,
        scratch_shapes=[
            pltpu.VMEM((1, wave_total), jnp.int32),
            pltpu.VMEM((capacity, lat_count), jnp.int32),
            pltpu.VMEM((1, lat_dev), jnp.float32),
            pltpu.VMEM(fourier.shape, jnp.bfloat16),
            pltpu.VMEM((lat_count, tiles * lat_dev + 8, LANES), jnp.bfloat16),
            pltpu.VMEM((tiles, (lat_count + 1) * lat_dev, LANES), jnp.float32),
            pltpu.VMEM((lat_dev, columns), jnp.float32),
            pltpu.SemaphoreType.DMA((lat_dev // 8 + 3,)),
            pltpu.SemaphoreType.DMA((lat_count // 8,)),
        ],
        compiler_params=pltpu.CompilerParams(vmem_limit_bytes=GRANT),
        name="pack",
    )(owner.reshape(1, wave_total), send_list[0].T, gauss.reshape(1, lat_dev), fourier)
    arrived = lax.all_to_all(message_one, "lat", split_axis=0, concat_axis=0, tiled=True)

    placed = (slot_of[:, None] == jnp.arange(slot_count, dtype=jnp.int32)[None, :]).astype(jnp.int32)
    owned = lax.dynamic_slice_in_dim(placed, device_row * slot_most, slot_most, 1)
    filled = jnp.sum(owned, axis=0) > 0
    slot_wave = jnp.sum(owned * wave_number[:, None], axis=0)
    degree_index = jnp.arange(degrees, dtype=jnp.int32)
    keep_mask = (filled[:, None] & (degree_index[None, :] >= slot_wave[:, None])).astype(jnp.float32)
    damping = keep_mask * damping_curve(degrees)[None, :]

    message_shape = (lat_count, entries // 8 * slot_most * 2, 8 * half)
    spectral_rows, message_two = pl.pallas_call(
        spectral_kernel,
        in_specs=[vmem, hbm, vmem],
        out_specs=[vmem, hbm],
        scratch_shapes=[
            pltpu.VMEM((slot_most, latitudes, degrees), jnp.bfloat16),
            pltpu.VMEM(message_shape, jnp.bfloat16),
            pltpu.VMEM((message_lanes, latitudes), jnp.bfloat16),
            pltpu.VMEM(((latitudes + 1) * 2 * slot_most, LANES), jnp.float32),
            pltpu.VMEM((entries, LANES), jnp.int32),
            pltpu.SMEM((entries, LANES), jnp.int32),
            pltpu.SemaphoreType.DMA,
            pltpu.SemaphoreType.DMA((slot_most,)),
            pltpu.SemaphoreType.DMA((lat_count // 4,)),
        ],
        out_shape=[
            jax.ShapeDtypeStruct((slot_most, per_slot, degrees), jnp.bfloat16),
            jax.ShapeDtypeStruct(message_shape, jnp.bfloat16),
        ],
        compiler_params=pltpu.CompilerParams(vmem_limit_bytes=52 * 2**20),
        name="spectral",
    )(arrived, legendre[0], damping)
    received = lax.all_to_all(message_two, "lat", split_axis=0, concat_axis=0, tiled=True)

    spectral = jnp.transpose(
        spectral_rows.reshape(slot_most, fields, 2, levels, degrees), (0, 1, 3, 2, 4)
    )
    slot_waves = jnp.sum(placed * wave_number[:, None], axis=0)
    slot_waves, spectral = lax.optimization_barrier((slot_waves, spectral))
    present = (jnp.sum(placed, axis=0) > 0).astype(jnp.float32)
    points = jnp.arange(NLON, dtype=jnp.int32).reshape(BLOCKS_X, 1, 1, BLK)
    phases = slot_waves[None, :, None, None] * points % NLON
    angles = phases.astype(jnp.float32) * (2.0 * math.pi / NLON)
    norm_factor = present[None, :, None, None] / math.sqrt(wave_total)
    zonal = jnp.concatenate([jnp.cos(angles) * norm_factor, -jnp.sin(angles) * norm_factor], axis=2)
    zonal = zonal.astype(jnp.bfloat16).reshape(BLOCKS_X, slot_count * 2, BLK)
    all_columns = arrived[:, tiles * lat_dev, entries:].reshape(lat_count, capacity, lat_count)
    column_of = lax.dynamic_index_in_dim(all_columns, device_row, 2, keepdims=False)
    column_of = column_of.astype(jnp.int32).reshape(-1)
    lev_count = lax.axis_size("lev")
    at_top = (lax.axis_index("lev") == lev_count - 1).astype(jnp.int32).reshape(1)
    vertical = vweight.T
    corners = stencil.reshape(arrivals // 32, 128)
    received, vertical, corners, at_top = lax.optimization_barrier((received, vertical, corners, at_top))
    blocks, lowest, highest, spread = pl.pallas_call(
        block_kernel,
        out_shape=[
            jax.ShapeDtypeStruct((entries, half, BLK), jnp.float32),
            jax.ShapeDtypeStruct((fields * entries, BLK), jnp.bfloat16),
            jax.ShapeDtypeStruct((fields * entries, BLK), jnp.bfloat16),
            jax.ShapeDtypeStruct((arrivals, levels, BLK), jnp.float32),
        ],
        in_specs=[smem, vmem, vmem, vmem],
        out_specs=[vmem, vmem, vmem, vmem],
        scratch_shapes=[pltpu.VMEM((fields * entries, BLK), jnp.float32)] * 2,
        compiler_params=pltpu.CompilerParams(vmem_limit_bytes=16 * 2**20),
        name="blocks",
    )(column_of, received, zonal, vertical)

    above = lax.ppermute(lowest, "lev", [(i, i - 1) for i in range(1, lev_count)])
    horizontal = pl.pallas_call(
        horizontal_kernel,
        out_shape=jax.ShapeDtypeStruct((arrivals, half, BLK), jnp.float32),
        in_specs=[smem, vmem, vmem],
        out_specs=vmem,
        compiler_params=pltpu.CompilerParams(vmem_limit_bytes=16 * 2**20),
        cost_estimate=pl.CostEstimate(
            flops=8 * arrivals * half * BLK, bytes_accessed=4 * arrivals * half * BLK, transcendentals=0
        ),
        name="horizontal",
    )(corners, blocks, hweight)
    arrival = pl.pallas_call(
        vertical_kernel,
        out_shape=jax.ShapeDtypeStruct((arrivals, fields, levels, BLK), jnp.bfloat16),
        in_specs=[smem, smem, vmem, vmem, vmem, vmem, vmem],
        out_specs=hbm,
        scratch_shapes=[
            pltpu.VMEM((arrivals, fields, levels, BLK), jnp.bfloat16),
            pltpu.VMEM((fields * entries + 8, BLK), jnp.float32),
            pltpu.SemaphoreType.DMA((arrivals // 32,)),
        ],
        compiler_params=pltpu.CompilerParams(vmem_limit_bytes=16 * 2**20),
        name="vertical",
    )(corners, at_top, horizontal, highest, above, hweight, spread)
    return (spectral[None], arrival)


def solution(mesh):
    return jax.shard_map(
        per_device,
        mesh=mesh,
        in_specs=(
            P("lat", None, "lev", None),
            P("lat"),
            P("lat", None, None, None),
            P(),
            P("lat", None, None),
            P("lat", None),
            P("lat", None, None),
            P("lat", "lev"),
        ),
        out_specs=(P("lat", None, None, "lev", None, None), P("lat", None, "lev", None)),
        check_vma=False,
    )
```
